256 devices in a mesh: grp: 8 (over y_lo, x), seq: 32 (over z, y_hi, core).
Axes of the slice: x: 4, y: 4 (y_hi: 2, y_lo: 2; y = y_hi * 2 + y_lo), z: 8, core: 2. Of those that a mesh axis runs over, the one named last changes fastest.
Arguments:
- fake_tokens: bfloat16 [8, 6144, 1536], P('grp', 'seq'), may hold values from -16 to 16
- real_tokens: bfloat16 [8, 6144, 1536], P('grp', 'seq'), may hold values from -6 to 6
- proj_weight: bfloat16 [1536, 2048], P('seq'), may hold values from -0.15625 to 0.15625
- score_vector: float32 [2048], replicated, may hold values from -0.25 to 0.25
Outputs:
- grad_weight: float32 [1536, 2048], P('seq')
The draws below stay inside these ranges and needn't reach their ends.
All inputs are finite; a program needn't handle non-finite values.
Results may differ from the reference program's by a relative error of at most 0.0003.
Values may be sent and summed in bfloat16 or wider, within the bound.
No kernel may reach another device: no remote copies, remote signals or barrier semaphores. Data moves between devices by JAX's collectives and lax.ppermute only.
A program may use at most 64 MiB of HBM per device.

```python
import math
import jax
import jax.numpy as jnp
from jax import lax

D_IN = 1536
HID = 2048
TOK_DEV = 192
CLIPS = 8
CLIP_LEN = 6144
N_SEQ = 32


def raised(array, own_key, source, target, shards_of, factor):
    def block_of(axis_at):
        return (jnp.arange(array.shape[axis_at]) // (array.shape[axis_at] // shards_of)).reshape((-1,) + (1,) * (array.ndim - 1 - axis_at))

    near = jax.random.permutation(own_key, shards_of)[block_of(target)]
    second = (block_of(target) + shards_of // 2) % shards_of
    return jnp.where((block_of(source) == near) | (block_of(source) == second), factor * array, array)


def levels(stream_key, extent, pieces, low, largest):
    loudness = 1.0
    for axis_at, shards_of in pieces:
        heights = jax.random.uniform(jax.random.fold_in(jax.random.fold_in(stream_key, 6), axis_at), (shards_of,), jnp.float32, low / len(pieces), largest / len(pieces))
        loudness = loudness * jnp.repeat(jnp.exp(heights), extent[axis_at] // shards_of).reshape((-1,) + (1,) * (len(extent) - 1 - axis_at))
    return loudness


def noise(stream_key, shape, spread, reach, pieces=(), held_as=jnp.bfloat16):
    drawn = spread * jax.random.normal(stream_key, shape, jnp.float32)
    if pieces:
        drawn = drawn * levels(stream_key, shape, pieces, -0.22, 0.18)
    return jnp.clip(drawn, -reach, reach).astype(held_as)


def bell_draw_with(own_key, shape, spread, bound, split, heavy, kind=jnp.bfloat16):
    entries = spread * jax.random.normal(own_key, shape, jnp.float32)
    if split:
        entries = entries * levels(own_key, shape, split, -0.22, 0.18)
    return jnp.clip(raised(entries, jax.random.fold_in(own_key, 3), *heavy), -bound, bound).astype(kind)


def setup_inputs(seed: int = 0) -> dict:
    keys = jax.random.split(jax.random.key(seed), 5)
    fake_tokens = bell_draw_with(keys[0], (CLIPS, CLIP_LEN, D_IN), 3.0, 16.0, ((0, 8), (1, 32)), (1, 2, 32, 2.75))
    real_tokens = bell_draw_with(keys[1], (CLIPS, CLIP_LEN, D_IN), 1.0, 6.0, ((0, 8), (1, 32)), (1, 2, 32, 2.75))
    proj_weight = noise(keys[2], (D_IN, HID), D_IN ** -0.5, 0.15625, ((0, 32),))
    score_vector = noise(keys[3], (HID,), (HID // 4) ** -0.5, 0.25, (), jnp.float32)
    return {"fake_tokens": fake_tokens, "real_tokens": real_tokens, "proj_weight": proj_weight, "score_vector": score_vector}


R1_WEIGHT = 40.0

def device_term(fake_rows, real_rows, weight, score_vec, loss_scale):
    tok_count = fake_rows.shape[0]
    joined = jnp.concatenate([fake_rows, real_rows], 0)
    preact = jnp.dot(joined, weight, preferred_element_type=jnp.float32)
    squash = jax.nn.sigmoid(preact)
    slopes = squash * (1.0 + preact * (1.0 - squash))
    curves = squash * (1.0 - squash) * (2.0 + preact * (1.0 - 2.0 * squash))
    logits = jnp.dot(preact * squash, score_vec, precision=lax.Precision.HIGHEST)
    slopes_real = slopes[tok_count:]
    lifted = (slopes_real * score_vec).astype(jnp.bfloat16)
    input_grad = lax.dot_general(lifted, weight, (((1,), (1,)), ((), ())), preferred_element_type=jnp.float32)
    r1_cot = (loss_scale * R1_WEIGHT * input_grad).astype(jnp.bfloat16)
    back_grad = jnp.dot(r1_cot, weight, preferred_element_type=jnp.float32)
    fake_cot = (loss_scale * jax.nn.sigmoid(logits[:tok_count])[:, None] * slopes[:tok_count] * score_vec).astype(jnp.bfloat16)
    real_cot = (-loss_scale * jax.nn.sigmoid(-logits[tok_count:])[:, None] * slopes_real * score_vec + back_grad * score_vec * curves[tok_count:]).astype(jnp.bfloat16)
    left_rows = jnp.concatenate([fake_rows, real_rows, r1_cot], 0)
    right_rows = jnp.concatenate([fake_cot, real_cot, lifted], 0)
    return lax.dot_general(left_rows, right_rows, (((0,), (0,)), ((), ())), preferred_element_type=jnp.float32)

def reference(fake_tokens, real_tokens, proj_weight, score_vector):
    loss_scale = math.sqrt(HID / (CLIPS * CLIP_LEN))

    def advance(summed, device_idx):
        clip_idx = device_idx // N_SEQ
        seq_idx = device_idx % N_SEQ
        offset = (seq_idx * TOK_DEV).astype(jnp.int32)
        fake_clip = lax.dynamic_index_in_dim(fake_tokens, clip_idx, 0, keepdims=False)
        real_clip = lax.dynamic_index_in_dim(real_tokens, clip_idx, 0, keepdims=False)
        fake_rows = lax.dynamic_slice_in_dim(fake_clip, offset, TOK_DEV, 0)
        real_rows = lax.dynamic_slice_in_dim(real_clip, offset, TOK_DEV, 0)
        grad_term = device_term(fake_rows, real_rows, proj_weight, score_vector, loss_scale)
        return (summed + grad_term.astype(jnp.float32), None)
    summed, _ = lax.scan(advance, jnp.zeros((D_IN, HID), jnp.float32), jnp.arange(CLIPS * N_SEQ, dtype=jnp.int32))
    return summed
```

```python
import math

import jax
import jax.numpy as jnp
from jax import lax
from jax.sharding import Mesh
from jax.sharding import PartitionSpec as P

R1_WEIGHT = 40.0
NX, NY, NZ = 4, 4, 8
AXES = ("ylo", "x", "z", "yhi", "c")
BF16, F16, F32 = jnp.bfloat16, jnp.float16, jnp.float32


def flat_index(x, y, z, c):
    return ((y % 2) * NX + x) * (NZ * 4) + z * 4 + (y // 2) * 2 + c


def shift(array, dx=0, dy=0, dc=0):
    pairs = [
        (flat_index(x, y, z, c), flat_index((x + dx) % NX, (y + dy) % NY, z, (c + dc) % 2))
        for x in range(NX)
        for y in range(NY)
        for z in range(NZ)
        for c in range(2)
    ]
    return lax.ppermute(array, AXES, pairs)


def by_source(pieces, me):
    turned = jnp.stack([pieces[0], pieces[3], pieces[2], pieces[1]] * 2)
    return lax.dynamic_slice_in_dim(turned, (4 - me) % 4, 4, 0)


def packed(piece, exponent):
    scaled = (piece * jnp.exp2(-exponent)).astype(F16)
    return jnp.concatenate([scaled, jnp.broadcast_to(exponent.astype(F16), (16, piece.shape[1]))], 0)


def unpacked(message):
    exponent = message[-16, 0].astype(F32)
    return message[:-16].astype(F32) * jnp.exp2(exponent), exponent


def per_device(fake_tokens, real_tokens, proj_weight, score_vector):
    ylo, x, z, yhi, c = (lax.axis_index(a) for a in AXES)
    y = yhi * 2 + ylo
    tok = fake_tokens.shape[1]
    rows, hid = proj_weight.shape
    half = hid // 2
    d_in = rows * NZ * 4
    loss_scale = math.sqrt(hid / (8 * 32 * tok))
    own_tokens = jnp.concatenate([fake_tokens[0], real_tokens[0]], 0)

    def slices_of(side):
        mine = lax.dynamic_slice_in_dim(proj_weight, side * half, half, 1)
        first = lax.dynamic_slice_in_dim(mine, x * 128, 128, 1)
        second = lax.dynamic_slice_in_dim(mine, 512 + ylo * 256 + (x % 2) * 128, 128, 1)
        return jnp.stack([first, second])

    swapped = shift(slices_of(1 - c), dc=1)
    holder = jnp.stack([ylo, x // 2])[:, None, None]
    block = jnp.where(holder == c, slices_of(c), swapped)
    over_z = lax.all_to_all(jnp.broadcast_to(block[None], (NZ, *block.shape)), "z", 0, 0)
    piece_a, piece_b = over_z[:, 0], over_z[:, 1]
    gathered_a = by_source([piece_a] + [shift(piece_a, dy=k) for k in (1, 2, 3)], y)
    gathered_b = by_source([piece_b] + [shift(piece_b, dx=k) for k in (1, 2, 3)], x)
    weight_a = gathered_a.transpose(1, 0, 2, 3).reshape(d_in, 128)
    weight_b = gathered_b.reshape(2, 2, NZ, rows, 128).transpose(2, 0, 3, 1, 4).reshape(d_in // 2, 256)
    parts_a = [weight_a] + [shift(weight_a, dx=k) for k in (1, 2, 3)]
    parts_b = [weight_b] + [shift(weight_b, dy=k) for k in (1, 2, 3)]
    yhi_of = [(y + 4 - k) % 4 // 2 for k in range(4)]

    def interleaved(near, far):
        flip = yhi_of[near] == 0
        low = jnp.where(flip, parts_b[near], parts_b[far]).reshape(NZ, 1, 2 * rows, 256)
        high = jnp.where(flip, parts_b[far], parts_b[near]).reshape(NZ, 1, 2 * rows, 256)
        return jnp.concatenate([low, high], 1).reshape(d_in, 256)

    weight = jnp.concatenate([*parts_a, interleaved(0, 2), interleaved(1, 3)], 1)

    def score_at(start, width):
        return lax.dynamic_slice_in_dim(score_vector, c * half + start, width, 0)

    score = jnp.concatenate(
        [score_at((x + 4 - k) % 4 * 128, 128) for k in range(4)]
        + [score_at(512 + ylo * 256, 256), score_at(512 + (1 - ylo) * 256, 256)]
    )

    other_tokens = shift(own_tokens, dc=1)
    tokens = jnp.concatenate(
        [own_tokens[:tok], other_tokens[:tok], own_tokens[tok:], other_tokens[tok:]], 0
    )
    n = 2 * tok

    def chip_sum(partial):
        theirs = shift(partial, dc=1)
        return partial + jnp.concatenate([theirs[tok:n], theirs[:tok], theirs[n + tok :], theirs[n : n + tok]], 0)

    preact = jnp.dot(tokens, weight, preferred_element_type=F32)
    squash = jax.nn.sigmoid(preact)
    slopes = squash * (1.0 + preact * (1.0 - squash))
    curves = squash[n:] * (1.0 - squash[n:]) * (2.0 + preact[n:] * (1.0 - 2.0 * squash[n:]))
    logits = chip_sum(jnp.sum(preact * squash * score, 1, keepdims=True))
    lifted = (slopes[n:] * score).astype(BF16)
    part_grad = lax.dot_general(lifted, weight, (((1,), (1,)), ((), ())), preferred_element_type=F32)
    theirs = shift(part_grad, dc=1)
    input_grad = part_grad + jnp.concatenate([theirs[tok:], theirs[:tok]], 0)
    r1_cot = (loss_scale * R1_WEIGHT * input_grad).astype(BF16)
    back_grad = jnp.dot(r1_cot, weight, preferred_element_type=F32)
    fake_cot = (loss_scale * jax.nn.sigmoid(logits[:n]) * slopes[:n] * score).astype(BF16)
    real_cot = (
        -loss_scale * jax.nn.sigmoid(-logits[n:]) * slopes[n:] * score + back_grad * score * curves
    ).astype(BF16)
    left = jnp.concatenate([tokens, r1_cot], 0)
    right = jnp.concatenate([fake_cot, real_cot, lifted], 0)

    def largest(array):
        return jnp.max(jnp.abs(array)).astype(F32)

    bound = n * (
        largest(tokens[:n]) * largest(fake_cot)
        + largest(tokens[n:]) * largest(real_cot)
        + largest(r1_cot) * largest(lifted)
    )
    exponent = jnp.ceil(jnp.log2(jnp.maximum(bound, 1e-30))) - 15.0

    term = lax.dot_general(left, right, (((0,), (0,)), ((), ())), preferred_element_type=F32)

    def summed(pieces, exponent, **axis):
        (name, sign), = axis.items()
        total = pieces[0]
        largest_exponent = exponent
        arrived = [shift(packed(pieces[k], exponent), **{name: -k}) for k in (1, 2, 3)]
        for message in arrived:
            values, theirs = unpacked(message)
            total = total + values
            largest_exponent = jnp.maximum(largest_exponent, theirs)
        return total, largest_exponent + 2.0

    def quarter_b(k):
        columns = term[:, 512 + 256 * (k % 2) : 768 + 256 * (k % 2)].reshape(NZ, 2, 2 * rows, 256)
        return lax.dynamic_index_in_dim(columns, yhi_of[k], 1, keepdims=False).reshape(d_in // 2, 256)

    sum_a, exp_a = summed([term[:, 128 * k : 128 * k + 128] for k in range(4)], exponent, dx=1)
    sum_b, exp_b = summed([quarter_b(k) for k in range(4)], exponent, dy=1)
    rows_a = sum_a.reshape(NZ, 4, rows, 128)
    rows_b = sum_b.reshape(NZ, 2, rows, 2, 128).transpose(0, 1, 3, 2, 4).reshape(NZ, 4, rows, 128)

    def quarters(array, me):
        return [
            lax.dynamic_index_in_dim(array, (me + 4 - k) % 4, 1, keepdims=False).reshape(NZ * rows, 128)
            for k in range(4)
        ]

    sum_a, _ = summed(quarters(rows_a, y), exp_a, dy=1)
    sum_b, _ = summed(quarters(rows_b, x), exp_b, dx=1)
    both = jnp.stack([sum_a.reshape(NZ, rows, 128), sum_b.reshape(NZ, rows, 128)], 1)
    both = jnp.sum(lax.all_to_all(both, "z", 0, 0), 0)
    spread = lax.all_to_all(jnp.broadcast_to(both[None], (8, *both.shape)), ("ylo", "x"), 0, 0)
    spread = spread.reshape(2, 4, 2, rows, 128)
    cols_a = spread[:, :, 0].transpose(0, 2, 1, 3).reshape(2, rows, 512)
    cols_b = spread[:, :, 1].reshape(2, 2, 2, rows, 128).transpose(1, 3, 0, 2, 4).reshape(2, rows, 512)
    my_half = jnp.concatenate([cols_a, cols_b], 2)
    mine = lax.dynamic_index_in_dim(my_half, c, 0, keepdims=False)
    theirs = shift(lax.dynamic_index_in_dim(my_half, 1 - c, 0, keepdims=False), dc=1)
    return jnp.concatenate([jnp.where(c == 0, mine, theirs), jnp.where(c == 0, theirs, mine)], 1)


def solution(mesh):
    split = Mesh(mesh.devices.reshape(2, NX, NZ, 2, 2), AXES)
    tokens = P(("ylo", "x"), ("z", "yhi", "c"), None)
    shard = P(("z", "yhi", "c"), None)
    return jax.shard_map(
        per_device, mesh=split, in_specs=(tokens, tokens, shard, P()), out_specs=shard, check_vma=False
    )
```

```python
import functools
import math

import jax
import jax.numpy as jnp
from jax import lax
from jax.experimental import pallas as pl
from jax.experimental.pallas import tpu as pltpu
from jax.sharding import Mesh
from jax.sharding import PartitionSpec as P

R1_WEIGHT = 40.0
NX, NY, NZ = 4, 4, 8
AXES = ("ylo", "x", "z", "yhi", "c")
BF16, F16, F32 = jnp.bfloat16, jnp.float16, jnp.float32
VMEM_BYTES = 20 * 1024 * 1024


def flat_index(x, y, z, c):
    return ((y % 2) * NX + x) * (NZ * 4) + z * 4 + (y // 2) * 2 + c


def send(array, to):
    pairs = []
    for x in range(NX):
        for y in range(NY):
            for z in range(NZ):
                for c in range(2):
                    tx, ty, tc = to(x, y, c)
                    pairs.append((flat_index(x, y, z, c), flat_index(tx % NX, ty % NY, z, tc)))
    return lax.ppermute(array, AXES, pairs)


def to_core(array):
    return send(array, lambda x, y, c: (x, y, 1 - c))


def together(arrays, routes):
    arrays = lax.optimization_barrier(tuple(arrays))
    return lax.optimization_barrier(tuple(send(a, to) for a, to in zip(arrays, routes, strict=True)))


RING = (
    lambda x, y, c: (x + 1, y, c),
    lambda x, y, c: (x - 1, y, c),
    lambda x, y, c: (x, y + 1, c),
    lambda x, y, c: (x, y - 1, c),
)


def ordered(first_is_mine, mine, theirs, axis):
    return jnp.concatenate(
        [jnp.where(first_is_mine, mine, theirs), jnp.where(first_is_mine, theirs, mine)], axis
    )


def packed(piece, exponent):
    scaled = (piece * jnp.exp2(-exponent)).astype(F16)
    return jnp.concatenate([scaled, jnp.broadcast_to(exponent.astype(F16), (16, piece.shape[1]))], 0)


def unpacked(message):
    exponent = message[-16:-15].astype(F32)
    return message[:-16].astype(F32) * jnp.exp2(exponent), exponent


def column_tiles(width):
    return [(start, min(256, width - start)) for start in range(0, width, 256)]


def nt(a, b):
    return lax.dot_general(a, b, (((1,), (1,)), ((), ())), preferred_element_type=F32)


def forward_tiles(tokens_ref, w_ref, score_ref, slope_ref, curve_ref, lifted_ref, logit_ref, first):
    n = tokens_ref.shape[0] // 2
    for kind in (0, 1):
        rows = slice(kind * n, kind * n + n)
        total = jnp.zeros((n, 128), F32) if first is None else first[rows, :]
        for start, width in column_tiles(w_ref.shape[1]):
            cols = slice(start, start + width)
            preact = jnp.dot(tokens_ref[rows, :], w_ref[:, cols], preferred_element_type=F32)
            score = score_ref[:, cols]
            squash = jax.nn.sigmoid(preact)
            rest = 1.0 - squash
            act = preact * squash * score
            for lane in range(0, width, 128):
                total = total + act[:, lane : lane + 128]
            slope = squash * (1.0 + preact * rest) * score
            slope_ref[rows, cols] = slope
            if kind == 1:
                lifted_ref[:, cols] = slope.astype(BF16)
                curve_ref[:, cols] = squash * rest * (2.0 + preact * (1.0 - 2.0 * squash)) * score
        logit_ref[rows, :] = total


def pull_back(w_ref, lifted_ref, part_ref, so_far):
    for start in range(0, w_ref.shape[0], 512):
        rows = slice(start, start + 512)
        value = nt(w_ref[rows, :], lifted_ref[...])
        part_ref[rows, :] = value if so_far is None else so_far[rows, :] + value


def place_pair(w_ref, column, low_ref, high_ref, swap):
    width = low_ref.shape[1]
    turn = w_ref.shape[0] // (2 * NZ)
    for z in range(NZ):
        rows = slice(z * turn, z * turn + turn)
        low, high = low_ref[rows, :], high_ref[rows, :]
        w_ref[2 * z * turn : 2 * z * turn + turn, column : column + width] = jnp.where(swap, high, low)
        w_ref[2 * z * turn + turn : 2 * z * turn + 2 * turn, column : column + width] = jnp.where(swap, low, high)


def first_kernel(flag_ref, tokens_ref, own_ref, left_ref, right_ref, low_ref, high_ref, score_ref,
                 w_ref, slope_ref, curve_ref, lifted_ref, logit_ref, part_ref):
    w_ref[:, 0:128] = own_ref[...]
    w_ref[:, 128:256] = left_ref[...]
    w_ref[:, 256:384] = right_ref[...]
    place_pair(w_ref, 384, low_ref, high_ref, flag_ref[0] == 1)
    forward_tiles(tokens_ref, w_ref, score_ref, slope_ref, curve_ref, lifted_ref, logit_ref, None)
    pull_back(w_ref, lifted_ref, part_ref, None)


def tokens_kernel(flag_ref, fake_ref, real_ref, other_ref, tokens_ref, tokens_t_ref, peak_ref):
    tok = fake_ref.shape[0]
    first = flag_ref[0] == 0
    for kind, own in enumerate((fake_ref, real_ref)):
        mine, theirs = own[...], other_ref[kind * tok : kind * tok + tok, :]
        start = 2 * kind * tok
        tokens_ref[start : start + tok, :] = jnp.where(first, mine, theirs)
        tokens_ref[start + tok : start + 2 * tok, :] = jnp.where(first, theirs, mine)
        peak = peak_of(tokens_ref[start : start + 2 * tok, :])
        peak_ref[8 * kind : 8 * kind + 8, :] = jnp.broadcast_to(peak, (8, 128))
    tokens_t_ref[...] = tokens_ref[...].T


def second_kernel(flag_ref, tokens_ref, low_ref, high_top_ref, high_bottom_ref, across_top_ref, across_bottom_ref,
                  score_ref, logit_in_ref, part_in_ref,
                  w_ref, slope_ref, curve_ref, lifted_ref, logit_ref, part_ref, high_ref):
    top = high_top_ref.shape[0]
    high_ref[0:top, :] = high_top_ref[...]
    high_ref[top : 2 * top, :] = high_bottom_ref[...]
    place_pair(w_ref, 0, low_ref, high_ref, flag_ref[0] == 1)
    top = across_top_ref.shape[0]
    w_ref[0:top, 256:384] = across_top_ref[...]
    w_ref[top : 2 * top, 256:384] = across_bottom_ref[...]
    forward_tiles(tokens_ref, w_ref, score_ref, slope_ref, curve_ref, lifted_ref, logit_ref, logit_in_ref)
    pull_back(w_ref, lifted_ref, part_ref, part_in_ref)


def peak_of(array):
    flat = jnp.max(jnp.abs(array).astype(F32), axis=0, keepdims=True)
    return jnp.max(flat, axis=1, keepdims=True)


def term_tiles(scale, tokens_t_ref, r1_t_ref, r1_ref, logits, w_ref, slope_ref, curve_ref, lifted_ref, peak_ref,
               outs, exp_ref, fake_ref, real_ref):
    n = lifted_ref.shape[0]
    fake_gain = scale * jax.nn.sigmoid(logits[:n])
    real_gain = -scale * jax.nn.sigmoid(-logits[n:])
    fake_ref[...] = (fake_gain * slope_ref[0:n, :]).astype(BF16)
    for start, width in column_tiles(w_ref.shape[1]):
        cols = slice(start, start + width)
        back = jnp.dot(r1_ref[...], w_ref[:, cols], preferred_element_type=F32)
        real_ref[:, cols] = (real_gain * slope_ref[n : 2 * n, cols] + back * curve_ref[:, cols]).astype(BF16)
    bound = n * (
        peak_ref[0:1, 0:1] * peak_of(fake_ref[...])
        + peak_ref[8:9, 0:1] * peak_of(real_ref[...])
        + peak_of(r1_t_ref[...]) * peak_of(lifted_ref[...])
    )
    bound = jnp.broadcast_to(bound, (16, 128))
    exp_ref[...] = jnp.ceil(jnp.log(jnp.maximum(bound, 1e-30)) * (1.0 / math.log(2.0)) + 0.01) - 15.0
    d_in = tokens_t_ref.shape[0]
    turn = d_in // (2 * NZ)
    height = 4 * turn
    for start, width, parts in outs:
        cols = slice(start, start + width)
        for row in range(0, d_in, height):
            rows = slice(row, row + height)
            value = (
                jnp.dot(tokens_t_ref[rows, 0:n], fake_ref[:, cols], preferred_element_type=F32)
                + jnp.dot(tokens_t_ref[rows, n : 2 * n], real_ref[:, cols], preferred_element_type=F32)
                + jnp.dot(r1_t_ref[rows, :], lifted_ref[:, cols], preferred_element_type=F32)
            )
            for column, turns, out in parts:
                piece = value[:, column : column + out.shape[1]]
                if turns is None:
                    out[rows, :] = piece
                else:
                    for k in range(2):
                        at = row // 2 + k * turn
                        out[at : at + turn, :] = piece[(2 * k + turns) * turn : (2 * k + turns + 1) * turn, :]


def third_kernel(scale, tokens_t_ref, part_ref, part_in_ref, logit_ref, logit_in_ref, w_ref, slope_ref, curve_ref,
                 lifted_ref, peak_ref, low_ref, high_ref, across_ref, exp_ref, r1_t_ref, r1_ref, logits_ref,
                 fake_ref, real_ref):
    r1_t_ref[...] = (scale * R1_WEIGHT * (part_ref[...] + part_in_ref[...])).astype(BF16)
    r1_ref[...] = r1_t_ref[...].T
    logits = jnp.sum(logit_ref[...] + logit_in_ref[...], axis=1, keepdims=True)
    logits_ref[...] = jnp.broadcast_to(logits, logits_ref.shape)
    outs = [(0, 256, [(0, 0, low_ref), (0, 1, high_ref)]), (256, 128, [(0, None, across_ref)])]
    term_tiles(scale, tokens_t_ref, r1_t_ref, r1_ref, logits, w_ref, slope_ref, curve_ref, lifted_ref, peak_ref,
               outs, exp_ref, fake_ref, real_ref)


def fourth_kernel(scale, tokens_t_ref, r1_t_ref, r1_ref, logits_ref, w_ref, slope_ref, curve_ref, lifted_ref, peak_ref,
                  own_ref, left_ref, right_ref, low_ref, high_ref, exp_ref, fake_ref, real_ref):
    outs = [
        (0, 256, [(0, None, own_ref), (128, None, left_ref)]),
        (256, 128, [(0, None, right_ref)]),
        (384, 256, [(0, 0, low_ref), (0, 1, high_ref)]),
    ]
    term_tiles(scale, tokens_t_ref, r1_t_ref, r1_ref, logits_ref[:, 0:1], w_ref, slope_ref, curve_ref, lifted_ref,
               peak_ref, outs, exp_ref, fake_ref, real_ref)


def call(kernel, flops, outs, scratch, *args, flags=None):
    vmem = pl.BlockSpec(memory_space=pltpu.VMEM)
    specs = [vmem] * len(args)
    if flags is not None:
        args, specs = (flags, *args), [pl.BlockSpec(memory_space=pltpu.SMEM), *specs]
    return pl.pallas_call(
        kernel,
        out_shape=[jax.ShapeDtypeStruct(shape, dtype) for shape, dtype in outs],
        in_specs=specs,
        out_specs=[vmem] * len(outs),
        scratch_shapes=[pltpu.VMEM(shape, dtype) for shape, dtype in scratch],
        compiler_params=pltpu.CompilerParams(vmem_limit_bytes=VMEM_BYTES),
        cost_estimate=pl.CostEstimate(flops=flops, bytes_accessed=8_000_000, transcendentals=0),
    )(*args)


def per_device(fake_tokens, real_tokens, proj_weight, score_vector):
    ylo, x, z, yhi, c = (lax.axis_index(a) for a in AXES)
    y = yhi * 2 + ylo
    gray_x, gray_y = ((v == 1) | (v == 2) for v in (x, y))
    core0 = c == 0
    tok = fake_tokens.shape[1]
    rows, hid = proj_weight.shape
    half = hid // 2
    d_in = rows * NZ * 4
    n = 2 * tok
    scale = math.sqrt(hid / (8 * 32 * tok))

    def slices_of(side):
        mine = lax.dynamic_slice_in_dim(proj_weight, side * half, half, 1)
        first = lax.dynamic_slice_in_dim(mine, x * 128, 128, 1)
        second = lax.dynamic_slice_in_dim(mine, 512 + ylo * 256 + gray_x * 128, 128, 1)
        return jnp.concatenate([first, second], 1)

    block = ordered(core0, slices_of(c), to_core(slices_of(1 - c)), 0)
    over_z = lax.all_to_all(jnp.broadcast_to(block[None], (NZ, *block.shape)), "z", 0, 0)
    piece_a, piece_b = over_z[:, :, :128], over_z[:, :, 128:].reshape(d_in // 2, 128)
    far_a, far_b = together(
        (piece_a.reshape(d_in // 2, 128), piece_b), (lambda x, y, c: (x, 3 - y, c), lambda x, y, c: (x ^ 1, y, c))
    )
    far_a = far_a.reshape(piece_a.shape)
    own_a = ordered(yhi == 0, piece_a[:, None], far_a[:, None], 1).reshape(d_in, 128)
    own_b = ordered(~gray_x, piece_b, far_b, 1)

    own_tokens = jnp.concatenate([fake_tokens[0], real_tokens[0]], 0)
    tokens, tokens_t, peak = call(
        tokens_kernel, 2 * n * d_in * 128, [((2 * n, d_in), BF16), ((d_in, 2 * n), BF16), ((16, 128), F32)], [],
        fake_tokens[0], real_tokens[0], to_core(own_tokens),
        flags=c[None].astype(jnp.int32),
    )

    left_a, right_a, left_b, right_b = together((own_a, own_a, own_b, own_b), RING)
    mid_a, mid_b = d_in // 2, d_in // 4
    across = together((left_a[:mid_a], right_a[mid_a:], left_b[:mid_b], right_b[mid_b:]), RING)
    across_a, across_b = across[:2], across[2:]

    def score_at(start, width):
        return lax.dynamic_slice_in_dim(score_vector, c * half + start, width, 0)

    score_1 = jnp.concatenate(
        [score_at((x + k) % 4 * 128, 128) for k in (0, 3, 1)] + [score_at(512 + (1 - ylo) * 256, 256)]
    )[None]
    score_2 = jnp.concatenate([score_at(512 + ylo * 256, 256), score_at((x + 2) % 4 * 128, 128)])[None]
    yhi_left, yhi_right = (y + 3) % 4 // 2, (y + 1) % 4 // 2

    def states(width):
        return [
            ((d_in, width), BF16),
            ((2 * n, width), F32),
            ((n, width), F32),
            ((n, width), BF16),
            ((2 * n, 128), F32),
            ((d_in, n), F32),
        ]

    wide, narrow = 640, 384
    w_1, slope_1, curve_1, lifted_1, logit_1, part_1 = call(
        first_kernel, 6 * n * d_in * wide, states(wide), [],
        tokens, own_a, left_a, right_a, left_b, right_b, score_1,
        flags=yhi_left[None].astype(jnp.int32),
    )
    w_2, slope_2, curve_2, lifted_2, logit, part = call(
        second_kernel, 6 * n * d_in * narrow, states(narrow), [((d_in // 2, 256), BF16)],
        tokens, own_b, *across_b, *across_a, score_2, logit_1, part_1,
        flags=yhi[None].astype(jnp.int32),
    )
    part_in, logit_in = to_core(part), to_core(logit)

    def works(width):
        return [((n, width), BF16)] * 2

    side = [((d_in // 2, 256), F32)] * 2
    strip = ((d_in, 128), F32)
    low_2, high_2, far_a, exp_2, r1_t, r1, logits = call(
        functools.partial(third_kernel, scale), 8 * n * d_in * narrow,
        [*side, strip, ((16, 128), F32), ((d_in, n), BF16), ((n, d_in), BF16), ((2 * n, 128), F32)],
        works(narrow),
        tokens_t, part, part_in, logit, logit_in, w_2, slope_2, curve_2, lifted_2, peak,
    )
    own_1, left_1, right_1, low_1, high_1, exp_1 = call(
        functools.partial(fourth_kernel, scale), 8 * n * d_in * wide,
        [strip, strip, strip, *side, ((16, 128), F32)], works(wide),
        tokens_t, r1_t, r1, logits, w_1, slope_1, curve_1, lifted_1, peak,
    )
    exp_1, exp_2 = exp_1[:1], exp_2[:1]
    twice = lambda row: jnp.concatenate([row, row], 1)

    own_2 = jnp.where(yhi == 0, low_2, high_2)
    far_b = jnp.where(yhi == 0, high_2, low_2)
    a_up, a_down, b_up, b_down = together(
        (
            packed(far_a[:mid_a], exp_2),
            packed(far_a[mid_a:], exp_2),
            packed(far_b[:mid_b], twice(exp_2)),
            packed(far_b[mid_b:], twice(exp_2)),
        ),
        RING,
    )

    def joined(piece, exponent, top=None, bottom=None):
        middle = piece.shape[0] // 2
        values, theirs = unpacked(bottom if top is None else top)
        exponent = jnp.maximum(exponent, theirs) + 1.0
        upper, lower = piece[:middle], piece[middle:]
        upper, lower = (upper, lower + values) if top is None else (upper + values, lower)
        return packed(jnp.concatenate([upper, lower], 0), exponent)

    right_b = jnp.where(yhi_right == 0, low_1, high_1)
    left_b = jnp.where(yhi_left == 0, low_1, high_1)
    from_left_a, from_right_a, from_left_b, from_right_b = together(
        (
            joined(right_1, exp_1, top=a_up),
            joined(left_1, exp_1, bottom=a_down),
            joined(right_b, twice(exp_1), top=b_up),
            joined(left_b, twice(exp_1), bottom=b_down),
        ),
        RING,
    )

    def three(own, exponent, one, two):
        (one, exp_one), (two, exp_two) = unpacked(one), unpacked(two)
        return own + one + two, jnp.maximum(exponent, jnp.maximum(exp_one, exp_two)) + 2.0

    top = jnp.maximum(exp_1, exp_2)
    sum_a, exp_a = three(own_1, top, from_left_a, from_right_a)
    sum_b, exp_b = three(own_2, twice(top), from_left_b, from_right_b)

    turns = sum_a.reshape(NZ, 2, 2 * rows, 128)
    keep_a = jnp.where(yhi == 0, turns[:, 0], turns[:, 1]).reshape(d_in // 2, 128)
    give_a = jnp.where(yhi == 0, turns[:, 1], turns[:, 0]).reshape(d_in // 2, 128)
    keep_b = jnp.where(gray_x, sum_b[:, 128:], sum_b[:, :128])
    give_b = jnp.where(gray_x, sum_b[:, :128], sum_b[:, 128:])
    got_a, got_b = together(
        (packed(give_a, exp_a), packed(give_b, exp_b[:, :128])),
        (lambda x, y, c: (x, 3 - y, c), lambda x, y, c: (x ^ 1, y, c)),
    )
    turns_a = (keep_a + unpacked(got_a)[0]).reshape(NZ, 2, rows, 128)
    turns_b = (keep_b + unpacked(got_b)[0]).reshape(NZ, 2, rows, 128)

    def split_rows(turns, second):
        return jnp.where(second, turns[:, 1], turns[:, 0]), jnp.where(second, turns[:, 0], turns[:, 1])

    keep_a, give_a = split_rows(turns_a, gray_y)
    keep_b, give_b = split_rows(turns_b, x >= 2)
    got_a, got_b = together(
        (give_a, give_b), (lambda x, y, c: (x, y ^ 1, c), lambda x, y, c: (3 - x, y, c))
    )
    both = jnp.concatenate([keep_a + got_a, keep_b + got_b], 2)
    both = jnp.sum(lax.all_to_all(both, "z", 0, 0), 0)

    spread = lax.all_to_all(jnp.broadcast_to(both[None], (8, *both.shape)), ("ylo", "x"), 0, 0)
    spread = spread.reshape(2, 4, rows, 256)

    def row_group(r):
        pick = jnp.where(yhi == r, spread[0, :, :, :128], spread[1, :, :, :128])
        order = (0, 1) if r == 0 else (3, 2)
        return jnp.concatenate(
            [pick[k] for k in range(4)] + [spread[v, k, :, 128:] for v in (0, 1) for k in order], 1
        )

    zero, one = row_group(0), row_group(1)
    theirs = to_core(jnp.where(core0, one, zero))
    return ordered(core0, jnp.where(core0, zero, one), theirs, 1)


def solution(mesh):
    split = Mesh(mesh.devices.reshape(2, NX, NZ, 2, 2), AXES)
    tokens = P(("ylo", "x"), ("z", "yhi", "c"), None)
    shard = P(("z", "yhi", "c"), None)
    return jax.shard_map(
        per_device, mesh=split, in_specs=(tokens, tokens, shard, P()), out_specs=shard, check_vma=False
    )
```

```python
import functools
import math

import jax
import jax.numpy as jnp
from jax import lax
from jax.experimental import pallas as pl
from jax.experimental.pallas import tpu as pltpu
from jax.sharding import Mesh
from jax.sharding import PartitionSpec as P

R1_WEIGHT = 40.0
NX, NY, NZ = 4, 4, 8
AXES = ("ylo", "x", "z", "yhi", "c")
BF16, F16, F32 = jnp.bfloat16, jnp.float16, jnp.float32
VMEM_BYTES = 26 * 1024 * 1024


def flat_index(x, y, z, c):
    return ((y % 2) * NX + x) * (NZ * 4) + z * 4 + (y // 2) * 2 + c


def send(array, to):
    pairs = []
    for x in range(NX):
        for y in range(NY):
            for z in range(NZ):
                for c in range(2):
                    tx, ty, tc = to(x, y, c)
                    pairs.append((flat_index(x, y, z, c), flat_index(tx % NX, ty % NY, z, tc)))
    return lax.ppermute(array, AXES, pairs)


def to_core(array):
    return send(array, lambda x, y, c: (x, y, 1 - c))


def together(arrays, routes):
    arrays = lax.optimization_barrier(tuple(arrays))
    return lax.optimization_barrier(tuple(send(a, to) for a, to in zip(arrays, routes, strict=True)))


RING = (
    lambda x, y, c: (x + 1, y, c),
    lambda x, y, c: (x - 1, y, c),
    lambda x, y, c: (x, y + 1, c),
    lambda x, y, c: (x, y - 1, c),
)


def ordered(first_is_mine, mine, theirs, axis):
    return jnp.concatenate(
        [jnp.where(first_is_mine, mine, theirs), jnp.where(first_is_mine, theirs, mine)], axis
    )


def packed(piece, exponent):
    scaled = (piece * jnp.exp2(-exponent)).astype(F16)
    return jnp.concatenate([scaled, jnp.broadcast_to(exponent.astype(F16), (16, piece.shape[1]))], 0)


def unpacked(message):
    exponent = message[-16:-15].astype(F32)
    return message[:-16].astype(F32) * jnp.exp2(exponent), exponent


def column_tiles(width):
    return [(start, min(256, width - start)) for start in range(0, width, 256)]


def nt(a, b):
    return lax.dot_general(a, b, (((1,), (1,)), ((), ())), preferred_element_type=F32)


def flat(block):
    return block.reshape(block.shape[0] * block.shape[1], block.shape[2])


def fetched(sems, *pairs):
    copies = [pltpu.make_async_copy(source, target, sems.at[k]) for k, (source, target) in enumerate(pairs)]
    for copy in copies:
        copy.start()
    return copies


def done(copies):
    for copy in copies:
        copy.wait()


def forward_tiles(tokens_ref, w_ref, score_ref, slope_ref, curve_ref, lifted_ref, logit_ref, first):
    n = tokens_ref.shape[0] // 2
    for kind in (0, 1):
        rows = slice(kind * n, kind * n + n)
        total = jnp.zeros((n, 128), F32) if first is None else first[rows, :]
        for start, width in column_tiles(w_ref.shape[2]):
            cols = slice(start, start + width)
            preact = jnp.dot(tokens_ref[rows, :], flat(w_ref[:, :, cols]), preferred_element_type=F32)
            score = score_ref[:, cols]
            squash = jax.nn.sigmoid(preact)
            rest = 1.0 - squash
            act = preact * squash * score
            for lane in range(0, width, 128):
                total = total + act[:, lane : lane + 128]
            slope = squash * (1.0 + preact * rest) * score
            slope_ref[rows, cols] = slope
            if kind == 1:
                lifted_ref[:, cols] = slope.astype(BF16)
                curve_ref[:, cols] = squash * rest * (2.0 + preact * (1.0 - 2.0 * squash)) * score
        logit_ref[rows, :] = total


def pull_back(w_ref, lifted_ref, part_ref, so_far):
    height = 2 * w_ref.shape[1]
    for k in range(w_ref.shape[0] // 2):
        rows = slice(k * height, k * height + height)
        value = nt(flat(w_ref[2 * k : 2 * k + 2]), lifted_ref[...])
        part_ref[rows, :] = value if so_far is None else so_far[rows, :] + value


def turn_of(w_ref, which, start, width):
    height = w_ref.shape[1] // 2
    return w_ref.at[:, pl.ds(pl.multiple_of(which * height, 16), height), pl.ds(start, width)]


def tokens_kernel(flag_ref, fake_hbm, real_hbm, other_hbm, tokens_hbm, tokens_t_hbm, peak_ref,
                  own_ref, other_ref, tokens_ref, tokens_t_ref, sems):
    tok = fake_hbm.shape[0]
    done(
        fetched(
            sems,
            (fake_hbm, own_ref.at[0:tok, :]),
            (real_hbm, own_ref.at[tok : 2 * tok, :]),
            (other_hbm, other_ref),
        )
    )
    first = flag_ref[0] == 0
    for kind in (0, 1):
        mine, theirs = (ref[kind * tok : kind * tok + tok, :] for ref in (own_ref, other_ref))
        start = 2 * kind * tok
        tokens_ref[start : start + tok, :] = jnp.where(first, mine, theirs)
        tokens_ref[start + tok : start + 2 * tok, :] = jnp.where(first, theirs, mine)
        peak = peak_of(tokens_ref[start : start + 2 * tok, :])
        peak_ref[8 * kind : 8 * kind + 8, :] = jnp.broadcast_to(peak, (8, 128))
    tokens_t_ref[...] = tokens_ref[...].T
    done(fetched(sems, (tokens_ref, tokens_hbm), (tokens_t_ref, tokens_t_hbm)))


def first_kernel(flag_ref, tokens_hbm, own_hbm, left_hbm, right_hbm, low_hbm, high_hbm, score_ref,
                 w_hbm, slope_hbm, curve_hbm, lifted_hbm, logit_hbm, part_hbm,
                 w_ref, slope_ref, curve_ref, lifted_ref, logit_ref, part_ref, tokens_ref, sems, out_sems):
    done(
        fetched(
            sems,
            (tokens_hbm, tokens_ref),
            (own_hbm, w_ref.at[:, :, pl.ds(0, 128)]),
            (left_hbm, w_ref.at[:, :, pl.ds(128, 128)]),
            (right_hbm, w_ref.at[:, :, pl.ds(256, 128)]),
            (low_hbm, turn_of(w_ref, flag_ref[0], 384, 256)),
            (high_hbm, turn_of(w_ref, 1 - flag_ref[0], 384, 256)),
        )
    )
    forward_tiles(tokens_ref, w_ref, score_ref, slope_ref, curve_ref, lifted_ref, logit_ref, None)
    out = fetched(
        out_sems,
        (w_ref, w_hbm), (slope_ref, slope_hbm), (curve_ref, curve_hbm), (lifted_ref, lifted_hbm), (logit_ref, logit_hbm),
    )
    pull_back(w_ref, lifted_ref, part_ref, None)
    done(out)
    done(fetched(sems, (part_ref, part_hbm)))


def second_kernel(flag_ref, tokens_hbm, low_hbm, high_hbm, across_hbm, score_ref, logit_in_hbm, part_in_hbm,
                  w_hbm, slope_hbm, curve_hbm, lifted_hbm, logit_hbm, part_hbm,
                  w_ref, slope_ref, curve_ref, lifted_ref, logit_ref, part_ref, tokens_ref, logit_in_ref, part_in_ref,
                  sems, out_sems):
    copies = fetched(
        sems,
        (tokens_hbm, tokens_ref),
        (low_hbm, turn_of(w_ref, flag_ref[0], 0, 256)),
        (high_hbm, turn_of(w_ref, 1 - flag_ref[0], 0, 256)),
        (across_hbm, w_ref.at[:, :, pl.ds(256, 128)]),
        (logit_in_hbm, logit_in_ref),
        (part_in_hbm, part_in_ref),
    )
    done(copies[:5])
    forward_tiles(tokens_ref, w_ref, score_ref, slope_ref, curve_ref, lifted_ref, logit_ref, logit_in_ref)
    out = fetched(
        out_sems,
        (w_ref, w_hbm), (slope_ref, slope_hbm), (curve_ref, curve_hbm), (lifted_ref, lifted_hbm), (logit_ref, logit_hbm),
    )
    done(copies[5:])
    pull_back(w_ref, lifted_ref, part_ref, part_in_ref)
    done(out)
    done(fetched(sems, (part_ref, part_hbm)))


def peak_of(array):
    tall = jnp.max(jnp.abs(array).astype(F32), axis=0, keepdims=True)
    return jnp.max(tall, axis=1, keepdims=True)


def term_tiles(scale, copies, tokens_t_ref, r1_t_ref, r1_ref, logits, w_ref, slope_ref, curve_ref, lifted_ref, peak_ref,
               outs, exp_ref, fake_ref, real_ref):
    n = lifted_ref.shape[0]
    fake_gain = scale * jax.nn.sigmoid(logits[:n])
    real_gain = -scale * jax.nn.sigmoid(-logits[n:])
    done(copies[:3])
    fake_ref[...] = (fake_gain * slope_ref[0:n, :]).astype(BF16)
    for start, width in column_tiles(w_ref.shape[2]):
        cols = slice(start, start + width)
        back = jnp.dot(r1_ref[...], flat(w_ref[:, :, cols]), preferred_element_type=F32)
        real_ref[:, cols] = (real_gain * slope_ref[n : 2 * n, cols] + back * curve_ref[:, cols]).astype(BF16)
    done(copies[3:])
    bound = n * (
        peak_ref[0:1, 0:1] * peak_of(fake_ref[...])
        + peak_ref[8:9, 0:1] * peak_of(real_ref[...])
        + peak_of(r1_t_ref[...]) * peak_of(lifted_ref[...])
    )
    bound = jnp.broadcast_to(bound, (16, 128))
    exp_ref[...] = jnp.ceil(jnp.log(jnp.maximum(bound, 1e-30)) * (1.0 / math.log(2.0)) + 0.01) - 15.0
    d_in = tokens_t_ref.shape[0]
    turn = d_in // (2 * NZ)
    height = 4 * turn
    for start, width, parts in outs:
        cols = slice(start, start + width)
        for row in range(0, d_in, height):
            rows = slice(row, row + height)
            value = (
                jnp.dot(tokens_t_ref[rows, 0:n], fake_ref[:, cols], preferred_element_type=F32)
                + jnp.dot(tokens_t_ref[rows, n : 2 * n], real_ref[:, cols], preferred_element_type=F32)
                + jnp.dot(r1_t_ref[rows, :], lifted_ref[:, cols], preferred_element_type=F32)
            )
            for column, turns, out in parts:
                piece = value[:, column : column + out.shape[1]]
                if turns is None:
                    out[rows, :] = piece
                else:
                    for k in range(2):
                        at = row // 2 + k * turn
                        out[at : at + turn, :] = piece[(2 * k + turns) * turn : (2 * k + turns + 1) * turn, :]


def third_kernel(scale, tokens_t_hbm, part_hbm, part_in_hbm, logit_hbm, logit_in_hbm, w_hbm, slope_hbm, curve_hbm,
                 lifted_hbm, peak_ref, low_ref, high_ref, across_ref, exp_ref, r1_t_hbm, r1_hbm, logits_hbm,
                 fake_ref, real_ref, tokens_t_ref, part_ref, part_in_ref, logit_ref, logit_in_ref, w_ref, slope_ref,
                 curve_ref, lifted_ref, r1_t_ref, r1_ref, logits_ref, sems, out_sems):
    copies = fetched(
        sems,
        (part_hbm, part_ref), (part_in_hbm, part_in_ref), (logit_hbm, logit_ref), (logit_in_hbm, logit_in_ref),
        (w_hbm, w_ref), (slope_hbm, slope_ref), (curve_hbm, curve_ref), (lifted_hbm, lifted_ref),
        (tokens_t_hbm, tokens_t_ref),
    )
    done(copies[:4])
    r1_t_ref[...] = (scale * R1_WEIGHT * (part_ref[...] + part_in_ref[...])).astype(BF16)
    r1_ref[...] = r1_t_ref[...].T
    logits = jnp.sum(logit_ref[...] + logit_in_ref[...], axis=1, keepdims=True)
    logits_ref[...] = jnp.broadcast_to(logits, logits_ref.shape)
    out = fetched(out_sems, (r1_t_ref, r1_t_hbm), (r1_ref, r1_hbm), (logits_ref, logits_hbm))
    outs = [(0, 256, [(0, 0, low_ref), (0, 1, high_ref)]), (256, 128, [(0, None, across_ref)])]
    term_tiles(scale, copies[4:], tokens_t_ref, r1_t_ref, r1_ref, logits, w_ref, slope_ref, curve_ref, lifted_ref,
               peak_ref, outs, exp_ref, fake_ref, real_ref)
    done(out)


def fourth_kernel(scale, tokens_t_hbm, r1_t_hbm, r1_hbm, logits_hbm, w_hbm, slope_hbm, curve_hbm, lifted_hbm, peak_ref,
                  own_ref, left_ref, right_ref, low_ref, high_ref, exp_ref,
                  fake_ref, real_ref, tokens_t_ref, r1_t_ref, r1_ref, logits_ref, w_ref, slope_ref, curve_ref,
                  lifted_ref, sems):
    copies = fetched(
        sems,
        (logits_hbm, logits_ref), (r1_hbm, r1_ref), (w_hbm, w_ref), (slope_hbm, slope_ref), (curve_hbm, curve_ref),
        (r1_t_hbm, r1_t_ref), (lifted_hbm, lifted_ref), (tokens_t_hbm, tokens_t_ref),
    )
    done(copies[:2])
    outs = [
        (0, 256, [(0, None, own_ref), (128, None, left_ref)]),
        (256, 128, [(0, None, right_ref)]),
        (384, 256, [(0, 0, low_ref), (0, 1, high_ref)]),
    ]
    term_tiles(scale, copies[2:], tokens_t_ref, r1_t_ref, r1_ref, logits_ref[:, 0:1], w_ref, slope_ref, curve_ref,
               lifted_ref, peak_ref, outs, exp_ref, fake_ref, real_ref)


def call(kernel, flops, outs, scratch, sems, *args, flags=None):
    vmem, there = pl.BlockSpec(memory_space=pltpu.VMEM), pl.BlockSpec(memory_space=pl.ANY)
    specs = [vmem if a.size <= 4096 else there for a in args]
    if flags is not None:
        args, specs = (flags, *args), [pl.BlockSpec(memory_space=pltpu.SMEM), *specs]
    return pl.pallas_call(
        kernel,
        out_shape=[jax.ShapeDtypeStruct(shape, dtype) for shape, dtype, _ in outs],
        in_specs=specs,
        out_specs=[vmem if inside else pl.BlockSpec(memory_space=pltpu.HBM) for *_, inside in outs],
        scratch_shapes=[pltpu.VMEM(shape, dtype) for shape, dtype in scratch]
        + [pltpu.SemaphoreType.DMA((k,)) for k in sems],
        compiler_params=pltpu.CompilerParams(vmem_limit_bytes=VMEM_BYTES),
        cost_estimate=pl.CostEstimate(flops=flops, bytes_accessed=8_000_000, transcendentals=0),
    )(*args)


def per_device(fake_tokens, real_tokens, proj_weight, score_vector):
    ylo, x, z, yhi, c = (lax.axis_index(a) for a in AXES)
    y = yhi * 2 + ylo
    gray_x, gray_y = ((v == 1) | (v == 2) for v in (x, y))
    core0 = c == 0
    tok = fake_tokens.shape[1]
    rows, hid = proj_weight.shape
    half = hid // 2
    d_in = rows * NZ * 4
    n = 2 * tok
    scale = math.sqrt(hid / (8 * 32 * tok))

    def slices_of(side):
        mine = lax.dynamic_slice_in_dim(proj_weight, side * half, half, 1)
        first = lax.dynamic_slice_in_dim(mine, x * 128, 128, 1)
        second = lax.dynamic_slice_in_dim(mine, 512 + ylo * 256 + gray_x * 128, 128, 1)
        return jnp.concatenate([first, second], 1)

    block = ordered(core0, slices_of(c), to_core(slices_of(1 - c)), 0)
    over_z = lax.all_to_all(jnp.broadcast_to(block[None], (NZ, *block.shape)), "z", 0, 0)
    piece_a, piece_b = over_z[:, :, :128], over_z[:, :, 128:].reshape(d_in // 2, 128)
    far_a, far_b = together(
        (piece_a.reshape(d_in // 2, 128), piece_b), (lambda x, y, c: (x, 3 - y, c), lambda x, y, c: (x ^ 1, y, c))
    )
    far_a = far_a.reshape(piece_a.shape)
    own_a = ordered(yhi == 0, piece_a[:, None], far_a[:, None], 1).reshape(d_in, 128)
    own_b = ordered(~gray_x, piece_b, far_b, 1)

    own_tokens = jnp.concatenate([fake_tokens[0], real_tokens[0]], 0)
    tokens, tokens_t, peak = call(
        tokens_kernel, 2 * n * d_in * 128,
        [((2 * n, d_in), BF16, False), ((d_in, 2 * n), BF16, False), ((16, 128), F32, True)],
        [((n, d_in), BF16), ((n, d_in), BF16), ((2 * n, d_in), BF16), ((d_in, 2 * n), BF16)], [3],
        fake_tokens[0], real_tokens[0], to_core(own_tokens),
        flags=c[None].astype(jnp.int32),
    )

    left_a, right_a, left_b, right_b = together((own_a, own_a, own_b, own_b), RING)
    across_a, across_b = together((left_a, left_b), (RING[0], RING[2]))

    def score_at(start, width):
        return lax.dynamic_slice_in_dim(score_vector, c * half + start, width, 0)

    score_1 = jnp.concatenate(
        [score_at((x + k) % 4 * 128, 128) for k in (0, 3, 1)] + [score_at(512 + (1 - ylo) * 256, 256)]
    )[None]
    score_2 = jnp.concatenate([score_at(512 + ylo * 256, 256), score_at((x + 2) % 4 * 128, 128)])[None]
    yhi_left, yhi_right = (y + 3) % 4 // 2, (y + 1) % 4 // 2

    turn = d_in // NZ
    in_turns = lambda array: array.reshape(NZ, array.shape[0] // NZ, array.shape[1])

    def states(width):
        return [
            ((NZ, turn, width), BF16),
            ((2 * n, width), F32),
            ((n, width), F32),
            ((n, width), BF16),
            ((2 * n, 128), F32),
            ((d_in, n), F32),
        ]

    def kept(shapes):
        return [(*shape, False) for shape in shapes]

    wide, narrow = 640, 384
    w_1, slope_1, curve_1, lifted_1, logit_1, part_1 = call(
        first_kernel, 6 * n * d_in * wide, kept(states(wide)), [*states(wide), ((2 * n, d_in), BF16)], [6, 5],
        tokens, *map(in_turns, (own_a, left_a, right_a, left_b, right_b)), score_1,
        flags=yhi_left[None].astype(jnp.int32),
    )
    w_2, slope_2, curve_2, lifted_2, logit, part = call(
        second_kernel, 6 * n * d_in * narrow, kept(states(narrow)),
        [*states(narrow), ((2 * n, d_in), BF16), *states(narrow)[4:]], [6, 5],
        tokens, *map(in_turns, (own_b, across_b, across_a)), score_2, logit_1, part_1,
        flags=yhi[None].astype(jnp.int32),
    )
    part_in, logit_in = to_core(part), to_core(logit)

    def works(width):
        return [((n, width), BF16)] * 2

    side = [((d_in // 2, 256), F32, True)] * 2
    strip, exps = ((d_in, 128), F32, True), ((16, 128), F32, True)
    r1s = [((d_in, n), BF16), ((n, d_in), BF16), ((2 * n, 128), F32)]
    tall = ((d_in, 2 * n), BF16)
    *_, logit_shape, part_shape = states(narrow)
    low_2, high_2, far_a, exp_2, r1_t, r1, logits = call(
        functools.partial(third_kernel, scale), 8 * n * d_in * narrow, [*side, strip, exps, *kept(r1s)],
        [*works(narrow), tall, part_shape, part_shape, logit_shape, logit_shape, *states(narrow)[:4], *r1s], [9, 3],
        tokens_t, part, part_in, logit, logit_in, w_2, slope_2, curve_2, lifted_2, peak,
    )
    own_1, left_1, right_1, low_1, high_1, exp_1 = call(
        functools.partial(fourth_kernel, scale), 8 * n * d_in * wide, [strip, strip, strip, *side, exps],
        [*works(wide), tall, *r1s, *states(wide)[:4]], [8],
        tokens_t, r1_t, r1, logits, w_1, slope_1, curve_1, lifted_1, peak,
    )
    exp_1, exp_2 = exp_1[:1], exp_2[:1]
    twice = lambda row: jnp.concatenate([row, row], 1)

    own_2 = jnp.where(yhi == 0, low_2, high_2)
    far_b = jnp.where(yhi == 0, high_2, low_2)
    a_up, b_up = together((packed(far_a, exp_2), packed(far_b, twice(exp_2))), (RING[0], RING[2]))

    def joined(piece, exponent, arrived):
        values, theirs = unpacked(arrived)
        return packed(piece + values, jnp.maximum(exponent, theirs) + 1.0)

    right_b = jnp.where(yhi_right == 0, low_1, high_1)
    left_b = jnp.where(yhi_left == 0, low_1, high_1)
    from_left_a, from_right_a, from_left_b, from_right_b = together(
        (
            joined(right_1, exp_1, a_up),
            packed(left_1, exp_1),
            joined(right_b, twice(exp_1), b_up),
            packed(left_b, twice(exp_1)),
        ),
        RING,
    )

    def three(own, exponent, one, two):
        (one, exp_one), (two, exp_two) = unpacked(one), unpacked(two)
        return own + one + two, jnp.maximum(exponent, jnp.maximum(exp_one, exp_two)) + 2.0

    top = jnp.maximum(exp_1, exp_2)
    sum_a, exp_a = three(own_1, top, from_left_a, from_right_a)
    sum_b, exp_b = three(own_2, twice(top), from_left_b, from_right_b)

    turns = sum_a.reshape(NZ, 2, 2 * rows, 128)
    keep_a = jnp.where(yhi == 0, turns[:, 0], turns[:, 1]).reshape(d_in // 2, 128)
    give_a = jnp.where(yhi == 0, turns[:, 1], turns[:, 0]).reshape(d_in // 2, 128)
    keep_b = jnp.where(gray_x, sum_b[:, 128:], sum_b[:, :128])
    give_b = jnp.where(gray_x, sum_b[:, :128], sum_b[:, 128:])
    got_a, got_b = together(
        (packed(give_a, exp_a), packed(give_b, exp_b[:, :128])),
        (lambda x, y, c: (x, 3 - y, c), lambda x, y, c: (x ^ 1, y, c)),
    )
    turns_a = (keep_a + unpacked(got_a)[0]).reshape(NZ, 2, rows, 128)
    turns_b = (keep_b + unpacked(got_b)[0]).reshape(NZ, 2, rows, 128)

    def split_rows(turns, second):
        return jnp.where(second, turns[:, 1], turns[:, 0]), jnp.where(second, turns[:, 0], turns[:, 1])

    keep_a, give_a = split_rows(turns_a, gray_y)
    keep_b, give_b = split_rows(turns_b, x >= 2)
    got_a, got_b = together(
        (give_a, give_b), (lambda x, y, c: (x, y ^ 1, c), lambda x, y, c: (3 - x, y, c))
    )
    both = jnp.concatenate([keep_a + got_a, keep_b + got_b], 2)
    both = jnp.sum(lax.all_to_all(both, "z", 0, 0), 0)

    spread = lax.all_to_all(jnp.broadcast_to(both[None], (8, *both.shape)), ("ylo", "x"), 0, 0)
    spread = spread.reshape(2, 4, rows, 256)

    def row_group(r):
        pick = jnp.where(yhi == r, spread[0, :, :, :128], spread[1, :, :, :128])
        order = (0, 1) if r == 0 else (3, 2)
        return jnp.concatenate(
            [pick[k] for k in range(4)] + [spread[v, k, :, 128:] for v in (0, 1) for k in order], 1
        )

    zero, one = row_group(0), row_group(1)
    theirs = to_core(jnp.where(core0, one, zero))
    return ordered(core0, jnp.where(core0, zero, one), theirs, 1)


def solution(mesh):
    split = Mesh(mesh.devices.reshape(2, NX, NZ, 2, 2), AXES)
    tokens = P(("ylo", "x"), ("z", "yhi", "c"), None)
    shard = P(("z", "yhi", "c"), None)
    return jax.shard_map(
        per_device, mesh=split, in_specs=(tokens, tokens, shard, P()), out_specs=shard, check_vma=False
    )
```

```python
import functools
import math

import jax
import jax.numpy as jnp
from jax import lax
from jax.experimental import pallas as pl
from jax.experimental.pallas import tpu as pltpu
from jax.sharding import Mesh
from jax.sharding import PartitionSpec as P

R1_WEIGHT = 40.0
NX, NY, NZ = 4, 4, 8
AXES = ("ylo", "x", "z", "yhi", "c")
BF16, F16, F32 = jnp.bfloat16, jnp.float16, jnp.float32
VMEM_BYTES = 56 * 1024 * 1024


def flat_index(x, y, z, c):
    return ((y % 2) * NX + x) * (NZ * 4) + z * 4 + (y // 2) * 2 + c


def send(array, to):
    pairs = []
    for x in range(NX):
        for y in range(NY):
            for z in range(NZ):
                for c in range(2):
                    tx, ty, tc = to(x, y, c)
                    pairs.append((flat_index(x, y, z, c), flat_index(tx % NX, ty % NY, z, tc)))
    return lax.ppermute(array, AXES, pairs)


def to_core(array):
    return send(array, lambda x, y, c: (x, y, 1 - c))


def together(arrays, routes, beside=None, extra=()):
    arrays = lax.optimization_barrier((*arrays, *extra))
    sent = tuple(send(a, to) for a, to in zip(arrays, routes))
    return lax.optimization_barrier((*sent, *(beside(*arrays[len(sent) :]) if beside else ())))


RING = (
    lambda x, y, c: (x + 1, y, c),
    lambda x, y, c: (x - 1, y, c),
    lambda x, y, c: (x, y + 1, c),
    lambda x, y, c: (x, y - 1, c),
)


def ordered(first_is_mine, mine, theirs, axis):
    return jnp.concatenate(
        [jnp.where(first_is_mine, mine, theirs), jnp.where(first_is_mine, theirs, mine)], axis
    )


def packed(piece, exponent):
    scaled = (piece * jnp.exp2(-exponent)).astype(F16)
    return jnp.concatenate([scaled, jnp.broadcast_to(exponent.astype(F16), (16, piece.shape[1]))], 0)


def unpacked(message):
    exponent = message[-16:-15].astype(F32)
    return message[:-16].astype(F32) * jnp.exp2(exponent), exponent


def column_tiles(width):
    return [(start, min(256, width - start)) for start in range(0, width, 256)]


def nt(a, b):
    return lax.dot_general(a, b, (((1,), (1,)), ((), ())), preferred_element_type=F32)


def flat(block):
    return block.reshape(block.shape[0] * block.shape[1], block.shape[2])


def fetched(sems, *pairs):
    copies = [pltpu.make_async_copy(source, target, sems.at[k]) for k, (source, target) in enumerate(pairs)]
    for copy in copies:
        copy.start()
    return copies


def done(copies):
    for copy in copies:
        copy.wait()


def forward_tiles(tokens_ref, w_ref, score_ref, slope_ref, curve_ref, lifted_ref, logit_ref, first):
    n = tokens_ref.shape[0] // 2
    for kind in (0, 1):
        rows = slice(kind * n, kind * n + n)
        total = jnp.zeros((n, 128), F32) if first is None else first[rows, :]
        for start, width in column_tiles(w_ref.shape[2]):
            cols = slice(start, start + width)
            preact = jnp.dot(tokens_ref[rows, :], flat(w_ref[:, :, cols]), preferred_element_type=F32)
            score = score_ref[:, cols]
            squash = jax.nn.sigmoid(preact)
            rest = 1.0 - squash
            act = preact * squash * score
            for lane in range(0, width, 128):
                total = total + act[:, lane : lane + 128]
            slope = squash * (1.0 + preact * rest) * score
            slope_ref[rows, cols] = slope
            if kind == 1:
                lifted_ref[:, cols] = slope.astype(BF16)
                curve_ref[:, cols] = squash * rest * (2.0 + preact * (1.0 - 2.0 * squash)) * score
        logit_ref[rows, :] = total


def pull_back(w_ref, lifted_ref, part_ref, so_far):
    height = 2 * w_ref.shape[1]
    for k in range(w_ref.shape[0] // 2):
        rows = slice(k * height, k * height + height)
        value = nt(flat(w_ref[2 * k : 2 * k + 2]), lifted_ref[...])
        part_ref[rows, :] = value if so_far is None else so_far[rows, :] + value


def turn_of(w_ref, which, start, width):
    height = w_ref.shape[1] // 2
    return w_ref.at[:, pl.ds(pl.multiple_of(which * height, 16), height), pl.ds(start, width)]


def tokens_kernel(flag_ref, fake_hbm, real_hbm, other_hbm, tokens_hbm, tokens_t_hbm, peak_ref,
                  own_ref, other_ref, tokens_ref, tokens_t_ref, sems):
    tok = fake_hbm.shape[0]
    done(
        fetched(
            sems,
            (fake_hbm, own_ref.at[0:tok, :]),
            (real_hbm, own_ref.at[tok : 2 * tok, :]),
            (other_hbm, other_ref),
        )
    )
    first = flag_ref[0] == 0
    for kind in (0, 1):
        mine, theirs = (ref[kind * tok : kind * tok + tok, :] for ref in (own_ref, other_ref))
        start = 2 * kind * tok
        tokens_ref[start : start + tok, :] = jnp.where(first, mine, theirs)
        tokens_ref[start + tok : start + 2 * tok, :] = jnp.where(first, theirs, mine)
        peak = peak_of(tokens_ref[start : start + 2 * tok, :])
        peak_ref[8 * kind : 8 * kind + 8, :] = jnp.broadcast_to(peak, (8, 128))
    tokens_t_ref[...] = tokens_ref[...].T
    done(fetched(sems, (tokens_ref, tokens_hbm), (tokens_t_ref, tokens_t_hbm)))


def first_kernel(flag_ref, tokens_hbm, own_hbm, left_hbm, right_hbm, low_hbm, high_hbm, score_ref,
                 w_hbm, slope_hbm, curve_hbm, lifted_hbm, logit_hbm, part_hbm,
                 w_ref, slope_ref, curve_ref, lifted_ref, logit_ref, part_ref, tokens_ref, sems, out_sems):
    done(
        fetched(
            sems,
            (tokens_hbm, tokens_ref),
            (own_hbm, w_ref.at[:, :, pl.ds(0, 128)]),
            (left_hbm, w_ref.at[:, :, pl.ds(128, 128)]),
            (right_hbm, w_ref.at[:, :, pl.ds(256, 128)]),
            (low_hbm, turn_of(w_ref, flag_ref[0], 384, 256)),
            (high_hbm, turn_of(w_ref, 1 - flag_ref[0], 384, 256)),
        )
    )
    forward_tiles(tokens_ref, w_ref, score_ref, slope_ref, curve_ref, lifted_ref, logit_ref, None)
    out = fetched(
        out_sems,
        (w_ref, w_hbm), (slope_ref, slope_hbm), (curve_ref, curve_hbm), (lifted_ref, lifted_hbm), (logit_ref, logit_hbm),
    )
    pull_back(w_ref, lifted_ref, part_ref, None)
    done(out)
    done(fetched(sems, (part_ref, part_hbm)))


def second_kernel(flag_ref, tokens_hbm, low_hbm, high_hbm, across_hbm, score_ref, logit_in_hbm, part_in_hbm,
                  w_hbm, slope_hbm, curve_hbm, lifted_hbm, logit_hbm, part_hbm,
                  w_ref, slope_ref, curve_ref, lifted_ref, logit_ref, part_ref, tokens_ref, logit_in_ref, part_in_ref,
                  sems, out_sems):
    copies = fetched(
        sems,
        (tokens_hbm, tokens_ref),
        (low_hbm, turn_of(w_ref, flag_ref[0], 0, 256)),
        (high_hbm, turn_of(w_ref, 1 - flag_ref[0], 0, 256)),
        (across_hbm, w_ref.at[:, :, pl.ds(256, 128)]),
        (logit_in_hbm, logit_in_ref),
        (part_in_hbm, part_in_ref),
    )
    done(copies[:5])
    forward_tiles(tokens_ref, w_ref, score_ref, slope_ref, curve_ref, lifted_ref, logit_ref, logit_in_ref)
    out = fetched(
        out_sems,
        (w_ref, w_hbm), (slope_ref, slope_hbm), (curve_ref, curve_hbm), (lifted_ref, lifted_hbm), (logit_ref, logit_hbm),
    )
    done(copies[5:])
    pull_back(w_ref, lifted_ref, part_ref, part_in_ref)
    done(out)
    done(fetched(sems, (part_ref, part_hbm)))


def peak_of(array):
    tall = jnp.max(jnp.abs(array).astype(F32), axis=0, keepdims=True)
    return jnp.max(tall, axis=1, keepdims=True)


def term_tiles(scale, copies, tokens_t_ref, r1_t_ref, r1_ref, logits, w_ref, slope_ref, curve_ref, lifted_ref, peak_ref,
               outs, out_sems, exp_ref, fake_ref, real_ref):
    n = lifted_ref.shape[0]
    fake_gain = scale * jax.nn.sigmoid(logits[:n])
    real_gain = -scale * jax.nn.sigmoid(-logits[n:])
    done(copies[:3])
    fake_ref[...] = (fake_gain * slope_ref[0:n, :]).astype(BF16)
    for start, width in column_tiles(w_ref.shape[2]):
        cols = slice(start, start + width)
        back = jnp.dot(r1_ref[...], flat(w_ref[:, :, cols]), preferred_element_type=F32)
        real_ref[:, cols] = (real_gain * slope_ref[n : 2 * n, cols] + back * curve_ref[:, cols]).astype(BF16)
    done(copies[3:])
    bound = n * (
        peak_ref[0:1, 0:1] * peak_of(fake_ref[...])
        + peak_ref[8:9, 0:1] * peak_of(real_ref[...])
        + peak_of(r1_t_ref[...]) * peak_of(lifted_ref[...])
    )
    bound = jnp.broadcast_to(bound, (16, 128))
    exp_ref[...] = jnp.ceil(jnp.log(jnp.maximum(bound, 1e-30)) * (1.0 / math.log(2.0)) + 0.01) - 15.0
    d_in = tokens_t_ref.shape[0]
    turn = d_in // (2 * NZ)
    height = 4 * turn
    leaving = []
    for start, width, parts in outs:
        cols = slice(start, start + width)
        for row in range(0, d_in, height):
            rows = slice(row, row + height)
            value = (
                jnp.dot(tokens_t_ref[rows, 0:n], fake_ref[:, cols], preferred_element_type=F32)
                + jnp.dot(tokens_t_ref[rows, n : 2 * n], real_ref[:, cols], preferred_element_type=F32)
                + jnp.dot(r1_t_ref[rows, :], lifted_ref[:, cols], preferred_element_type=F32)
            )
            for column, turns, out, out_hbm in parts:
                piece = value[:, column : column + out.shape[1]]
                if turns is None:
                    there = rows
                    out[rows, :] = piece
                else:
                    there = slice(row // 2, row // 2 + 2 * turn)
                    for k in range(2):
                        at = row // 2 + k * turn
                        out[at : at + turn, :] = piece[(2 * k + turns) * turn : (2 * k + turns + 1) * turn, :]
                leaving.append(
                    pltpu.make_async_copy(out.at[there, :], out_hbm.at[there, :], out_sems.at[len(leaving)])
                )
                leaving[-1].start()
    done(leaving)


def third_kernel(scale, tokens_t_hbm, part_hbm, part_in_hbm, logit_hbm, logit_in_hbm, w_hbm, slope_hbm, curve_hbm,
                 lifted_hbm, peak_ref, low_hbm, high_hbm, across_hbm, exp_ref, r1_t_hbm, r1_hbm, logits_hbm,
                 fake_ref, real_ref, tokens_t_ref, part_ref, part_in_ref, logit_ref, logit_in_ref, w_ref, slope_ref,
                 curve_ref, lifted_ref, r1_t_ref, r1_ref, logits_ref, low_ref, high_ref, across_ref, sems, r1_sems, out_sems):
    copies = fetched(
        sems,
        (part_hbm, part_ref), (part_in_hbm, part_in_ref), (logit_hbm, logit_ref), (logit_in_hbm, logit_in_ref),
        (w_hbm, w_ref), (slope_hbm, slope_ref), (curve_hbm, curve_ref), (lifted_hbm, lifted_ref),
        (tokens_t_hbm, tokens_t_ref),
    )
    done(copies[:4])
    r1_t_ref[...] = (scale * R1_WEIGHT * (part_ref[...] + part_in_ref[...])).astype(BF16)
    r1_ref[...] = r1_t_ref[...].T
    logits = jnp.sum(logit_ref[...] + logit_in_ref[...], axis=1, keepdims=True)
    logits_ref[...] = jnp.broadcast_to(logits, logits_ref.shape)
    out = fetched(r1_sems, (r1_t_ref, r1_t_hbm), (r1_ref, r1_hbm), (logits_ref, logits_hbm))
    outs = [
        (0, 256, [(0, 0, low_ref, low_hbm), (0, 1, high_ref, high_hbm)]),
        (256, 128, [(0, None, across_ref, across_hbm)]),
    ]
    term_tiles(scale, copies[4:], tokens_t_ref, r1_t_ref, r1_ref, logits, w_ref, slope_ref, curve_ref, lifted_ref,
               peak_ref, outs, out_sems, exp_ref, fake_ref, real_ref)
    done(out)


def fourth_kernel(scale, tokens_t_hbm, r1_t_hbm, r1_hbm, logits_hbm, w_hbm, slope_hbm, curve_hbm, lifted_hbm, peak_ref,
                  own_hbm, left_hbm, right_hbm, low_hbm, high_hbm, exp_ref,
                  fake_ref, real_ref, tokens_t_ref, r1_t_ref, r1_ref, logits_ref, w_ref, slope_ref, curve_ref,
                  lifted_ref, own_ref, left_ref, right_ref, low_ref, high_ref, sems, out_sems):
    copies = fetched(
        sems,
        (logits_hbm, logits_ref), (r1_hbm, r1_ref), (w_hbm, w_ref), (slope_hbm, slope_ref), (curve_hbm, curve_ref),
        (r1_t_hbm, r1_t_ref), (lifted_hbm, lifted_ref), (tokens_t_hbm, tokens_t_ref),
    )
    done(copies[:2])
    outs = [
        (128, 256, [(0, None, left_ref, left_hbm), (128, None, right_ref, right_hbm)]),
        (384, 256, [(0, 0, low_ref, low_hbm), (0, 1, high_ref, high_hbm)]),
        (0, 128, [(0, None, own_ref, own_hbm)]),
    ]
    term_tiles(scale, copies[2:], tokens_t_ref, r1_t_ref, r1_ref, logits_ref[:, 0:1], w_ref, slope_ref, curve_ref,
               lifted_ref, peak_ref, outs, out_sems, exp_ref, fake_ref, real_ref)


def call(kernel, flops, outs, scratch, sems, *args, flags=None):
    vmem, there = pl.BlockSpec(memory_space=pltpu.VMEM), pl.BlockSpec(memory_space=pl.ANY)
    specs = [vmem if a.size <= 4096 else there for a in args]
    if flags is not None:
        args, specs = (flags, *args), [pl.BlockSpec(memory_space=pltpu.SMEM), *specs]
    return pl.pallas_call(
        kernel,
        out_shape=[jax.ShapeDtypeStruct(shape, dtype) for shape, dtype, _ in outs],
        in_specs=specs,
        out_specs=[vmem if inside else pl.BlockSpec(memory_space=pltpu.HBM) for *_, inside in outs],
        scratch_shapes=[pltpu.VMEM(shape, dtype) for shape, dtype in scratch]
        + [pltpu.SemaphoreType.DMA((k,)) for k in sems],
        compiler_params=pltpu.CompilerParams(vmem_limit_bytes=VMEM_BYTES),
        cost_estimate=pl.CostEstimate(flops=flops, bytes_accessed=8_000_000, transcendentals=0),
    )(*args)


def per_device(fake_tokens, real_tokens, proj_weight, score_vector):
    ylo, x, z, yhi, c = (lax.axis_index(a) for a in AXES)
    y = yhi * 2 + ylo
    gray_x, gray_y = ((v == 1) | (v == 2) for v in (x, y))
    core0 = c == 0
    tok = fake_tokens.shape[1]
    rows, hid = proj_weight.shape
    half = hid // 2
    d_in = rows * NZ * 4
    n = 2 * tok
    scale = math.sqrt(hid / (8 * 32 * tok))

    def slices_of(side):
        mine = lax.dynamic_slice_in_dim(proj_weight, side * half, half, 1)
        first = lax.dynamic_slice_in_dim(mine, x * 128, 128, 1)
        second = lax.dynamic_slice_in_dim(mine, 512 + ylo * 256 + gray_x * 128, 128, 1)
        return jnp.concatenate([first, second], 1)

    block = ordered(core0, slices_of(c), to_core(slices_of(1 - c)), 0)
    over_z = lax.all_to_all(jnp.broadcast_to(block[None], (NZ, *block.shape)), "z", 0, 0)
    piece_a, piece_b = over_z[:, :, :128], over_z[:, :, 128:].reshape(d_in // 2, 128)
    far_a, far_b = together(
        (piece_a.reshape(d_in // 2, 128), piece_b), (lambda x, y, c: (x, 3 - y, c), lambda x, y, c: (x ^ 1, y, c))
    )
    far_a = far_a.reshape(piece_a.shape)
    own_a = ordered(yhi == 0, piece_a[:, None], far_a[:, None], 1).reshape(d_in, 128)
    own_b = ordered(~gray_x, piece_b, far_b, 1)

    own_tokens = jnp.concatenate([fake_tokens[0], real_tokens[0]], 0)
    def join_tokens(other_tokens):
        return call(
            tokens_kernel, 2 * n * d_in * 128,
            [((2 * n, d_in), BF16, False), ((d_in, 2 * n), BF16, False), ((16, 128), F32, True)],
            [((n, d_in), BF16), ((n, d_in), BF16), ((2 * n, d_in), BF16), ((d_in, 2 * n), BF16)], [3],
            fake_tokens[0], real_tokens[0], other_tokens,
            flags=c[None].astype(jnp.int32),
        )

    left_a, right_a, left_b, right_b, tokens, tokens_t, peak = together(
        (own_a, own_a, own_b, own_b), RING, join_tokens, (to_core(own_tokens),)
    )
    across_a, across_b = together((left_a, left_b), (RING[0], RING[2]))

    def score_at(start, width):
        return lax.dynamic_slice_in_dim(score_vector, c * half + start, width, 0)

    score_1 = jnp.concatenate(
        [score_at((x + k) % 4 * 128, 128) for k in (0, 3, 1)] + [score_at(512 + (1 - ylo) * 256, 256)]
    )[None]
    score_2 = jnp.concatenate([score_at(512 + ylo * 256, 256), score_at((x + 2) % 4 * 128, 128)])[None]
    yhi_left, yhi_right = (y + 3) % 4 // 2, (y + 1) % 4 // 2

    turn = d_in // NZ
    in_turns = lambda array: array.reshape(NZ, array.shape[0] // NZ, array.shape[1])

    def states(width):
        return [
            ((NZ, turn, width), BF16),
            ((2 * n, width), F32),
            ((n, width), F32),
            ((n, width), BF16),
            ((2 * n, 128), F32),
            ((d_in, n), F32),
        ]

    def kept(shapes):
        return [(*shape, False) for shape in shapes]

    wide, narrow = 640, 384
    w_1, slope_1, curve_1, lifted_1, logit_1, part_1 = call(
        first_kernel, 6 * n * d_in * wide, kept(states(wide)), [*states(wide), ((2 * n, d_in), BF16)], [6, 5],
        tokens, *map(in_turns, (own_a, left_a, right_a, left_b, right_b)), score_1,
        flags=yhi_left[None].astype(jnp.int32),
    )
    w_2, slope_2, curve_2, lifted_2, logit, part = call(
        second_kernel, 6 * n * d_in * narrow, kept(states(narrow)),
        [*states(narrow), ((2 * n, d_in), BF16), *states(narrow)[4:]], [6, 5],
        tokens, *map(in_turns, (own_b, across_b, across_a)), score_2, logit_1, part_1,
        flags=yhi[None].astype(jnp.int32),
    )
    part_in, logit_in = to_core(part), to_core(logit)

    def works(width):
        return [((n, width), BF16)] * 2

    side = [((d_in // 2, 256), F32)] * 2
    strip, exps = ((d_in, 128), F32), ((16, 128), F32, True)
    r1s = [((d_in, n), BF16), ((n, d_in), BF16), ((2 * n, 128), F32)]
    tall = ((d_in, 2 * n), BF16)
    *_, logit_shape, part_shape = states(narrow)
    low_2, high_2, far_a, exp_2, r1_t, r1, logits = call(
        functools.partial(third_kernel, scale), 8 * n * d_in * narrow, [*kept([*side, strip]), exps, *kept(r1s)],
        [*works(narrow), tall, part_shape, part_shape, logit_shape, logit_shape, *states(narrow)[:4], *r1s, *side, strip],
        [9, 3, 12],
        tokens_t, part, part_in, logit, logit_in, w_2, slope_2, curve_2, lifted_2, peak,
    )
    exp_2 = exp_2[:1]
    twice = lambda row: jnp.concatenate([row, row], 1)

    own_2 = jnp.where(yhi == 0, low_2, high_2)
    far_b = jnp.where(yhi == 0, high_2, low_2)

    def rest_of_term(r1_t):
        return call(
            functools.partial(fourth_kernel, scale), 8 * n * d_in * wide, [*kept([strip] * 3 + side), exps],
            [*works(wide), tall, *r1s, *states(wide)[:4], *[strip] * 3, *side], [8, 20],
            tokens_t, r1_t, r1, logits, w_1, slope_1, curve_1, lifted_1, peak,
        )

    across_a, across_b, own_1, left_1, right_1, low_1, high_1, exp_1 = together(
        (packed(far_a, exp_2), packed(far_b, twice(exp_2))),
        (lambda x, y, c: (x + 2, y, c), lambda x, y, c: (x, y + 2, c)),
        rest_of_term,
        (r1_t,),
    )
    exp_1 = exp_1[:1]
    right_b = jnp.where(yhi_right == 0, low_1, high_1)
    left_b = jnp.where(yhi_left == 0, low_1, high_1)
    from_left_a, from_right_a, from_left_b, from_right_b = together(
        (
            packed(right_1, exp_1),
            packed(left_1, exp_1),
            packed(right_b, twice(exp_1)),
            packed(left_b, twice(exp_1)),
        ),
        RING,
    )

    def summed(own, exponent, *messages):
        for values, theirs in map(unpacked, messages):
            own, exponent = own + values, jnp.maximum(exponent, theirs)
        return own, exponent + 2.0

    top = jnp.maximum(exp_1, exp_2)
    sum_a, exp_a = summed(own_1, top, from_left_a, from_right_a, across_a)
    sum_b, exp_b = summed(own_2, twice(top), from_left_b, from_right_b, across_b)

    turns = sum_a.reshape(NZ, 2, 2 * rows, 128)
    keep_a = jnp.where(yhi == 0, turns[:, 0], turns[:, 1]).reshape(d_in // 2, 128)
    give_a = jnp.where(yhi == 0, turns[:, 1], turns[:, 0]).reshape(d_in // 2, 128)
    keep_b = jnp.where(gray_x, sum_b[:, 128:], sum_b[:, :128])
    give_b = jnp.where(gray_x, sum_b[:, :128], sum_b[:, 128:])
    got_a, got_b = together(
        (packed(give_a, exp_a), packed(give_b, exp_b[:, :128])),
        (lambda x, y, c: (x, 3 - y, c), lambda x, y, c: (x ^ 1, y, c)),
    )
    turns_a = (keep_a + unpacked(got_a)[0]).reshape(NZ, 2, rows, 128)
    turns_b = (keep_b + unpacked(got_b)[0]).reshape(NZ, 2, rows, 128)

    def split_rows(turns, second):
        return jnp.where(second, turns[:, 1], turns[:, 0]), jnp.where(second, turns[:, 0], turns[:, 1])

    keep_a, give_a = split_rows(turns_a, gray_y)
    keep_b, give_b = split_rows(turns_b, x >= 2)
    got_a, got_b = together(
        (give_a, give_b), (lambda x, y, c: (x, y ^ 1, c), lambda x, y, c: (3 - x, y, c))
    )
    both = jnp.concatenate([keep_a + got_a, keep_b + got_b], 2)
    both = jnp.sum(lax.all_to_all(both, "z", 0, 0), 0)

    spread = lax.all_to_all(jnp.broadcast_to(both[None], (8, *both.shape)), ("ylo", "x"), 0, 0)
    spread = spread.reshape(2, 4, rows, 256)

    def row_group(r):
        pick = jnp.where(yhi == r, spread[0, :, :, :128], spread[1, :, :, :128])
        order = (0, 1) if r == 0 else (3, 2)
        return jnp.concatenate(
            [pick[k] for k in range(4)] + [spread[v, k, :, 128:] for v in (0, 1) for k in order], 1
        )

    zero, one = row_group(0), row_group(1)
    theirs = to_core(jnp.where(core0, one, zero))
    return ordered(core0, jnp.where(core0, zero, one), theirs, 1)


def solution(mesh):
    split = Mesh(mesh.devices.reshape(2, NX, NZ, 2, 2), AXES)
    tokens = P(("ylo", "x"), ("z", "yhi", "c"), None)
    shard = P(("z", "yhi", "c"), None)
    return jax.shard_map(
        per_device, mesh=split, in_specs=(tokens, tokens, shard, P()), out_specs=shard, check_vma=False
    )
```

```python
import functools
import math

import jax
import jax.numpy as jnp
from jax import lax
from jax.experimental import pallas as pl
from jax.experimental.pallas import tpu as pltpu
from jax.sharding import Mesh
from jax.sharding import PartitionSpec as P

R1_WEIGHT = 40.0
NX, NY, NZ = 4, 4, 8
AXES = ("ylo", "x", "z", "yhi", "c")
BF16, F16, F32 = jnp.bfloat16, jnp.float16, jnp.float32


def flat_index(x, y, z, c):
    return ((y % 2) * NX + x) * (NZ * 4) + z * 4 + (y // 2) * 2 + c


def send(array, to):
    pairs = []
    for x in range(NX):
        for y in range(NY):
            for z in range(NZ):
                for c in range(2):
                    tx, ty, tc = to(x, y, c)
                    pairs.append((flat_index(x, y, z, c), flat_index(tx % NX, ty % NY, z, tc)))
    return lax.ppermute(array, AXES, pairs)


def to_core(array):
    return send(array, lambda x, y, c: (x, y, 1 - c))


def together(arrays, routes, beside=None, extra=()):
    arrays = lax.optimization_barrier((*arrays, *extra))
    sent = tuple(send(a, to) for a, to in zip(arrays, routes))
    return lax.optimization_barrier((*sent, *(beside(*arrays[len(sent) :]) if beside else ())))


RING = (
    lambda x, y, c: (x + 1, y, c),
    lambda x, y, c: (x - 1, y, c),
    lambda x, y, c: (x, y + 1, c),
    lambda x, y, c: (x, y - 1, c),
)


def ordered(first_is_mine, mine, theirs, axis):
    return jnp.concatenate(
        [jnp.where(first_is_mine, mine, theirs), jnp.where(first_is_mine, theirs, mine)], axis
    )


def packed(piece, exponent):
    scaled = (piece * jnp.exp2(-exponent)).astype(F16)
    return jnp.concatenate([scaled, jnp.broadcast_to(exponent.astype(F16), (16, piece.shape[1]))], 0)


def unpacked(message):
    exponent = message[-16:-15].astype(F32)
    return message[:-16].astype(F32) * jnp.exp2(exponent), exponent


def column_tiles(width):
    return [(start, min(256, width - start)) for start in range(0, width, 256)]


def nt(a, b):
    return lax.dot_general(a, b, (((1,), (1,)), ((), ())), preferred_element_type=F32)


def forward_tiles(tokens_ref, w_ref, score_ref, slope_ref, curve_ref, lifted_ref, logit_ref, first):
    n = tokens_ref.shape[0] // 2
    for kind in (0, 1):
        rows = slice(kind * n, kind * n + n)
        total = jnp.zeros((n, 128), F32) if first is None else first[rows, :]
        for start, width in column_tiles(w_ref.shape[1]):
            cols = slice(start, start + width)
            preact = jnp.dot(tokens_ref[rows, :], w_ref[:, cols], preferred_element_type=F32)
            score = score_ref[:, cols]
            squash = jax.nn.sigmoid(preact)
            rest = 1.0 - squash
            act = preact * squash * score
            for lane in range(0, width, 128):
                total = total + act[:, lane : lane + 128]
            slope = squash * (1.0 + preact * rest) * score
            slope_ref[rows, cols] = slope
            if kind == 1:
                lifted_ref[:, cols] = slope.astype(BF16)
                curve_ref[:, cols] = squash * rest * (2.0 + preact * (1.0 - 2.0 * squash)) * score
        logit_ref[rows, :] = total


def pull_back(w_ref, lifted_ref, part_ref, so_far):
    for start in range(0, w_ref.shape[0], 512):
        rows = slice(start, start + 512)
        value = nt(w_ref[rows, :], lifted_ref[...])
        part_ref[rows, :] = value if so_far is None else so_far[rows, :] + value


def place_pair(w_ref, column, low_ref, high_ref, swap):
    width = low_ref.shape[1]
    turn = w_ref.shape[0] // (2 * NZ)
    for z in range(NZ):
        rows = slice(z * turn, z * turn + turn)
        low, high = low_ref[rows, :], high_ref[rows, :]
        w_ref[2 * z * turn : 2 * z * turn + turn, column : column + width] = jnp.where(swap, high, low)
        w_ref[2 * z * turn + turn : 2 * z * turn + 2 * turn, column : column + width] = jnp.where(swap, low, high)


def fetched(sems, *pairs):
    copies = [pltpu.make_async_copy(source, target, sems.at[k]) for k, (source, target) in enumerate(pairs)]
    for copy in copies:
        copy.start()
    return copies


def done(copies):
    for copy in copies:
        copy.wait()


def first_kernel(flag_ref, tokens_ref, own_ref, left_ref, right_ref, low_ref, high_ref, score_ref,
                 w_hbm, slope_hbm, curve_hbm, lifted_hbm, logit_ref, part_ref,
                 w_ref, slope_ref, curve_ref, lifted_ref, sems):
    w_ref[:, 0:128] = own_ref[...]
    w_ref[:, 128:256] = left_ref[...]
    w_ref[:, 256:384] = right_ref[...]
    place_pair(w_ref, 384, low_ref, high_ref, flag_ref[0] == 1)
    forward_tiles(tokens_ref, w_ref, score_ref, slope_ref, curve_ref, lifted_ref, logit_ref, None)
    copies = fetched(
        sems, (w_ref, w_hbm), (slope_ref, slope_hbm), (curve_ref, curve_hbm), (lifted_ref, lifted_hbm)
    )
    pull_back(w_ref, lifted_ref, part_ref, None)
    done(copies)


def tokens_kernel(flag_ref, fake_ref, real_ref, other_ref, tokens_ref, tokens_t_hbm, peak_ref, tokens_t_ref, sems):
    tok = fake_ref.shape[0]
    first = flag_ref[0] == 0
    for kind, own in enumerate((fake_ref, real_ref)):
        mine, theirs = own[...], other_ref[kind * tok : kind * tok + tok, :]
        start = 2 * kind * tok
        tokens_ref[start : start + tok, :] = jnp.where(first, mine, theirs)
        tokens_ref[start + tok : start + 2 * tok, :] = jnp.where(first, theirs, mine)
        peak = peak_of(tokens_ref[start : start + 2 * tok, :])
        peak_ref[8 * kind : 8 * kind + 8, :] = jnp.broadcast_to(peak, (8, 128))
    tokens_t_ref[...] = tokens_ref[...].T
    done(fetched(sems, (tokens_t_ref, tokens_t_hbm)))


def second_kernel(flag_ref, tokens_ref, low_ref, high_ref, across_ref, score_ref, logit_in_ref, part_in_ref,
                  w_hbm, slope_hbm, curve_hbm, lifted_hbm, logit_ref, part_ref,
                  w_ref, slope_ref, curve_ref, lifted_ref, sems):
    place_pair(w_ref, 0, low_ref, high_ref, flag_ref[0] == 1)
    w_ref[:, 256:384] = across_ref[...]
    forward_tiles(tokens_ref, w_ref, score_ref, slope_ref, curve_ref, lifted_ref, logit_ref, logit_in_ref)
    copies = fetched(
        sems, (w_ref, w_hbm), (slope_ref, slope_hbm), (curve_ref, curve_hbm), (lifted_ref, lifted_hbm)
    )
    pull_back(w_ref, lifted_ref, part_ref, part_in_ref)
    done(copies)


def peak_of(array):
    flat = jnp.max(jnp.abs(array).astype(F32), axis=0, keepdims=True)
    return jnp.max(flat, axis=1, keepdims=True)


def cotangents(scale, logits, r1_ref, w_ref, slope_ref, curve_ref, fake_ref, real_ref):
    n = r1_ref.shape[0]
    fake_ref[...] = (scale * jax.nn.sigmoid(logits[:n]) * slope_ref[0:n, :]).astype(BF16)
    real_gain = -scale * jax.nn.sigmoid(-logits[n:])
    for start, width in column_tiles(w_ref.shape[1]):
        cols = slice(start, start + width)
        back = jnp.dot(r1_ref[...], w_ref[:, cols], preferred_element_type=F32)
        real_ref[:, cols] = (real_gain * slope_ref[n : 2 * n, cols] + back * curve_ref[:, cols]).astype(BF16)


def third_kernel(scale, part_ref, part_in_ref, logit_ref, logit_in_ref, peak_ref,
                 w_2_hbm, slope_2_hbm, curve_2_hbm, lifted_2_hbm, tokens_t_hbm, w_1_hbm, slope_1_hbm, curve_1_hbm, lifted_1_hbm,
                 across_hbm, far_low_hbm, far_high_hbm, left_hbm, right_hbm, low_hbm, high_hbm, own_hbm, exp_ref,
                 across_ref, far_low_ref, far_high_ref, left_ref, right_ref, low_ref, high_ref, own_ref,
                 r1_t_ref, r1_ref, fake_1_ref, real_1_ref, fake_2_ref, real_2_ref,
                 tokens_t_ref, w_1_ref, slope_1_ref, curve_1_ref, lifted_1_ref,
                 w_2_ref, slope_2_ref, curve_2_ref, lifted_2_ref, sems, out_sems):
    copies = fetched(
        sems,
        (w_2_hbm, w_2_ref), (slope_2_hbm, slope_2_ref), (curve_2_hbm, curve_2_ref), (lifted_2_hbm, lifted_2_ref),
        (w_1_hbm, w_1_ref), (slope_1_hbm, slope_1_ref), (curve_1_hbm, curve_1_ref), (lifted_1_hbm, lifted_1_ref),
        (tokens_t_hbm, tokens_t_ref),
    )
    r1_t_ref[...] = (scale * R1_WEIGHT * (part_ref[...] + part_in_ref[...])).astype(BF16)
    r1_ref[...] = r1_t_ref[...].T
    logits = jnp.sum(logit_ref[...] + logit_in_ref[...], axis=1, keepdims=True)
    done(copies[:4])
    cotangents(scale, logits, r1_ref, w_2_ref, slope_2_ref, curve_2_ref, fake_2_ref, real_2_ref)
    done(copies[4:])
    cotangents(scale, logits, r1_ref, w_1_ref, slope_1_ref, curve_1_ref, fake_1_ref, real_1_ref)
    first, second = (fake_1_ref, real_1_ref, lifted_1_ref), (fake_2_ref, real_2_ref, lifted_2_ref)
    peaks = [jnp.maximum(peak_of(one[...]), peak_of(two[...])) for one, two in zip(first, second)]
    n = r1_ref.shape[0]
    bound = n * (
        peak_ref[0:1, 0:1] * peaks[0] + peak_ref[8:9, 0:1] * peaks[1] + peak_of(r1_t_ref[...]) * peaks[2]
    )
    bound = jnp.broadcast_to(bound, (16, 128))
    exp_ref[...] = jnp.ceil(jnp.log(jnp.maximum(bound, 1e-30)) * (1.0 / math.log(2.0)) + 0.01) - 15.0
    outs = [
        (second, 256, 128, [(0, None, across_ref, across_hbm)]),
        (second, 0, 256, [(0, 0, far_low_ref, far_low_hbm), (0, 1, far_high_ref, far_high_hbm)]),
        (first, 128, 256, [(0, None, left_ref, left_hbm), (128, None, right_ref, right_hbm)]),
        (first, 384, 256, [(0, 0, low_ref, low_hbm), (0, 1, high_ref, high_hbm)]),
        (first, 0, 128, [(0, None, own_ref, own_hbm)]),
    ]
    d_in = tokens_t_ref.shape[0]
    turn = d_in // (2 * NZ)
    height = 4 * turn
    leaving = []
    for (fake_ref, real_ref, lifted_ref), start, width, parts in outs:
        cols = slice(start, start + width)
        for row in range(0, d_in, height):
            rows = slice(row, row + height)
            value = (
                jnp.dot(tokens_t_ref[rows, 0:n], fake_ref[:, cols], preferred_element_type=F32)
                + jnp.dot(tokens_t_ref[rows, n : 2 * n], real_ref[:, cols], preferred_element_type=F32)
                + jnp.dot(r1_t_ref[rows, :], lifted_ref[:, cols], preferred_element_type=F32)
            )
            for column, turns, out, out_hbm in parts:
                piece = value[:, column : column + out.shape[1]]
                if turns is None:
                    there = rows
                    out[rows, :] = piece
                else:
                    there = slice(row // 2, row // 2 + 2 * turn)
                    for k in range(2):
                        at = row // 2 + k * turn
                        out[at : at + turn, :] = piece[(2 * k + turns) * turn : (2 * k + turns + 1) * turn, :]
                leaving.append(
                    pltpu.make_async_copy(out.at[there, :], out_hbm.at[there, :], out_sems.at[len(leaving)])
                )
                leaving[-1].start()
    done(leaving)


def call(kernel, flops, outs, scratch, *args, flags=None, there=(), sems=(), vmem_mib=20):
    vmem = pl.BlockSpec(memory_space=pltpu.VMEM)
    specs = [vmem] * len(args) + [pl.BlockSpec(memory_space=pltpu.HBM)] * len(there)
    args = (*args, *(pltpu.with_memory_space_constraint(a, pltpu.HBM) for a in there))
    if flags is not None:
        args, specs = (flags, *args), [pl.BlockSpec(memory_space=pltpu.SMEM), *specs]
    return pl.pallas_call(
        kernel,
        out_shape=[(pltpu.HBM if len(out) == 3 else pltpu.VMEM)(*out[:2]) for out in outs],
        in_specs=specs,
        out_specs=[pl.BlockSpec(memory_space=pltpu.HBM) if len(out) == 3 else vmem for out in outs],
        scratch_shapes=[pltpu.VMEM(shape, dtype) for shape, dtype in scratch]
        + [pltpu.SemaphoreType.DMA((k,)) for k in sems],
        compiler_params=pltpu.CompilerParams(vmem_limit_bytes=vmem_mib * 1024 * 1024),
        cost_estimate=pl.CostEstimate(flops=flops, bytes_accessed=8_000_000, transcendentals=0),
    )(*args)


def per_device(fake_tokens, real_tokens, proj_weight, score_vector):
    ylo, x, z, yhi, c = (lax.axis_index(a) for a in AXES)
    y = yhi * 2 + ylo
    gray_x, gray_y = ((v == 1) | (v == 2) for v in (x, y))
    core0 = c == 0
    tok = fake_tokens.shape[1]
    rows, hid = proj_weight.shape
    half = hid // 2
    d_in = rows * NZ * 4
    n = 2 * tok
    scale = math.sqrt(hid / (8 * 32 * tok))

    def slices_of(side):
        mine = lax.dynamic_slice_in_dim(proj_weight, side * half, half, 1)
        first = lax.dynamic_slice_in_dim(mine, x * 128, 128, 1)
        second = lax.dynamic_slice_in_dim(mine, 512 + ylo * 256 + gray_x * 128, 128, 1)
        return jnp.concatenate([first, second], 1)

    block = ordered(core0, slices_of(c), to_core(slices_of(1 - c)), 0)
    over_z = lax.all_to_all(jnp.broadcast_to(block[None], (NZ, *block.shape)), "z", 0, 0)
    piece_a, piece_b = over_z[:, :, :128], over_z[:, :, 128:].reshape(d_in // 2, 128)
    far_a, far_b = together(
        (piece_a.reshape(d_in // 2, 128), piece_b), (lambda x, y, c: (x, 3 - y, c), lambda x, y, c: (x ^ 1, y, c))
    )
    far_a = far_a.reshape(piece_a.shape)
    own_a = ordered(yhi == 0, piece_a[:, None], far_a[:, None], 1).reshape(d_in, 128)
    own_b = ordered(~gray_x, piece_b, far_b, 1)

    own_tokens = jnp.concatenate([fake_tokens[0], real_tokens[0]], 0)
    def join_tokens(other_tokens):
        return call(
            tokens_kernel, 2 * n * d_in * 128,
            [((2 * n, d_in), BF16), ((d_in, 2 * n), BF16, True), ((16, 128), F32)], [((d_in, 2 * n), BF16)],
            fake_tokens[0], real_tokens[0], other_tokens,
            flags=c[None].astype(jnp.int32), sems=[1],
        )

    left_a, right_a, left_b, right_b, tokens, tokens_t, peak = together(
        (own_a, own_a, own_b, own_b), RING, join_tokens, (to_core(own_tokens),)
    )
    across_a, across_b = together((left_a, left_b), (RING[0], RING[2]))

    def score_at(start, width):
        return lax.dynamic_slice_in_dim(score_vector, c * half + start, width, 0)

    score_1 = jnp.concatenate(
        [score_at((x + k) % 4 * 128, 128) for k in (0, 3, 1)] + [score_at(512 + (1 - ylo) * 256, 256)]
    )[None]
    score_2 = jnp.concatenate([score_at(512 + ylo * 256, 256), score_at((x + 2) % 4 * 128, 128)])[None]
    yhi_left, yhi_right = (y + 3) % 4 // 2, (y + 1) % 4 // 2

    def states(width):
        return [
            ((d_in, width), BF16),
            ((2 * n, width), F32),
            ((n, width), F32),
            ((n, width), BF16),
            ((2 * n, 128), F32),
            ((d_in, n), F32),
        ]

    wide, narrow = 640, 384
    w_1, slope_1, curve_1, lifted_1, logit_1, part_1 = call(
        first_kernel, 6 * n * d_in * wide,
        [*((*state, True) for state in states(wide)[:4]), *states(wide)[4:]], states(wide)[:4],
        tokens, own_a, left_a, right_a, left_b, right_b, score_1,
        flags=yhi_left[None].astype(jnp.int32), sems=[4],
    )
    w_2, slope_2, curve_2, lifted_2, logit, part = call(
        second_kernel, 6 * n * d_in * narrow,
        [*((*state, True) for state in states(narrow)[:4]), *states(narrow)[4:]], states(narrow)[:4],
        tokens, own_b, across_b, across_a, score_2, logit_1, part_1,
        flags=yhi[None].astype(jnp.int32), sems=[4],
    )
    part_in, logit_in = to_core(part), to_core(logit)

    def works(width):
        return [((n, width), BF16)] * 2

    strip, side = ((d_in, 128), F32), [((d_in // 2, 256), F32)] * 2
    results = [strip, *side, strip, strip, *side, strip]
    across_a, far_low, far_high, left_a, right_a, low_b, high_b, own_a, exponent = call(
        functools.partial(third_kernel, scale), 8 * n * d_in * half,
        [*((*shape, True) for shape in results), ((16, 128), F32)],
        [*results, ((d_in, n), BF16), ((n, d_in), BF16), *works(wide), *works(narrow), ((d_in, 2 * n), BF16),
         *states(wide)[:4], *states(narrow)[:4]],
        part, part_in, logit, logit_in, peak,
        there=(w_2, slope_2, curve_2, lifted_2, tokens_t, w_1, slope_1, curve_1, lifted_1), sems=[9, 32], vmem_mib=36,
    )
    exponent = exponent[:1]
    twice = lambda row: jnp.concatenate([row, row], 1)

    own_b = jnp.where(yhi == 0, far_low, far_high)
    across_b = jnp.where(yhi == 0, far_high, far_low)
    right_b = jnp.where(yhi_right == 0, low_b, high_b)
    left_b = jnp.where(yhi_left == 0, low_b, high_b)
    arrived = together(
        (
            packed(across_a, exponent),
            packed(across_b, twice(exponent)),
            packed(right_a, exponent),
            packed(left_a, exponent),
            packed(right_b, twice(exponent)),
            packed(left_b, twice(exponent)),
        ),
        (lambda x, y, c: (x + 2, y, c), lambda x, y, c: (x, y + 2, c), *RING),
    )

    def summed(own, exponent, *messages):
        for values, theirs in map(unpacked, messages):
            own, exponent = own + values, jnp.maximum(exponent, theirs)
        return own, exponent + 2.0

    sum_a, exp_a = summed(own_a, exponent, arrived[2], arrived[3], arrived[0])
    sum_b, exp_b = summed(own_b, twice(exponent), arrived[4], arrived[5], arrived[1])

    turns = sum_a.reshape(NZ, 2, 2 * rows, 128)
    keep_a = jnp.where(yhi == 0, turns[:, 0], turns[:, 1]).reshape(d_in // 2, 128)
    give_a = jnp.where(yhi == 0, turns[:, 1], turns[:, 0]).reshape(d_in // 2, 128)
    keep_b = jnp.where(gray_x, sum_b[:, 128:], sum_b[:, :128])
    give_b = jnp.where(gray_x, sum_b[:, :128], sum_b[:, 128:])
    got_a, got_b = together(
        (packed(give_a, exp_a), packed(give_b, exp_b[:, :128])),
        (lambda x, y, c: (x, 3 - y, c), lambda x, y, c: (x ^ 1, y, c)),
    )
    turns_a = (keep_a + unpacked(got_a)[0]).reshape(NZ, 2, rows, 128)
    turns_b = (keep_b + unpacked(got_b)[0]).reshape(NZ, 2, rows, 128)

    def split_rows(turns, second):
        return jnp.where(second, turns[:, 1], turns[:, 0]), jnp.where(second, turns[:, 0], turns[:, 1])

    keep_a, give_a = split_rows(turns_a, gray_y)
    keep_b, give_b = split_rows(turns_b, x >= 2)
    got_a, got_b = together(
        (give_a, give_b), (lambda x, y, c: (x, y ^ 1, c), lambda x, y, c: (3 - x, y, c))
    )
    both = jnp.concatenate([keep_a + got_a, keep_b + got_b], 2)
    both = jnp.sum(lax.all_to_all(both, "z", 0, 0), 0)

    spread = lax.all_to_all(jnp.broadcast_to(both[None], (8, *both.shape)), ("ylo", "x"), 0, 0)
    spread = spread.reshape(2, 4, rows, 256)

    def row_group(r):
        pick = jnp.where(yhi == r, spread[0, :, :, :128], spread[1, :, :, :128])
        order = (0, 1) if r == 0 else (3, 2)
        return jnp.concatenate(
            [pick[k] for k in range(4)] + [spread[v, k, :, 128:] for v in (0, 1) for k in order], 1
        )

    zero, one = row_group(0), row_group(1)
    theirs = to_core(jnp.where(core0, one, zero))
    return ordered(core0, jnp.where(core0, zero, one), theirs, 1)


def solution(mesh):
    split = Mesh(mesh.devices.reshape(2, NX, NZ, 2, 2), AXES)
    tokens = P(("ylo", "x"), ("z", "yhi", "c"), None)
    shard = P(("z", "yhi", "c"), None)
    return jax.shard_map(
        per_device, mesh=split, in_specs=(tokens, tokens, shard, P()), out_specs=shard, check_vma=False
    )
```

```python
import functools
import math

import jax
import jax.numpy as jnp
from jax import lax
from jax.experimental import pallas as pl
from jax.experimental.pallas import tpu as pltpu
from jax.sharding import Mesh
from jax.sharding import PartitionSpec as P

R1_WEIGHT = 40.0
NX, NY, NZ = 4, 4, 8
AXES = ("ylo", "x", "z", "yhi", "c")
BF16, F16, F32 = jnp.bfloat16, jnp.float16, jnp.float32


def flat_index(x, y, z, c):
    return ((y % 2) * NX + x) * (NZ * 4) + z * 4 + (y // 2) * 2 + c


def send(array, to):
    pairs = []
    for x in range(NX):
        for y in range(NY):
            for z in range(NZ):
                for c in range(2):
                    tx, ty, tc = to(x, y, c)
                    pairs.append((flat_index(x, y, z, c), flat_index(tx % NX, ty % NY, z, tc)))
    return lax.ppermute(array, AXES, pairs)


def to_core(array):
    return send(array, lambda x, y, c: (x, y, 1 - c))


def together(arrays, routes, beside=None, extra=()):
    arrays = lax.optimization_barrier((*arrays, *extra))
    sent = tuple(send(a, to) for a, to in zip(arrays, routes))
    return lax.optimization_barrier((*sent, *(beside(*arrays[len(sent) :]) if beside else ())))


RING = (
    lambda x, y, c: (x + 1, y, c),
    lambda x, y, c: (x - 1, y, c),
    lambda x, y, c: (x, y + 1, c),
    lambda x, y, c: (x, y - 1, c),
)


def ordered(first_is_mine, mine, theirs, axis):
    return jnp.concatenate(
        [jnp.where(first_is_mine, mine, theirs), jnp.where(first_is_mine, theirs, mine)], axis
    )


def packed(piece, exponent):
    scaled = (piece * jnp.exp2(-exponent)).astype(F16)
    return jnp.concatenate([scaled, jnp.broadcast_to(exponent.astype(F16), (16, piece.shape[1]))], 0)


def unpacked(message):
    exponent = message[-16:-15].astype(F32)
    return message[:-16].astype(F32) * jnp.exp2(exponent), exponent


def column_tiles(width):
    return [(start, min(256, width - start)) for start in range(0, width, 256)]


def nt(a, b):
    return lax.dot_general(a, b, (((1,), (1,)), ((), ())), preferred_element_type=F32)


def forward_tiles(tokens_ref, w_ref, score_ref, slope_ref, curve_ref, lifted_ref, logit_ref, first):
    n = tokens_ref.shape[0] // 2
    for kind in (0, 1):
        rows = slice(kind * n, kind * n + n)
        total = jnp.zeros((n, 128), F32) if first is None else first[rows, :]
        for start, width in column_tiles(w_ref.shape[1]):
            cols = slice(start, start + width)
            preact = jnp.dot(tokens_ref[rows, :], w_ref[:, cols], preferred_element_type=F32)
            score = score_ref[:, cols]
            squash = jax.nn.sigmoid(preact)
            rest = 1.0 - squash
            act = preact * squash * score
            for lane in range(0, width, 128):
                total = total + act[:, lane : lane + 128]
            slope = squash * (1.0 + preact * rest) * score
            slope_ref[rows, cols] = slope
            if kind == 1:
                lifted_ref[:, cols] = slope.astype(BF16)
                curve_ref[:, cols] = squash * rest * (2.0 + preact * (1.0 - 2.0 * squash)) * score
        logit_ref[rows, :] = total


def pull_back(w_ref, lifted_ref, part_ref, so_far):
    for start in range(0, w_ref.shape[0], 512):
        rows = slice(start, start + 512)
        value = nt(w_ref[rows, :], lifted_ref[...])
        part_ref[rows, :] = value if so_far is None else so_far[rows, :] + value


def place_pair(w_ref, column, low_ref, high_ref, swap):
    width = low_ref.shape[1]
    turn = w_ref.shape[0] // (2 * NZ)
    for z in range(NZ):
        rows = slice(z * turn, z * turn + turn)
        low, high = low_ref[rows, :], high_ref[rows, :]
        w_ref[2 * z * turn : 2 * z * turn + turn, column : column + width] = jnp.where(swap, high, low)
        w_ref[2 * z * turn + turn : 2 * z * turn + 2 * turn, column : column + width] = jnp.where(swap, low, high)


def fetched(sems, *pairs):
    copies = [pltpu.make_async_copy(source, target, sems.at[k]) for k, (source, target) in enumerate(pairs)]
    for copy in copies:
        copy.start()
    return copies


def done(copies):
    for copy in copies:
        copy.wait()


def first_kernel(flag_ref, tokens_ref, own_ref, left_ref, right_ref, low_ref, high_ref, score_ref,
                 w_hbm, slope_hbm, curve_hbm, lifted_hbm, logit_ref, part_ref,
                 w_ref, slope_ref, curve_ref, lifted_ref, sems):
    w_ref[:, 0:128] = own_ref[...]
    w_ref[:, 128:256] = left_ref[...]
    w_ref[:, 256:384] = right_ref[...]
    place_pair(w_ref, 384, low_ref, high_ref, flag_ref[0] == 1)
    forward_tiles(tokens_ref, w_ref, score_ref, slope_ref, curve_ref, lifted_ref, logit_ref, None)
    copies = fetched(
        sems, (w_ref, w_hbm), (slope_ref, slope_hbm), (curve_ref, curve_hbm), (lifted_ref, lifted_hbm)
    )
    pull_back(w_ref, lifted_ref, part_ref, None)
    done(copies)


def tokens_kernel(flag_ref, fake_hbm, real_hbm, other_hbm, tokens_ref, tokens_t_hbm, peak_ref,
                  own_ref, other_ref, tokens_t_ref, sems):
    tok = fake_hbm.shape[0]
    done(
        fetched(
            sems, (fake_hbm, own_ref.at[0:tok, :]), (real_hbm, own_ref.at[tok : 2 * tok, :]), (other_hbm, other_ref)
        )
    )
    first = flag_ref[0] == 0
    for kind in (0, 1):
        mine, theirs = (ref[kind * tok : kind * tok + tok, :] for ref in (own_ref, other_ref))
        start = 2 * kind * tok
        tokens_ref[start : start + tok, :] = jnp.where(first, mine, theirs)
        tokens_ref[start + tok : start + 2 * tok, :] = jnp.where(first, theirs, mine)
        peak = peak_of(tokens_ref[start : start + 2 * tok, :])
        peak_ref[8 * kind : 8 * kind + 8, :] = jnp.broadcast_to(peak, (8, 128))
    tokens_t_ref[...] = tokens_ref[...].T
    done(fetched(sems, (tokens_t_ref, tokens_t_hbm)))


def second_kernel(flag_ref, tokens_ref, low_ref, high_ref, across_ref, score_ref, logit_in_ref, part_in_ref,
                  w_hbm, slope_hbm, curve_hbm, lifted_hbm, logit_ref, part_ref,
                  w_ref, slope_ref, curve_ref, lifted_ref, sems):
    place_pair(w_ref, 0, low_ref, high_ref, flag_ref[0] == 1)
    w_ref[:, 256:384] = across_ref[...]
    forward_tiles(tokens_ref, w_ref, score_ref, slope_ref, curve_ref, lifted_ref, logit_ref, logit_in_ref)
    copies = fetched(
        sems, (w_ref, w_hbm), (slope_ref, slope_hbm), (curve_ref, curve_hbm), (lifted_ref, lifted_hbm)
    )
    pull_back(w_ref, lifted_ref, part_ref, part_in_ref)
    done(copies)


def peak_of(array):
    flat = jnp.max(jnp.abs(array).astype(F32), axis=0, keepdims=True)
    return jnp.max(flat, axis=1, keepdims=True)


def cotangents(scale, logits, r1_ref, w_ref, slope_ref, curve_ref, fake_ref, real_ref):
    n = r1_ref.shape[0]
    fake_ref[...] = (scale * jax.nn.sigmoid(logits[:n]) * slope_ref[0:n, :]).astype(BF16)
    real_gain = -scale * jax.nn.sigmoid(-logits[n:])
    for start, width in column_tiles(w_ref.shape[1]):
        cols = slice(start, start + width)
        back = jnp.dot(r1_ref[...], w_ref[:, cols], preferred_element_type=F32)
        real_ref[:, cols] = (real_gain * slope_ref[n : 2 * n, cols] + back * curve_ref[:, cols]).astype(BF16)


def term_tiles(outs, tokens_t_ref, r1_t_ref, sems):
    d_in, n = r1_t_ref.shape
    turn = d_in // (2 * NZ)
    height = 4 * turn
    leaving = []
    for (fake_ref, real_ref, lifted_ref), start, width, parts in outs:
        cols = slice(start, start + width)
        for row in range(0, d_in, height):
            rows = slice(row, row + height)
            value = (
                jnp.dot(tokens_t_ref[rows, 0:n], fake_ref[:, cols], preferred_element_type=F32)
                + jnp.dot(tokens_t_ref[rows, n : 2 * n], real_ref[:, cols], preferred_element_type=F32)
                + jnp.dot(r1_t_ref[rows, :], lifted_ref[:, cols], preferred_element_type=F32)
            )
            for column, turns, out, out_hbm in parts:
                piece = value[:, column : column + out.shape[1]]
                if turns is None:
                    there = rows
                    out[rows, :] = piece
                else:
                    there = slice(row // 2, row // 2 + 2 * turn)
                    for k in range(2):
                        at = row // 2 + k * turn
                        out[at : at + turn, :] = piece[(2 * k + turns) * turn : (2 * k + turns + 1) * turn, :]
                leaving.append(
                    pltpu.make_async_copy(out.at[there, :], out_hbm.at[there, :], sems.at[len(leaving)])
                )
                leaving[-1].start()
    done(leaving)


def third_kernel(scale, part_ref, part_in_ref, logit_ref, logit_in_ref, peak_ref,
                 w_2_hbm, slope_2_hbm, curve_2_hbm, w_1_hbm, slope_1_hbm, curve_1_hbm, lifted_1_hbm, lifted_2_hbm,
                 tokens_t_hbm,
                 across_hbm, low_hbm, high_hbm, r1_t_hbm, fake_1_hbm, real_1_hbm, exp_ref,
                 across_ref, low_ref, high_ref, r1_t_ref, fake_1_ref, real_1_ref, r1_ref, fake_2_ref, real_2_ref,
                 w_2_ref, slope_2_ref, curve_2_ref, w_1_ref, slope_1_ref, curve_1_ref, lifted_1_ref, lifted_2_ref,
                 tokens_t_ref, sems, r1_sems, out_sems):
    copies = fetched(
        sems,
        (w_2_hbm, w_2_ref), (slope_2_hbm, slope_2_ref), (curve_2_hbm, curve_2_ref),
        (w_1_hbm, w_1_ref), (slope_1_hbm, slope_1_ref), (curve_1_hbm, curve_1_ref),
        (lifted_1_hbm, lifted_1_ref), (lifted_2_hbm, lifted_2_ref), (tokens_t_hbm, tokens_t_ref),
    )
    r1_t_ref[...] = (scale * R1_WEIGHT * (part_ref[...] + part_in_ref[...])).astype(BF16)
    r1_ref[...] = r1_t_ref[...].T
    logits = jnp.sum(logit_ref[...] + logit_in_ref[...], axis=1, keepdims=True)
    done(copies[:3])
    cotangents(scale, logits, r1_ref, w_2_ref, slope_2_ref, curve_2_ref, fake_2_ref, real_2_ref)
    done(copies[3:6])
    cotangents(scale, logits, r1_ref, w_1_ref, slope_1_ref, curve_1_ref, fake_1_ref, real_1_ref)
    passed = fetched(r1_sems, (r1_t_ref, r1_t_hbm), (fake_1_ref, fake_1_hbm), (real_1_ref, real_1_hbm))
    done(copies[6:])
    first, second = (fake_1_ref, real_1_ref, lifted_1_ref), (fake_2_ref, real_2_ref, lifted_2_ref)
    peaks = [jnp.maximum(peak_of(one[...]), peak_of(two[...])) for one, two in zip(first, second)]
    n = r1_ref.shape[0]
    bound = n * (
        peak_ref[0:1, 0:1] * peaks[0] + peak_ref[8:9, 0:1] * peaks[1] + peak_of(r1_t_ref[...]) * peaks[2]
    )
    bound = jnp.broadcast_to(bound, (16, 128))
    exp_ref[...] = jnp.ceil(jnp.log(jnp.maximum(bound, 1e-30)) * (1.0 / math.log(2.0)) + 0.01) - 15.0
    outs = [
        (second, 256, 128, [(0, None, across_ref, across_hbm)]),
        (second, 0, 256, [(0, 0, low_ref, low_hbm), (0, 1, high_ref, high_hbm)]),
    ]
    term_tiles(outs, tokens_t_ref, r1_t_ref, out_sems)
    done(passed)


def fourth_kernel(r1_t_hbm, fake_hbm, real_hbm, lifted_hbm, tokens_t_hbm,
                  left_hbm, right_hbm, low_hbm, high_hbm, own_hbm,
                  left_ref, right_ref, low_ref, high_ref, own_ref,
                  r1_t_ref, fake_ref, real_ref, lifted_ref, tokens_t_ref, sems, out_sems):
    done(
        fetched(
            sems,
            (r1_t_hbm, r1_t_ref), (fake_hbm, fake_ref), (real_hbm, real_ref), (lifted_hbm, lifted_ref),
            (tokens_t_hbm, tokens_t_ref),
        )
    )
    first = fake_ref, real_ref, lifted_ref
    outs = [
        (first, 128, 256, [(0, None, left_ref, left_hbm), (128, None, right_ref, right_hbm)]),
        (first, 384, 256, [(0, 0, low_ref, low_hbm), (0, 1, high_ref, high_hbm)]),
        (first, 0, 128, [(0, None, own_ref, own_hbm)]),
    ]
    term_tiles(outs, tokens_t_ref, r1_t_ref, out_sems)


def call(kernel, flops, outs, scratch, *args, flags=None, there=(), sems=(), vmem_mib=20):
    vmem = pl.BlockSpec(memory_space=pltpu.VMEM)
    specs = [vmem] * len(args) + [pl.BlockSpec(memory_space=pltpu.HBM)] * len(there)
    args = (*args, *(pltpu.with_memory_space_constraint(a, pltpu.HBM) for a in there))
    if flags is not None:
        args, specs = (flags, *args), [pl.BlockSpec(memory_space=pltpu.SMEM), *specs]
    return pl.pallas_call(
        kernel,
        out_shape=[(pltpu.HBM if len(out) == 3 else pltpu.VMEM)(*out[:2]) for out in outs],
        in_specs=specs,
        out_specs=[pl.BlockSpec(memory_space=pltpu.HBM) if len(out) == 3 else vmem for out in outs],
        scratch_shapes=[pltpu.VMEM(shape, dtype) for shape, dtype in scratch]
        + [pltpu.SemaphoreType.DMA((k,)) for k in sems],
        compiler_params=pltpu.CompilerParams(vmem_limit_bytes=vmem_mib * 1024 * 1024),
        cost_estimate=pl.CostEstimate(flops=flops, bytes_accessed=8_000_000, transcendentals=0),
    )(*args)


def per_device(fake_tokens, real_tokens, proj_weight, score_vector):
    ylo, x, z, yhi, c = (lax.axis_index(a) for a in AXES)
    y = yhi * 2 + ylo
    gray_x, gray_y = ((v == 1) | (v == 2) for v in (x, y))
    core0 = c == 0
    tok = fake_tokens.shape[1]
    rows, hid = proj_weight.shape
    half = hid // 2
    d_in = rows * NZ * 4
    n = 2 * tok
    scale = math.sqrt(hid / (8 * 32 * tok))

    def slices_of(side):
        mine = lax.dynamic_slice_in_dim(proj_weight, side * half, half, 1)
        first = lax.dynamic_slice_in_dim(mine, x * 128, 128, 1)
        second = lax.dynamic_slice_in_dim(mine, 512 + ylo * 256 + gray_x * 128, 128, 1)
        return jnp.concatenate([first, second], 1)

    block = ordered(core0, slices_of(c), to_core(slices_of(1 - c)), 0)
    over_z = lax.all_to_all(jnp.broadcast_to(block[None], (NZ, *block.shape)), "z", 0, 0)
    piece_a, piece_b = over_z[:, :, :128], over_z[:, :, 128:].reshape(d_in // 2, 128)
    far_a, far_b = together(
        (piece_a.reshape(d_in // 2, 128), piece_b), (lambda x, y, c: (x, 3 - y, c), lambda x, y, c: (x ^ 1, y, c))
    )
    far_a = far_a.reshape(piece_a.shape)
    own_a = ordered(yhi == 0, piece_a[:, None], far_a[:, None], 1).reshape(d_in, 128)
    own_b = ordered(~gray_x, piece_b, far_b, 1)

    own_tokens = jnp.concatenate([fake_tokens[0], real_tokens[0]], 0)
    def join_tokens(other_tokens):
        return call(
            tokens_kernel, 2 * n * d_in * 128,
            [((2 * n, d_in), BF16), ((d_in, 2 * n), BF16, True), ((16, 128), F32)],
            [((n, d_in), BF16), ((n, d_in), BF16), ((d_in, 2 * n), BF16)],
            flags=c[None].astype(jnp.int32), there=(fake_tokens[0], real_tokens[0], other_tokens), sems=[3],
        )

    left_a, right_a, left_b, right_b, tokens, tokens_t, peak = together(
        (own_a, own_a, own_b, own_b), RING, join_tokens, (to_core(own_tokens),)
    )
    across_a, across_b = together((left_a, left_b), (RING[0], RING[2]))

    def score_at(start, width):
        return lax.dynamic_slice_in_dim(score_vector, c * half + start, width, 0)

    score_1 = jnp.concatenate(
        [score_at((x + k) % 4 * 128, 128) for k in (0, 3, 1)] + [score_at(512 + (1 - ylo) * 256, 256)]
    )[None]
    score_2 = jnp.concatenate([score_at(512 + ylo * 256, 256), score_at((x + 2) % 4 * 128, 128)])[None]
    yhi_left, yhi_right = (y + 3) % 4 // 2, (y + 1) % 4 // 2

    def states(width):
        return [
            ((d_in, width), BF16),
            ((2 * n, width), F32),
            ((n, width), F32),
            ((n, width), BF16),
            ((2 * n, 128), F32),
            ((d_in, n), F32),
        ]

    wide, narrow = 640, 384
    w_1, slope_1, curve_1, lifted_1, logit_1, part_1 = call(
        first_kernel, 6 * n * d_in * wide,
        [*((*state, True) for state in states(wide)[:4]), *states(wide)[4:]], states(wide)[:4],
        tokens, own_a, left_a, right_a, left_b, right_b, score_1,
        flags=yhi_left[None].astype(jnp.int32), sems=[4],
    )
    w_2, slope_2, curve_2, lifted_2, logit, part = call(
        second_kernel, 6 * n * d_in * narrow,
        [*((*state, True) for state in states(narrow)[:4]), *states(narrow)[4:]], states(narrow)[:4],
        tokens, own_b, across_b, across_a, score_2, logit_1, part_1,
        flags=yhi[None].astype(jnp.int32), sems=[4],
    )
    part_in, logit_in = to_core(part), to_core(logit)

    def works(width):
        return [((n, width), BF16)] * 2

    marked = lambda shapes: [(*shape, True) for shape in shapes]
    strip, side = ((d_in, 128), F32), [((d_in // 2, 256), F32)] * 2
    tall, r1_shape = ((d_in, 2 * n), BF16), ((d_in, n), BF16)
    results = [strip, *side, r1_shape, *works(wide)]
    across_a, far_low, far_high, r1_t, fake_1, real_1, exponent = call(
        functools.partial(third_kernel, scale), 6 * n * d_in * half,
        [*marked(results), ((16, 128), F32)],
        [*results, ((n, d_in), BF16), *works(narrow), *states(narrow)[:3], *states(wide)[:4], states(narrow)[3], tall],
        part, part_in, logit, logit_in, peak,
        there=(w_2, slope_2, curve_2, w_1, slope_1, curve_1, lifted_1, lifted_2, tokens_t),
        sems=[9, 3, 12], vmem_mib=36,
    )
    exponent = exponent[:1]
    twice = lambda row: jnp.concatenate([row, row], 1)

    own_b = jnp.where(yhi == 0, far_low, far_high)
    across_b = jnp.where(yhi == 0, far_high, far_low)

    def rest_of_term(r1_t):
        shapes = [strip, strip, *side, strip]
        left_a, right_a, low_b, high_b, own_a = call(
            fourth_kernel, 6 * n * d_in * wide, marked(shapes), [*shapes, r1_shape, *works(wide), states(wide)[3], tall],
            there=(r1_t, fake_1, real_1, lifted_1, tokens_t), sems=[5, 20], vmem_mib=28,
        )
        right_b = jnp.where(yhi_right == 0, low_b, high_b)
        left_b = jnp.where(yhi_left == 0, low_b, high_b)
        return (
            packed(right_a, exponent),
            packed(left_a, exponent),
            packed(right_b, twice(exponent)),
            packed(left_b, twice(exponent)),
            own_a,
        )

    across_a, across_b, *beside, own_a = together(
        (packed(across_a, exponent), packed(across_b, twice(exponent))),
        (lambda x, y, c: (x + 2, y, c), lambda x, y, c: (x, y + 2, c)),
        rest_of_term,
        (r1_t,),
    )
    arrived = (across_a, across_b, *together(beside, RING))

    def summed(own, exponent, *messages):
        for values, theirs in map(unpacked, messages):
            own, exponent = own + values, jnp.maximum(exponent, theirs)
        return own, exponent + 2.0

    sum_a, exp_a = summed(own_a, exponent, arrived[2], arrived[3], arrived[0])
    sum_b, exp_b = summed(own_b, twice(exponent), arrived[4], arrived[5], arrived[1])

    quarters_a = sum_a.reshape(NZ, 4, rows, 128)
    turns_b = sum_b.reshape(NZ, 2, rows, 256)
    quarters_b = jnp.stack(
        [turns_b[:, 0, :, :128], turns_b[:, 0, :, 128:], turns_b[:, 1, :, 128:], turns_b[:, 1, :, :128]], 1
    )
    gray_order = (0, 1, 3, 2)
    quarters_a = jnp.stack([quarters_a[:, k] for k in gray_order], 1)

    def quarter(array, k):
        return lax.dynamic_index_in_dim(array, k % 4, 1, keepdims=False).reshape(NZ * rows, 128)

    away = (1, 3, 2)
    got = together(
        [packed(quarter(quarters_a, y + k), exp_a) for k in away]
        + [packed(quarter(quarters_b, x + k), exp_b[:, :128]) for k in away],
        [RING[2], RING[3], lambda x, y, c: (x, y + 2, c), RING[0], RING[1], lambda x, y, c: (x + 2, y, c)],
    )
    sum_a, _ = summed(quarter(quarters_a, y), exp_a, *got[:3])
    sum_b, _ = summed(quarter(quarters_b, x), exp_b[:, :128], *got[3:])
    both = jnp.concatenate([sum_a, sum_b], 1).reshape(NZ, rows, 256)
    both = jnp.sum(lax.all_to_all(both, "z", 0, 0), 0)

    spread = lax.all_to_all(jnp.broadcast_to(both[None], (8, *both.shape)), ("ylo", "x"), 0, 0)
    spread = spread.reshape(2, 4, rows, 256)

    def row_group(r):
        pick = jnp.where(yhi == r, spread[0, :, :, :128], spread[1, :, :, :128])
        order = (0, 1) if r == 0 else (3, 2)
        return jnp.concatenate(
            [pick[k] for k in range(4)] + [spread[v, k, :, 128:] for v in (0, 1) for k in order], 1
        )

    zero, one = row_group(0), row_group(1)
    theirs = to_core(jnp.where(core0, one, zero))
    return ordered(core0, jnp.where(core0, zero, one), theirs, 1)


def solution(mesh):
    split = Mesh(mesh.devices.reshape(2, NX, NZ, 2, 2), AXES)
    tokens = P(("ylo", "x"), ("z", "yhi", "c"), None)
    shard = P(("z", "yhi", "c"), None)
    return jax.shard_map(
        per_device, mesh=split, in_specs=(tokens, tokens, shard, P()), out_specs=shard, check_vma=False
    )
```

```python
import functools
import math

import jax
import jax.numpy as jnp
from jax import lax
from jax.experimental import pallas as pl
from jax.experimental.pallas import tpu as pltpu
from jax.sharding import Mesh
from jax.sharding import PartitionSpec as P

R1_WEIGHT = 40.0
NX, NY, NZ = 4, 4, 8
AXES = ("ylo", "x", "z", "yhi", "c")
BF16, F16, F32 = jnp.bfloat16, jnp.float16, jnp.float32


def flat_index(x, y, z, c):
    return ((y % 2) * NX + x) * (NZ * 4) + z * 4 + (y // 2) * 2 + c


def send(array, to):
    pairs = []
    for x in range(NX):
        for y in range(NY):
            for z in range(NZ):
                for c in range(2):
                    tx, ty, tc = to(x, y, c)
                    pairs.append((flat_index(x, y, z, c), flat_index(tx % NX, ty % NY, z, tc)))
    return lax.ppermute(array, AXES, pairs)


def to_core(array):
    return send(array, lambda x, y, c: (x, y, 1 - c))


def together(arrays, routes, beside=None, extra=()):
    arrays = lax.optimization_barrier((*arrays, *extra))
    sent = tuple(send(a, to) for a, to in zip(arrays, routes))
    return lax.optimization_barrier((*sent, *(beside(*arrays[len(sent) :]) if beside else ())))


def ring(step):
    return lambda x, y, c: (x + step, y, c) if c == 0 else (x, y + step, c)


def other_ring(step):
    return lambda x, y, c: (x, y + step, c) if c == 0 else (x + step, y, c)


def pair(x, y, c):
    return (x, 3 - y, c) if c == 0 else (x ^ 1, y, c)


def ordered(first_is_mine, mine, theirs, axis):
    return jnp.concatenate(
        [jnp.where(first_is_mine, mine, theirs), jnp.where(first_is_mine, theirs, mine)], axis
    )


def packed(piece, exponent):
    scaled = (piece * jnp.exp2(-exponent)).astype(F16)
    return jnp.concatenate([scaled, jnp.broadcast_to(exponent.astype(F16), (16, piece.shape[1]))], 0)


def unpacked(message):
    exponent = message[-16:-15].astype(F32)
    return message[:-16].astype(F32) * jnp.exp2(exponent), exponent


def column_tiles(width):
    return [(start, min(256, width - start)) for start in range(0, width, 256)]


def nt(a, b):
    return lax.dot_general(a, b, (((1,), (1,)), ((), ())), preferred_element_type=F32)


def flat(block):
    return block.reshape(block.shape[0] * block.shape[1], block.shape[2])


def forward_tiles(tokens_ref, w_ref, score_ref, slope_ref, curve_ref, lifted_ref, logit_ref, first, arriving):
    n = tokens_ref.shape[0] // 2
    for kind in (0, 1):
        arriving[kind].wait()
        rows = slice(kind * n, kind * n + n)
        total = jnp.zeros((n, 128), F32) if first is None else first[rows, :]
        for start, width in column_tiles(w_ref.shape[2]):
            cols = slice(start, start + width)
            preact = jnp.dot(tokens_ref[rows, :], flat(w_ref[:, :, cols]), preferred_element_type=F32)
            score = score_ref[:, cols]
            squash = jax.nn.sigmoid(preact)
            rest = 1.0 - squash
            act = preact * squash * score
            for lane in range(0, width, 128):
                total = total + act[:, lane : lane + 128]
            slope = squash * (1.0 + preact * rest) * score
            slope_ref[rows, cols] = slope
            if kind == 1:
                lifted_ref[:, cols] = slope.astype(BF16)
                curve_ref[:, cols] = squash * rest * (2.0 + preact * (1.0 - 2.0 * squash)) * score
        logit_ref[rows, :] = total


def pull_back(w_ref, lifted_ref, part_ref, so_far):
    height = 2 * w_ref.shape[1]
    for k in range(w_ref.shape[0] // 2):
        rows = slice(k * height, k * height + height)
        value = nt(flat(w_ref[2 * k : 2 * k + 2]), lifted_ref[...])
        part_ref[rows, :] = value if so_far is None else so_far[rows, :] + value


def place_of(flag_ref, piece, sub):
    return jnp.where(flag_ref[0] == 0, sub, flag_ref[1] ^ piece), jnp.where(flag_ref[0] == 0, piece, sub)


def laid(flag_ref, one_hbm, two_hbm, w_ref):
    height = one_hbm.shape[2]
    pairs = []
    for piece, ref in enumerate((one_hbm, two_hbm)):
        for sub in (0, 1):
            half, block = place_of(flag_ref, piece, sub)
            rows = pl.ds(pl.multiple_of(half * height, 16), height)
            pairs.append((ref.at[sub], w_ref.at[:, rows, pl.ds(pl.multiple_of(block * 256, 128), 256)]))
    return pairs


def fetched(sems, *pairs):
    copies = [pltpu.make_async_copy(source, target, sems.at[k]) for k, (source, target) in enumerate(pairs)]
    for copy in copies:
        copy.start()
    return copies


def done(copies):
    for copy in copies:
        copy.wait()


def forward_kernel(flag_ref, score_ref, *refs, so_far):
    earlier, refs = (refs[:2], refs[2:]) if so_far else ((None, None), refs)
    (tokens_hbm, one_hbm, two_hbm, w_hbm, slope_hbm, curve_hbm, lifted_hbm, logit_ref, part_ref,
     tokens_ref, w_ref, slope_ref, curve_ref, lifted_ref, sems, out_sems) = refs
    n = lifted_ref.shape[0]
    copies = fetched(
        sems,
        *laid(flag_ref, one_hbm, two_hbm, w_ref),
        *((tokens_hbm.at[k * n : k * n + n, :], tokens_ref.at[k * n : k * n + n, :]) for k in (0, 1)),
    )
    done(copies[:4])
    forward_tiles(tokens_ref, w_ref, score_ref, slope_ref, curve_ref, lifted_ref, logit_ref, earlier[0], copies[4:])
    copies = fetched(
        out_sems, (w_ref, w_hbm), (slope_ref, slope_hbm), (curve_ref, curve_hbm), (lifted_ref, lifted_hbm)
    )
    pull_back(w_ref, lifted_ref, part_ref, earlier[1])
    done(copies)


def tokens_kernel(flag_ref, fake_hbm, real_hbm, other_hbm, tokens_ref, tokens_t_hbm, peak_ref,
                  own_ref, other_ref, tokens_t_ref, sems):
    tok = fake_hbm.shape[0]
    done(
        fetched(
            sems, (fake_hbm, own_ref.at[0:tok, :]), (real_hbm, own_ref.at[tok : 2 * tok, :]), (other_hbm, other_ref)
        )
    )
    first = flag_ref[0] == 0
    for kind in (0, 1):
        mine, theirs = (ref[kind * tok : kind * tok + tok, :] for ref in (own_ref, other_ref))
        start = 2 * kind * tok
        tokens_ref[start : start + tok, :] = jnp.where(first, mine, theirs)
        tokens_ref[start + tok : start + 2 * tok, :] = jnp.where(first, theirs, mine)
        peak = peak_of(tokens_ref[start : start + 2 * tok, :])
        peak_ref[8 * kind : 8 * kind + 8, :] = jnp.broadcast_to(peak, (8, 128))
    tokens_t_ref[...] = tokens_ref[...].T
    done(fetched(sems, (tokens_t_ref, tokens_t_hbm)))


def peak_of(array):
    flat = jnp.max(jnp.abs(array).astype(F32), axis=0, keepdims=True)
    return jnp.max(flat, axis=1, keepdims=True)


def cotangents(scale, logits, r1_ref, w_ref, slope_ref, curve_ref, fake_ref, real_ref):
    n = r1_ref.shape[0]
    fake_ref[...] = (scale * jax.nn.sigmoid(logits[:n]) * slope_ref[0:n, :]).astype(BF16)
    real_gain = -scale * jax.nn.sigmoid(-logits[n:])
    for start, width in column_tiles(w_ref.shape[2]):
        cols = slice(start, start + width)
        back = jnp.dot(r1_ref[...], flat(w_ref[:, :, cols]), preferred_element_type=F32)
        real_ref[:, cols] = (real_gain * slope_ref[n : 2 * n, cols] + back * curve_ref[:, cols]).astype(BF16)


def term_tiles(flag_ref, cotangent_refs, tokens_t_ref, r1_t_ref, term_ref, term_hbm, sems):
    fake_ref, real_ref, lifted_ref = cotangent_refs
    d_in, n = r1_t_ref.shape
    turn = d_in // (2 * NZ)
    leaving = []
    for block in (0, 1):
        cols = slice(256 * block, 256 * block + 256)
        for row in range(0, d_in, 4 * turn):
            rows = slice(row, row + 4 * turn)
            value = (
                jnp.dot(tokens_t_ref[rows, 0:n], fake_ref[:, cols], preferred_element_type=F32)
                + jnp.dot(tokens_t_ref[rows, n : 2 * n], real_ref[:, cols], preferred_element_type=F32)
                + jnp.dot(r1_t_ref[rows, :], lifted_ref[:, cols], preferred_element_type=F32)
            )
            there = slice(row // 2, row // 2 + 2 * turn)
            for half in (0, 1):
                for k in range(2):
                    at = row // 2 + k * turn
                    term_ref[half, block, at : at + turn, :] = value[(2 * k + half) * turn : (2 * k + half + 1) * turn, :]
                piece = jnp.where(flag_ref[0] == 0, block, flag_ref[1] ^ half)
                sub = jnp.where(flag_ref[0] == 0, half, block)
                leaving.append(
                    pltpu.make_async_copy(
                        term_ref.at[half, block, there, :], term_hbm.at[piece, sub, there, :], sems.at[len(leaving)]
                    )
                )
                leaving[-1].start()
    done(leaving)


def third_kernel(scale, flag_ref, part_ref, part_in_ref, logit_ref, logit_in_ref, peak_ref,
                 w_2_hbm, slope_2_hbm, curve_2_hbm, w_1_hbm, slope_1_hbm, curve_1_hbm, lifted_1_hbm, lifted_2_hbm,
                 tokens_t_hbm,
                 term_hbm, r1_t_hbm, fake_1_hbm, real_1_hbm, exp_ref,
                 term_ref, r1_t_ref, fake_1_ref, real_1_ref, r1_ref, fake_2_ref, real_2_ref,
                 w_2_ref, slope_2_ref, curve_2_ref, w_1_ref, slope_1_ref, curve_1_ref, lifted_1_ref, lifted_2_ref,
                 tokens_t_ref, sems, r1_sems, out_sems):
    copies = fetched(
        sems,
        (w_2_hbm, w_2_ref), (slope_2_hbm, slope_2_ref), (curve_2_hbm, curve_2_ref),
        (w_1_hbm, w_1_ref), (slope_1_hbm, slope_1_ref), (curve_1_hbm, curve_1_ref),
        (lifted_1_hbm, lifted_1_ref), (lifted_2_hbm, lifted_2_ref), (tokens_t_hbm, tokens_t_ref),
    )
    r1_t_ref[...] = (scale * R1_WEIGHT * (part_ref[...] + part_in_ref[...])).astype(BF16)
    r1_ref[...] = r1_t_ref[...].T
    logits = jnp.sum(logit_ref[...] + logit_in_ref[...], axis=1, keepdims=True)
    done(copies[:3])
    cotangents(scale, logits, r1_ref, w_2_ref, slope_2_ref, curve_2_ref, fake_2_ref, real_2_ref)
    done(copies[3:6])
    cotangents(scale, logits, r1_ref, w_1_ref, slope_1_ref, curve_1_ref, fake_1_ref, real_1_ref)
    passed = fetched(r1_sems, (r1_t_ref, r1_t_hbm), (fake_1_ref, fake_1_hbm), (real_1_ref, real_1_hbm))
    done(copies[6:])
    first, second = (fake_1_ref, real_1_ref, lifted_1_ref), (fake_2_ref, real_2_ref, lifted_2_ref)
    peaks = [jnp.maximum(peak_of(one[...]), peak_of(two[...])) for one, two in zip(first, second)]
    n = r1_ref.shape[0]
    bound = n * (
        peak_ref[0:1, 0:1] * peaks[0] + peak_ref[8:9, 0:1] * peaks[1] + peak_of(r1_t_ref[...]) * peaks[2]
    )
    bound = jnp.broadcast_to(bound, (16, 128))
    exp_ref[...] = jnp.ceil(jnp.log(jnp.maximum(bound, 1e-30)) * (1.0 / math.log(2.0)) + 0.01) - 15.0
    term_tiles(flag_ref, second, tokens_t_ref, r1_t_ref, term_ref, term_hbm, out_sems)
    done(passed)


def fourth_kernel(flag_ref, r1_t_hbm, fake_hbm, real_hbm, lifted_hbm, tokens_t_hbm, term_hbm,
                  term_ref, r1_t_ref, fake_ref, real_ref, lifted_ref, tokens_t_ref, sems, out_sems):
    done(
        fetched(
            sems,
            (r1_t_hbm, r1_t_ref), (fake_hbm, fake_ref), (real_hbm, real_ref), (lifted_hbm, lifted_ref),
            (tokens_t_hbm, tokens_t_ref),
        )
    )
    term_tiles(flag_ref, (fake_ref, real_ref, lifted_ref), tokens_t_ref, r1_t_ref, term_ref, term_hbm, out_sems)


def call(kernel, flops, outs, scratch, *args, flags=None, there=(), sems=(), vmem_mib=20):
    vmem = pl.BlockSpec(memory_space=pltpu.VMEM)
    specs = [vmem] * len(args) + [pl.BlockSpec(memory_space=pltpu.HBM)] * len(there)
    args = (*args, *(pltpu.with_memory_space_constraint(a, pltpu.HBM) for a in there))
    if flags is not None:
        args, specs = (flags, *args), [pl.BlockSpec(memory_space=pltpu.SMEM), *specs]
    return pl.pallas_call(
        kernel,
        out_shape=[(pltpu.HBM if len(out) == 3 else pltpu.VMEM)(*out[:2]) for out in outs],
        in_specs=specs,
        out_specs=[pl.BlockSpec(memory_space=pltpu.HBM) if len(out) == 3 else vmem for out in outs],
        scratch_shapes=[pltpu.VMEM(shape, dtype) for shape, dtype in scratch]
        + [pltpu.SemaphoreType.DMA((k,)) for k in sems],
        compiler_params=pltpu.CompilerParams(vmem_limit_bytes=vmem_mib * 1024 * 1024),
        cost_estimate=pl.CostEstimate(flops=flops, bytes_accessed=8_000_000, transcendentals=0),
    )(*args)


def per_device(fake_tokens, real_tokens, proj_weight, score_vector):
    ylo, x, z, yhi, c = (lax.axis_index(a) for a in AXES)
    y = yhi * 2 + ylo
    gray_x = (x == 1) | (x == 2)
    core0 = c == 0
    tok = fake_tokens.shape[1]
    rows, hid = proj_weight.shape
    half = hid // 2
    d_in = rows * NZ * 4
    n = 2 * tok
    scale = math.sqrt(hid / (8 * 32 * tok))

    def slice_of(side):
        start = jnp.where(side == 0, x * 256, half + ylo * 512 + gray_x * 256)
        return lax.dynamic_slice_in_dim(proj_weight, start, 256, 1)

    block = ordered(core0, slice_of(c), to_core(slice_of(1 - c)), 0)
    over_z = lax.all_to_all(jnp.broadcast_to(block[None], (NZ, *block.shape)), "z", 0, 0)
    sub = over_z.reshape(d_in // 2, 256)
    own = ordered(jnp.where(core0, yhi == 0, ~gray_x), sub, send(sub, pair), 0)

    own_tokens = jnp.concatenate([fake_tokens[0], real_tokens[0]], 0)
    def join_tokens(other_tokens):
        return call(
            tokens_kernel, 2 * n * d_in * 128,
            [((2 * n, d_in), BF16), ((d_in, 2 * n), BF16, True), ((16, 128), F32)],
            [((n, d_in), BF16), ((n, d_in), BF16), ((d_in, 2 * n), BF16)],
            flags=c[None].astype(jnp.int32), there=(fake_tokens[0], real_tokens[0], other_tokens), sems=[3],
        )

    left, right, tokens, tokens_t, peak = together((own, own), (ring(1), ring(-1)), join_tokens, (to_core(own_tokens),))
    across = send(left, ring(1))

    def score_at(start):
        return lax.dynamic_slice_in_dim(score_vector, c * half + start, 256, 0)

    def scores(one, two, group):
        blocks = (jnp.where(core0, one % 4 * 256, group * 512), jnp.where(core0, two % 4 * 256, group * 512 + 256))
        return jnp.concatenate([score_at(b) for b in blocks])[None]

    flags_1, flags_2 = (jnp.stack([c, at]).astype(jnp.int32) for at in ((y + 3) % 4 // 2, yhi))
    turn, wide = d_in // NZ, half // 2
    states = [((NZ, turn, wide), BF16), ((2 * n, wide), F32), ((n, wide), F32), ((n, wide), BF16)]
    sums = [((2 * n, 128), F32), ((d_in, n), F32)]
    marked = lambda shapes: [(*shape, True) for shape in shapes]

    def forward(flags, score, one, two, earlier):
        pieces = [p.reshape(2, NZ, 2 * rows, 256) for p in (one, two)]
        return call(
            functools.partial(forward_kernel, so_far=bool(earlier)), 6 * n * d_in * wide, [*marked(states), *sums],
            [((2 * n, d_in), BF16), *states], score, *earlier,
            flags=flags, there=(tokens, *pieces), sems=[6, 4], vmem_mib=24,
        )

    w_1, slope_1, curve_1, lifted_1, *earlier = forward(flags_1, scores(x + 3, x + 1, 1 - ylo), left, right, ())
    w_2, slope_2, curve_2, lifted_2, logit, part = forward(flags_2, scores(x, x + 2, ylo), own, across, earlier)
    part_in, logit_in = to_core(part), to_core(logit)

    works = [((n, wide), BF16)] * 2
    terms, tall, r1_shape = ((2, 2, d_in // 2, 256), F32), ((d_in, 2 * n), BF16), ((d_in, n), BF16)
    term_2, r1_t, fake_1, real_1, exponent = call(
        functools.partial(third_kernel, scale), 6 * n * d_in * half,
        [*marked([terms, r1_shape, *works]), ((16, 128), F32)],
        [terms, r1_shape, *works, ((n, d_in), BF16), *works, *states[:3], *states, states[3], tall],
        part, part_in, logit, logit_in, peak, flags=flags_2,
        there=(w_2, slope_2, curve_2, w_1, slope_1, curve_1, lifted_1, lifted_2, tokens_t),
        sems=[9, 3, 16], vmem_mib=36,
    )
    exponent = jnp.concatenate([exponent[:1]] * 2, 1)

    def rest_of_term(r1_t):
        (term_1,) = call(
            fourth_kernel, 6 * n * d_in * wide, marked([terms]), [terms, r1_shape, *works, states[3], tall],
            flags=flags_1, there=(r1_t, fake_1, real_1, lifted_1, tokens_t), sems=[5, 16], vmem_mib=28,
        )
        return [packed(term_1[k].reshape(d_in, 256), exponent) for k in (1, 0)]

    across, *beside = together(
        (packed(term_2[1].reshape(d_in, 256), exponent),), (ring(2),), rest_of_term, (r1_t,)
    )
    from_left, from_right = together(beside, (ring(1), ring(-1)))

    def summed(own, exponent, *messages):
        for values, theirs in map(unpacked, messages):
            own, exponent = own + values, jnp.maximum(exponent, theirs)
        return own, exponent + 2.0

    total, exponent = summed(term_2[0].reshape(d_in, 256), exponent, from_left, from_right, across)

    place = jnp.where(core0, y, x)
    total = total.reshape(2, NZ, 2, rows, 256)

    def quarter(k):
        at = (place + k) % 4
        zero = jnp.zeros_like(at)
        return lax.dynamic_slice(total, (at // 2, zero, at % 2, zero, zero), (1, NZ, 1, rows, 256)).reshape(NZ * rows, 256)

    away = (1, 3, 2)
    got = together([packed(quarter(k), exponent) for k in away], [other_ring(k) for k in away])
    both = summed(quarter(0), exponent, *got)[0].reshape(NZ, rows, 256)
    both = jnp.sum(lax.all_to_all(both, "z", 0, 0), 0)

    spread = lax.all_to_all(jnp.broadcast_to(both[None], (8, *both.shape)), ("ylo", "x"), 0, 0)
    spread = spread.reshape(2, 4, rows, 256)

    def row_group(r):
        first = [spread[r, k] for k in range(4)]
        second = [spread[v, 2 * j + r] for v in (0, 1) for j in (0, 1)]
        return jnp.concatenate([jnp.where(core0, f, g) for f, g in zip(first, second)], 1)

    zero, one = row_group(0), row_group(1)
    theirs = to_core(jnp.where(core0, one, zero))
    return ordered(core0, jnp.where(core0, zero, one), theirs, 1)


def solution(mesh):
    split = Mesh(mesh.devices.reshape(2, NX, NZ, 2, 2), AXES)
    tokens = P(("ylo", "x"), ("z", "yhi", "c"), None)
    shard = P(("z", "yhi", "c"), None)
    return jax.shard_map(
        per_device, mesh=split, in_specs=(tokens, tokens, shard, P()), out_specs=shard, check_vma=False
    )
```

```python
import functools
import math

import jax
import jax.numpy as jnp
from jax import lax
from jax.experimental import pallas as pl
from jax.experimental.pallas import tpu as pltpu
from jax.sharding import Mesh
from jax.sharding import PartitionSpec as P

R1_WEIGHT = 40.0
NX, NY, NZ = 4, 4, 8
AXES = ("ylo", "x", "z", "yhi", "c")
BF16, F16, F32 = jnp.bfloat16, jnp.float16, jnp.float32


def flat_index(x, y, z, c):
    return ((y % 2) * NX + x) * (NZ * 4) + z * 4 + (y // 2) * 2 + c


def send(array, to):
    pairs = []
    for x in range(NX):
        for y in range(NY):
            for z in range(NZ):
                for c in range(2):
                    tx, ty, tc = to(x, y, c)
                    pairs.append((flat_index(x, y, z, c), flat_index(tx % NX, ty % NY, z, tc)))
    return lax.ppermute(array, AXES, pairs)


def to_core(array):
    return send(array, lambda x, y, c: (x, y, 1 - c))


def together(arrays, routes, beside=None, extra=()):
    arrays = lax.optimization_barrier((*arrays, *extra))
    sent = tuple(send(a, to) for a, to in zip(arrays, routes))
    return lax.optimization_barrier((*sent, *(beside(*arrays[len(sent) :]) if beside else ())))


def ring(step):
    return lambda x, y, c: (x + step, y, c) if c == 0 else (x, y + step, c)


def other_ring(step):
    return lambda x, y, c: (x, y + step, c) if c == 0 else (x + step, y, c)


def pair(x, y, c):
    return (x, 3 - y, c) if c == 0 else (x ^ 1, y, c)


def ordered(first_is_mine, mine, theirs, axis):
    return jnp.concatenate(
        [jnp.where(first_is_mine, mine, theirs), jnp.where(first_is_mine, theirs, mine)], axis
    )


def packed(piece, exponent):
    scaled = (piece * jnp.exp2(-exponent)).astype(F16)
    return jnp.concatenate([scaled, jnp.broadcast_to(exponent.astype(F16), (16, piece.shape[1]))], 0)


def unpacked(message):
    exponent = message[-16:-15].astype(F32)
    return message[:-16].astype(F32) * jnp.exp2(exponent), exponent


def column_tiles(width):
    return [(start, min(256, width - start)) for start in range(0, width, 256)]


def nt(a, b):
    return lax.dot_general(a, b, (((1,), (1,)), ((), ())), preferred_element_type=F32)


def flat(block):
    return block.reshape(block.shape[0] * block.shape[1], block.shape[2])


def forward_tiles(tokens_ref, w_ref, score_ref, slope_ref, curve_ref, lifted_ref, logit_ref, first, arriving):
    n = tokens_ref.shape[0] // 2
    for kind in (0, 1):
        arriving[kind].wait()
        rows = slice(kind * n, kind * n + n)
        total = jnp.zeros((n, 128), F32) if first is None else first[rows, :]
        for start, width in column_tiles(w_ref.shape[2]):
            cols = slice(start, start + width)
            preact = jnp.dot(tokens_ref[rows, :], flat(w_ref[:, :, cols]), preferred_element_type=F32)
            score = score_ref[:, cols]
            squash = jax.nn.sigmoid(preact)
            rest = 1.0 - squash
            act = preact * squash * score
            for lane in range(0, width, 128):
                total = total + act[:, lane : lane + 128]
            slope = squash * (1.0 + preact * rest) * score
            slope_ref[rows, cols] = slope
            if kind == 1:
                lifted_ref[:, cols] = slope.astype(BF16)
                curve_ref[:, cols] = squash * rest * (2.0 + preact * (1.0 - 2.0 * squash)) * score
        logit_ref[rows, :] = total


def pull_back(w_ref, lifted_ref, part_ref, so_far):
    height = 2 * w_ref.shape[1]
    for k in range(w_ref.shape[0] // 2):
        rows = slice(k * height, k * height + height)
        value = nt(flat(w_ref[2 * k : 2 * k + 2]), lifted_ref[...])
        part_ref[rows, :] = value if so_far is None else so_far[rows, :] + value


def place_of(flag_ref, piece, sub):
    return jnp.where(flag_ref[0] == 0, sub, flag_ref[1] ^ piece), jnp.where(flag_ref[0] == 0, piece, sub)


def laid(flag_ref, subs, w_ref):
    pairs = []
    for piece in (0, 1):
        for sub in (0, 1):
            half, block = place_of(flag_ref, piece, sub)
            ref = subs[2 * piece + sub]
            height = ref.shape[1]
            rows = pl.ds(pl.multiple_of(half * height, 16), height)
            pairs.append((ref, w_ref.at[:, rows, pl.ds(pl.multiple_of(block * 256, 128), 256)]))
    return pairs


def fetched(sems, *pairs):
    copies = [pltpu.make_async_copy(source, target, sems.at[k]) for k, (source, target) in enumerate(pairs)]
    for copy in copies:
        copy.start()
    return copies


def done(copies):
    for copy in copies:
        copy.wait()


def forward_kernel(flag_ref, score_ref, *refs, so_far):
    earlier, refs = (refs[:2], refs[2:]) if so_far else ((None, None), refs)
    tokens_hbm, one_hbm, refs = refs[0], refs[1], refs[2:]
    two, refs = ((refs[0], refs[1]), refs[2:]) if so_far else ((refs[0].at[0], refs[0].at[1]), refs[1:])
    (w_hbm, slope_hbm, curve_hbm, lifted_hbm, logit_ref, part_ref,
     tokens_ref, w_ref, slope_ref, curve_ref, lifted_ref, sems, out_sems) = refs
    n = lifted_ref.shape[0]
    copies = fetched(
        sems,
        *laid(flag_ref, (one_hbm.at[0], one_hbm.at[1], *two), w_ref),
        *((tokens_hbm.at[k * n : k * n + n, :], tokens_ref.at[k * n : k * n + n, :]) for k in (0, 1)),
    )
    done(copies[:4])
    forward_tiles(tokens_ref, w_ref, score_ref, slope_ref, curve_ref, lifted_ref, logit_ref, earlier[0], copies[4:])
    copies = fetched(
        out_sems, (w_ref, w_hbm), (slope_ref, slope_hbm), (curve_ref, curve_hbm), (lifted_ref, lifted_hbm)
    )
    pull_back(w_ref, lifted_ref, part_ref, earlier[1])
    done(copies)


def tokens_kernel(flag_ref, fake_hbm, real_hbm, other_hbm, tokens_ref, tokens_t_hbm, peak_ref,
                  own_ref, other_ref, tokens_t_ref, sems):
    tok = fake_hbm.shape[0]
    done(
        fetched(
            sems, (fake_hbm, own_ref.at[0:tok, :]), (real_hbm, own_ref.at[tok : 2 * tok, :]), (other_hbm, other_ref)
        )
    )
    first = flag_ref[0] == 0
    for kind in (0, 1):
        mine, theirs = (ref[kind * tok : kind * tok + tok, :] for ref in (own_ref, other_ref))
        start = 2 * kind * tok
        tokens_ref[start : start + tok, :] = jnp.where(first, mine, theirs)
        tokens_ref[start + tok : start + 2 * tok, :] = jnp.where(first, theirs, mine)
        peak = peak_of(tokens_ref[start : start + 2 * tok, :])
        peak_ref[8 * kind : 8 * kind + 8, :] = jnp.broadcast_to(peak, (8, 128))
    tokens_t_ref[...] = tokens_ref[...].T
    done(fetched(sems, (tokens_t_ref, tokens_t_hbm)))


def peak_of(array):
    flat = jnp.max(jnp.abs(array).astype(F32), axis=0, keepdims=True)
    return jnp.max(flat, axis=1, keepdims=True)


def cotangents(scale, logits, r1_ref, w_ref, slope_ref, curve_ref, fake_ref, real_ref):
    n = r1_ref.shape[0]
    fake_ref[...] = (scale * jax.nn.sigmoid(logits[:n]) * slope_ref[0:n, :]).astype(BF16)
    real_gain = -scale * jax.nn.sigmoid(-logits[n:])
    for start, width in column_tiles(w_ref.shape[2]):
        cols = slice(start, start + width)
        back = jnp.dot(r1_ref[...], flat(w_ref[:, :, cols]), preferred_element_type=F32)
        real_ref[:, cols] = (real_gain * slope_ref[n : 2 * n, cols] + back * curve_ref[:, cols]).astype(BF16)


def term_tiles(flag_ref, cotangent_refs, tokens_t_ref, r1_t_ref, term_ref, term_hbm, sems):
    fake_ref, real_ref, lifted_ref = cotangent_refs
    d_in, n = r1_t_ref.shape
    turn = d_in // (2 * NZ)
    leaving = []
    for block in (0, 1):
        cols = slice(256 * block, 256 * block + 256)
        for row in range(0, d_in, 4 * turn):
            rows = slice(row, row + 4 * turn)
            value = (
                jnp.dot(tokens_t_ref[rows, 0:n], fake_ref[:, cols], preferred_element_type=F32)
                + jnp.dot(tokens_t_ref[rows, n : 2 * n], real_ref[:, cols], preferred_element_type=F32)
                + jnp.dot(r1_t_ref[rows, :], lifted_ref[:, cols], preferred_element_type=F32)
            )
            there = slice(row // 2, row // 2 + 2 * turn)
            for half in (0, 1):
                for k in range(2):
                    at = row // 2 + k * turn
                    term_ref[half, block, at : at + turn, :] = value[(2 * k + half) * turn : (2 * k + half + 1) * turn, :]
                piece = jnp.where(flag_ref[0] == 0, block, flag_ref[1] ^ half)
                sub = jnp.where(flag_ref[0] == 0, half, block)
                leaving.append(
                    pltpu.make_async_copy(
                        term_ref.at[half, block, there, :], term_hbm.at[piece, sub, there, :], sems.at[len(leaving)]
                    )
                )
                leaving[-1].start()
    done(leaving)


def third_kernel(scale, flag_ref, part_ref, part_in_ref, logit_ref, logit_in_ref, peak_ref,
                 w_2_hbm, slope_2_hbm, curve_2_hbm, w_1_hbm, slope_1_hbm, curve_1_hbm, lifted_1_hbm, lifted_2_hbm,
                 tokens_t_hbm,
                 term_hbm, r1_t_hbm, fake_1_hbm, real_1_hbm, exp_ref,
                 term_ref, r1_t_ref, fake_1_ref, real_1_ref, r1_ref, fake_2_ref, real_2_ref,
                 w_2_ref, slope_2_ref, curve_2_ref, w_1_ref, slope_1_ref, curve_1_ref, lifted_1_ref, lifted_2_ref,
                 tokens_t_ref, sems, r1_sems, out_sems):
    copies = fetched(
        sems,
        (w_2_hbm, w_2_ref), (slope_2_hbm, slope_2_ref), (curve_2_hbm, curve_2_ref),
        (w_1_hbm, w_1_ref), (slope_1_hbm, slope_1_ref), (curve_1_hbm, curve_1_ref),
        (lifted_1_hbm, lifted_1_ref), (lifted_2_hbm, lifted_2_ref), (tokens_t_hbm, tokens_t_ref),
    )
    r1_t_ref[...] = (scale * R1_WEIGHT * (part_ref[...] + part_in_ref[...])).astype(BF16)
    r1_ref[...] = r1_t_ref[...].T
    logits = jnp.sum(logit_ref[...] + logit_in_ref[...], axis=1, keepdims=True)
    done(copies[:3])
    cotangents(scale, logits, r1_ref, w_2_ref, slope_2_ref, curve_2_ref, fake_2_ref, real_2_ref)
    done(copies[3:6])
    cotangents(scale, logits, r1_ref, w_1_ref, slope_1_ref, curve_1_ref, fake_1_ref, real_1_ref)
    passed = fetched(r1_sems, (r1_t_ref, r1_t_hbm), (fake_1_ref, fake_1_hbm), (real_1_ref, real_1_hbm))
    done(copies[6:])
    first, second = (fake_1_ref, real_1_ref, lifted_1_ref), (fake_2_ref, real_2_ref, lifted_2_ref)
    peaks = [jnp.maximum(peak_of(one[...]), peak_of(two[...])) for one, two in zip(first, second)]
    n = r1_ref.shape[0]
    bound = n * (
        peak_ref[0:1, 0:1] * peaks[0] + peak_ref[8:9, 0:1] * peaks[1] + peak_of(r1_t_ref[...]) * peaks[2]
    )
    bound = jnp.broadcast_to(bound, (16, 128))
    exp_ref[...] = jnp.ceil(jnp.log(jnp.maximum(bound, 1e-30)) * (1.0 / math.log(2.0)) + 0.01) - 15.0
    term_tiles(flag_ref, second, tokens_t_ref, r1_t_ref, term_ref, term_hbm, out_sems)
    done(passed)


def fourth_kernel(flag_ref, r1_t_hbm, fake_hbm, real_hbm, lifted_hbm, tokens_t_hbm, term_hbm,
                  term_ref, r1_t_ref, fake_ref, real_ref, lifted_ref, tokens_t_ref, sems, out_sems):
    done(
        fetched(
            sems,
            (r1_t_hbm, r1_t_ref), (fake_hbm, fake_ref), (real_hbm, real_ref), (lifted_hbm, lifted_ref),
            (tokens_t_hbm, tokens_t_ref),
        )
    )
    term_tiles(flag_ref, (fake_ref, real_ref, lifted_ref), tokens_t_ref, r1_t_ref, term_ref, term_hbm, out_sems)


def call(kernel, flops, outs, scratch, *args, flags=None, there=(), anywhere=(), sems=(), vmem_mib=20):
    vmem = pl.BlockSpec(memory_space=pltpu.VMEM)
    specs = [vmem] * len(args) + [pl.BlockSpec(memory_space=pltpu.HBM)] * len(there)
    specs += [pl.BlockSpec(memory_space=pl.ANY)] * len(anywhere)
    args = (*args, *(pltpu.with_memory_space_constraint(a, pltpu.HBM) for a in there), *anywhere)
    if flags is not None:
        args, specs = (flags, *args), [pl.BlockSpec(memory_space=pltpu.SMEM), *specs]
    return pl.pallas_call(
        kernel,
        out_shape=[(pltpu.HBM if len(out) == 3 else pltpu.VMEM)(*out[:2]) for out in outs],
        in_specs=specs,
        out_specs=[pl.BlockSpec(memory_space=pltpu.HBM) if len(out) == 3 else vmem for out in outs],
        scratch_shapes=[pltpu.VMEM(shape, dtype) for shape, dtype in scratch]
        + [pltpu.SemaphoreType.DMA((k,)) for k in sems],
        compiler_params=pltpu.CompilerParams(vmem_limit_bytes=vmem_mib * 1024 * 1024),
        cost_estimate=pl.CostEstimate(flops=flops, bytes_accessed=8_000_000, transcendentals=0),
    )(*args)


def per_device(fake_tokens, real_tokens, proj_weight, score_vector):
    ylo, x, z, yhi, c = (lax.axis_index(a) for a in AXES)
    y = yhi * 2 + ylo
    gray_x = (x == 1) | (x == 2)
    core0 = c == 0
    tok = fake_tokens.shape[1]
    rows, hid = proj_weight.shape
    half = hid // 2
    d_in = rows * NZ * 4
    n = 2 * tok
    scale = math.sqrt(hid / (8 * 32 * tok))

    def slice_of(side):
        start = jnp.where(side == 0, x * 256, half + ylo * 512 + gray_x * 256)
        return lax.dynamic_slice_in_dim(proj_weight, start, 256, 1)

    block = ordered(core0, slice_of(c), to_core(slice_of(1 - c)), 0)
    over_z = lax.all_to_all(jnp.broadcast_to(block[None], (NZ, *block.shape)), "z", 0, 0)
    sub = over_z.reshape(d_in // 2, 256)
    own = ordered(jnp.where(core0, yhi == 0, ~gray_x), sub, send(sub, pair), 0)

    own_tokens = jnp.concatenate([fake_tokens[0], real_tokens[0]], 0)
    def join_tokens(other_tokens):
        return call(
            tokens_kernel, 2 * n * d_in * 128,
            [((2 * n, d_in), BF16), ((d_in, 2 * n), BF16, True), ((16, 128), F32)],
            [((n, d_in), BF16), ((n, d_in), BF16), ((d_in, 2 * n), BF16)],
            flags=c[None].astype(jnp.int32), there=(fake_tokens[0], real_tokens[0], other_tokens), sems=[3],
        )

    left, right, tokens, tokens_t, peak = together((own, own), (ring(1), ring(-1)), join_tokens, (to_core(own_tokens),))
    across = together((left[: d_in // 2], right[d_in // 2 :]), (ring(1), ring(-1)))

    def score_at(start):
        return lax.dynamic_slice_in_dim(score_vector, c * half + start, 256, 0)

    def scores(one, two, group):
        blocks = (jnp.where(core0, one % 4 * 256, group * 512), jnp.where(core0, two % 4 * 256, group * 512 + 256))
        return jnp.concatenate([score_at(b) for b in blocks])[None]

    flags_1, flags_2 = (jnp.stack([c, at]).astype(jnp.int32) for at in ((y + 3) % 4 // 2, yhi))
    turn, wide = d_in // NZ, half // 2
    states = [((NZ, turn, wide), BF16), ((2 * n, wide), F32), ((n, wide), F32), ((n, wide), BF16)]
    sums = [((2 * n, 128), F32), ((d_in, n), F32)]
    marked = lambda shapes: [(*shape, True) for shape in shapes]

    def forward(flags, score, pieces, earlier):
        return call(
            functools.partial(forward_kernel, so_far=bool(earlier)), 6 * n * d_in * wide, [*marked(states), *sums],
            [((2 * n, d_in), BF16), *states], score, *earlier,
            flags=flags, there=(tokens,), anywhere=pieces, sems=[6, 4], vmem_mib=24,
        )

    left, right, own = (p.reshape(2, NZ, 2 * rows, 256) for p in (left, right, own))
    w_1, slope_1, curve_1, lifted_1, *earlier = forward(flags_1, scores(x + 3, x + 1, 1 - ylo), (left, right), ())
    across = [p.reshape(NZ, 2 * rows, 256) for p in across]
    w_2, slope_2, curve_2, lifted_2, logit, part = forward(flags_2, scores(x, x + 2, ylo), (own, *across), earlier)
    part_in, logit_in = to_core(part), to_core(logit)

    works = [((n, wide), BF16)] * 2
    terms, tall, r1_shape = ((2, 2, d_in // 2, 256), F32), ((d_in, 2 * n), BF16), ((d_in, n), BF16)
    term_2, r1_t, fake_1, real_1, exponent = call(
        functools.partial(third_kernel, scale), 6 * n * d_in * half,
        [*marked([terms, r1_shape, *works]), ((16, 128), F32)],
        [terms, r1_shape, *works, ((n, d_in), BF16), *works, *states[:3], *states, states[3], tall],
        part, part_in, logit, logit_in, peak, flags=flags_2,
        there=(w_2, slope_2, curve_2, w_1, slope_1, curve_1, lifted_1, lifted_2, tokens_t),
        sems=[9, 3, 16], vmem_mib=36,
    )
    exponent = jnp.concatenate([exponent[:1]] * 2, 1)

    def rest_of_term(r1_t):
        (term_1,) = call(
            fourth_kernel, 6 * n * d_in * wide, marked([terms]), [terms, r1_shape, *works, states[3], tall],
            flags=flags_1, there=(r1_t, fake_1, real_1, lifted_1, tokens_t), sems=[5, 16], vmem_mib=28,
        )
        return (term_1,)

    across, term_1 = together(
        (packed(term_2[1].reshape(d_in, 256), exponent),), (ring(2),), rest_of_term, (r1_t,)
    )
    beside = [packed(term_1[k].reshape(d_in, 256), exponent) for k in (1, 0)]
    from_left, from_right = together(beside, (ring(1), ring(-1)))

    def summed(own, exponent, *messages):
        for values, theirs in map(unpacked, messages):
            own, exponent = own + values, jnp.maximum(exponent, theirs)
        return own, exponent + 2.0

    total, exponent = summed(term_2[0].reshape(d_in, 256), exponent, from_left, from_right, across)

    place = jnp.where(core0, y, x)
    total = total.reshape(2, NZ, 2, rows, 256)

    def quarter(k):
        at = (place + k) % 4
        zero = jnp.zeros_like(at)
        return lax.dynamic_slice(total, (at // 2, zero, at % 2, zero, zero), (1, NZ, 1, rows, 256)).reshape(NZ * rows, 256)

    away = (1, 3, 2)
    got = together([packed(quarter(k), exponent) for k in away], [other_ring(k) for k in away])
    both = summed(quarter(0), exponent, *got)[0].reshape(NZ, rows, 256)
    both = jnp.sum(lax.all_to_all(both, "z", 0, 0), 0)

    spread = lax.all_to_all(jnp.broadcast_to(both[None], (8, *both.shape)), ("ylo", "x"), 0, 0)
    spread = spread.reshape(2, 4, rows, 256)

    def row_group(r):
        first = [spread[r, k] for k in range(4)]
        second = [spread[v, 2 * j + r] for v in (0, 1) for j in (0, 1)]
        return jnp.concatenate([jnp.where(core0, f, g) for f, g in zip(first, second)], 1)

    zero, one = row_group(0), row_group(1)
    theirs = to_core(jnp.where(core0, one, zero))
    return ordered(core0, jnp.where(core0, zero, one), theirs, 1)


def solution(mesh):
    split = Mesh(mesh.devices.reshape(2, NX, NZ, 2, 2), AXES)
    tokens = P(("ylo", "x"), ("z", "yhi", "c"), None)
    shard = P(("z", "yhi", "c"), None)
    return jax.shard_map(
        per_device, mesh=split, in_specs=(tokens, tokens, shard, P()), out_specs=shard, check_vma=False
    )
```

```python
import functools
import math

import jax
import jax.numpy as jnp
from jax import lax
from jax.experimental import pallas as pl
from jax.experimental.pallas import tpu as pltpu
from jax.sharding import Mesh
from jax.sharding import PartitionSpec as P

R1_WEIGHT = 40.0
NX, NY, NZ = 4, 4, 8
AXES = ("ylo", "x", "z", "yhi", "c")
BF16, F16, F32 = jnp.bfloat16, jnp.float16, jnp.float32


def flat_index(x, y, z, c):
    return ((y % 2) * NX + x) * (NZ * 4) + z * 4 + (y // 2) * 2 + c


def send(array, to):
    pairs = []
    for x in range(NX):
        for y in range(NY):
            for z in range(NZ):
                for c in range(2):
                    tx, ty, tc = to(x, y, c)
                    pairs.append((flat_index(x, y, z, c), flat_index(tx % NX, ty % NY, z, tc)))
    return lax.ppermute(array, AXES, pairs)


def to_core(array):
    return send(array, lambda x, y, c: (x, y, 1 - c))


def together(arrays, routes, beside=None, extra=()):
    arrays = lax.optimization_barrier((*arrays, *extra))
    sent = tuple(send(a, to) for a, to in zip(arrays, routes))
    return lax.optimization_barrier((*sent, *(beside(*arrays[len(sent) :]) if beside else ())))


def ring(step):
    return lambda x, y, c: (x + step, y, c) if c == 0 else (x, y + step, c)


def other_ring(step):
    return lambda x, y, c: (x, y + step, c) if c == 0 else (x + step, y, c)


def pair(x, y, c):
    return (x, 3 - y, c) if c == 0 else (x ^ 1, y, c)


def ordered(first_is_mine, mine, theirs, axis):
    return jnp.concatenate(
        [jnp.where(first_is_mine, mine, theirs), jnp.where(first_is_mine, theirs, mine)], axis
    )


def scaled_down(array, exponent):
    return (array * jnp.exp2(-exponent)).astype(F16)


def packed(piece, exponent):
    scaled = piece if piece.dtype == F16 else scaled_down(piece, exponent)
    return jnp.concatenate([scaled, jnp.broadcast_to(exponent.astype(F16), (16, piece.shape[1]))], 0)


def unpacked(message):
    exponent = message[-16:-15].astype(F32)
    return message[:-16].astype(F32) * jnp.exp2(exponent), exponent


def column_tiles(width):
    return [(start, min(256, width - start)) for start in range(0, width, 256)]


def nt(a, b):
    return lax.dot_general(a, b, (((1,), (1,)), ((), ())), preferred_element_type=F32)


def flat(block):
    return block.reshape(block.shape[0] * block.shape[1], block.shape[2])


def forward_tiles(tokens_ref, w_ref, score_ref, slope_ref, curve_ref, lifted_ref, logit_ref, first, arriving):
    n = tokens_ref.shape[0] // 2
    for kind in (0, 1):
        arriving[kind].wait()
        rows = slice(kind * n, kind * n + n)
        total = jnp.zeros((n, 128), F32) if first is None else first[rows, :]
        for start, width in column_tiles(w_ref.shape[2]):
            cols = slice(start, start + width)
            preact = jnp.dot(tokens_ref[rows, :], flat(w_ref[:, :, cols]), preferred_element_type=F32)
            score = score_ref[:, cols]
            squash = jax.nn.sigmoid(preact)
            rest = 1.0 - squash
            act = preact * squash * score
            for lane in range(0, width, 128):
                total = total + act[:, lane : lane + 128]
            slope = squash * (1.0 + preact * rest) * score
            slope_ref[rows, cols] = slope
            if kind == 1:
                lifted_ref[:, cols] = slope.astype(BF16)
                curve_ref[:, cols] = squash * rest * (2.0 + preact * (1.0 - 2.0 * squash)) * score
        logit_ref[rows, :] = total


def pull_back(w_ref, lifted_ref, part_ref, so_far):
    height = 2 * w_ref.shape[1]
    for k in range(w_ref.shape[0] // 2):
        rows = slice(k * height, k * height + height)
        value = nt(flat(w_ref[2 * k : 2 * k + 2]), lifted_ref[...])
        part_ref[rows, :] = value if so_far is None else so_far[rows, :] + value


def place_of(flag_ref, piece, sub):
    return jnp.where(flag_ref[0] == 0, sub, flag_ref[1] ^ piece), jnp.where(flag_ref[0] == 0, piece, sub)


def laid(flag_ref, subs, w_ref):
    pairs = []
    for piece in (0, 1):
        for sub in (0, 1):
            half, block = place_of(flag_ref, piece, sub)
            ref = subs[2 * piece + sub]
            height = ref.shape[1]
            rows = pl.ds(pl.multiple_of(half * height, 16), height)
            pairs.append((ref, w_ref.at[:, rows, pl.ds(pl.multiple_of(block * 256, 128), 256)]))
    return pairs


def fetched(sems, *pairs):
    copies = [pltpu.make_async_copy(source, target, sems.at[k]) for k, (source, target) in enumerate(pairs)]
    for copy in copies:
        copy.start()
    return copies


def done(copies):
    for copy in copies:
        copy.wait()


def forward_kernel(flag_ref, score_ref, *refs, so_far):
    earlier, refs = (refs[:2], refs[2:]) if so_far else ((None, None), refs)
    tokens_hbm, one_hbm, refs = refs[0], refs[1], refs[2:]
    two, refs = ((refs[0], refs[1]), refs[2:]) if so_far else ((refs[0].at[0], refs[0].at[1]), refs[1:])
    (w_hbm, slope_hbm, curve_hbm, lifted_hbm, logit_ref, part_ref,
     tokens_ref, w_ref, slope_ref, curve_ref, lifted_ref, sems, out_sems) = refs
    n = lifted_ref.shape[0]
    copies = fetched(
        sems,
        *laid(flag_ref, (one_hbm.at[0], one_hbm.at[1], *two), w_ref),
        *((tokens_hbm.at[k * n : k * n + n, :], tokens_ref.at[k * n : k * n + n, :]) for k in (0, 1)),
    )
    done(copies[:4])
    forward_tiles(tokens_ref, w_ref, score_ref, slope_ref, curve_ref, lifted_ref, logit_ref, earlier[0], copies[4:])
    copies = fetched(
        out_sems, (w_ref, w_hbm), (slope_ref, slope_hbm), (curve_ref, curve_hbm), (lifted_ref, lifted_hbm)
    )
    pull_back(w_ref, lifted_ref, part_ref, earlier[1])
    done(copies)


def tokens_kernel(flag_ref, fake_hbm, real_hbm, other_hbm, tokens_ref, tokens_t_hbm, peak_ref,
                  own_ref, other_ref, tokens_t_ref, sems):
    tok = fake_hbm.shape[0]
    done(
        fetched(
            sems, (fake_hbm, own_ref.at[0:tok, :]), (real_hbm, own_ref.at[tok : 2 * tok, :]), (other_hbm, other_ref)
        )
    )
    first = flag_ref[0] == 0
    for kind in (0, 1):
        mine, theirs = (ref[kind * tok : kind * tok + tok, :] for ref in (own_ref, other_ref))
        start = 2 * kind * tok
        tokens_ref[start : start + tok, :] = jnp.where(first, mine, theirs)
        tokens_ref[start + tok : start + 2 * tok, :] = jnp.where(first, theirs, mine)
        peak = peak_of(tokens_ref[start : start + 2 * tok, :])
        peak_ref[8 * kind : 8 * kind + 8, :] = jnp.broadcast_to(peak, (8, 128))
    tokens_t_ref[...] = tokens_ref[...].T
    done(fetched(sems, (tokens_t_ref, tokens_t_hbm)))


def peak_of(array):
    flat = jnp.max(jnp.abs(array).astype(F32), axis=0, keepdims=True)
    return jnp.max(flat, axis=1, keepdims=True)


def cotangents(scale, logits, r1_ref, w_ref, slope_ref, curve_ref, fake_ref, real_ref):
    n = r1_ref.shape[0]
    fake_ref[...] = (scale * jax.nn.sigmoid(logits[:n]) * slope_ref[0:n, :]).astype(BF16)
    real_gain = -scale * jax.nn.sigmoid(-logits[n:])
    for start, width in column_tiles(w_ref.shape[2]):
        cols = slice(start, start + width)
        back = jnp.dot(r1_ref[...], flat(w_ref[:, :, cols]), preferred_element_type=F32)
        real_ref[:, cols] = (real_gain * slope_ref[n : 2 * n, cols] + back * curve_ref[:, cols]).astype(BF16)


def term_tiles(flag_ref, cotangent_refs, tokens_t_ref, r1_t_ref, term_ref, term_hbm, sems):
    fake_ref, real_ref, lifted_ref = cotangent_refs
    d_in, n = r1_t_ref.shape
    turn = d_in // (2 * NZ)
    leaving = []
    for block in (0, 1):
        cols = slice(256 * block, 256 * block + 256)
        for row in range(0, d_in, 4 * turn):
            rows = slice(row, row + 4 * turn)
            value = (
                jnp.dot(tokens_t_ref[rows, 0:n], fake_ref[:, cols], preferred_element_type=F32)
                + jnp.dot(tokens_t_ref[rows, n : 2 * n], real_ref[:, cols], preferred_element_type=F32)
                + jnp.dot(r1_t_ref[rows, :], lifted_ref[:, cols], preferred_element_type=F32)
            )
            there = slice(row // 2, row // 2 + 2 * turn)
            for half in (0, 1):
                for k in range(2):
                    at = row // 2 + k * turn
                    term_ref[half, block, at : at + turn, :] = value[(2 * k + half) * turn : (2 * k + half + 1) * turn, :]
                piece = jnp.where(flag_ref[0] == 0, block, flag_ref[1] ^ half)
                sub = jnp.where(flag_ref[0] == 0, half, block)
                leaving.append(
                    pltpu.make_async_copy(
                        term_ref.at[half, block, there, :], term_hbm.at[piece, sub, there, :], sems.at[len(leaving)]
                    )
                )
                leaving[-1].start()
    done(leaving)


def third_kernel(scale, flag_ref, part_ref, part_in_ref, logit_ref, logit_in_ref, peak_ref,
                 w_2_hbm, slope_2_hbm, curve_2_hbm, w_1_hbm, slope_1_hbm, curve_1_hbm, lifted_1_hbm, lifted_2_hbm,
                 tokens_t_hbm,
                 term_hbm, r1_t_hbm, fake_1_hbm, real_1_hbm, exp_ref,
                 term_ref, r1_t_ref, fake_1_ref, real_1_ref, r1_ref, fake_2_ref, real_2_ref,
                 w_2_ref, slope_2_ref, curve_2_ref, w_1_ref, slope_1_ref, curve_1_ref, lifted_1_ref, lifted_2_ref,
                 tokens_t_ref, sems, r1_sems, out_sems):
    copies = fetched(
        sems,
        (w_2_hbm, w_2_ref), (slope_2_hbm, slope_2_ref), (curve_2_hbm, curve_2_ref),
        (w_1_hbm, w_1_ref), (slope_1_hbm, slope_1_ref), (curve_1_hbm, curve_1_ref),
        (lifted_1_hbm, lifted_1_ref), (lifted_2_hbm, lifted_2_ref), (tokens_t_hbm, tokens_t_ref),
    )
    r1_t_ref[...] = (scale * R1_WEIGHT * (part_ref[...] + part_in_ref[...])).astype(BF16)
    r1_ref[...] = r1_t_ref[...].T
    logits = jnp.sum(logit_ref[...] + logit_in_ref[...], axis=1, keepdims=True)
    done(copies[:3])
    cotangents(scale, logits, r1_ref, w_2_ref, slope_2_ref, curve_2_ref, fake_2_ref, real_2_ref)
    done(copies[3:6])
    cotangents(scale, logits, r1_ref, w_1_ref, slope_1_ref, curve_1_ref, fake_1_ref, real_1_ref)
    passed = fetched(r1_sems, (r1_t_ref, r1_t_hbm), (fake_1_ref, fake_1_hbm), (real_1_ref, real_1_hbm))
    done(copies[6:])
    first, second = (fake_1_ref, real_1_ref, lifted_1_ref), (fake_2_ref, real_2_ref, lifted_2_ref)
    peaks = [jnp.maximum(peak_of(one[...]), peak_of(two[...])) for one, two in zip(first, second)]
    n = r1_ref.shape[0]
    bound = n * (
        peak_ref[0:1, 0:1] * peaks[0] + peak_ref[8:9, 0:1] * peaks[1] + peak_of(r1_t_ref[...]) * peaks[2]
    )
    bound = jnp.broadcast_to(bound, (16, 128))
    exp_ref[...] = jnp.ceil(jnp.log(jnp.maximum(bound, 1e-30)) * (1.0 / math.log(2.0)) + 0.01) - 15.0
    term_tiles(flag_ref, second, tokens_t_ref, r1_t_ref, term_ref, term_hbm, out_sems)
    done(passed)


def fourth_kernel(flag_ref, r1_t_hbm, fake_hbm, real_hbm, lifted_hbm, tokens_t_hbm, term_hbm,
                  term_ref, r1_t_ref, fake_ref, real_ref, lifted_ref, tokens_t_ref, sems, out_sems):
    done(
        fetched(
            sems,
            (r1_t_hbm, r1_t_ref), (fake_hbm, fake_ref), (real_hbm, real_ref), (lifted_hbm, lifted_ref),
            (tokens_t_hbm, tokens_t_ref),
        )
    )
    term_tiles(flag_ref, (fake_ref, real_ref, lifted_ref), tokens_t_ref, r1_t_ref, term_ref, term_hbm, out_sems)


def call(kernel, flops, outs, scratch, *args, flags=None, there=(), anywhere=(), sems=(), vmem_mib=20):
    vmem = pl.BlockSpec(memory_space=pltpu.VMEM)
    specs = [vmem] * len(args) + [pl.BlockSpec(memory_space=pltpu.HBM)] * len(there)
    specs += [pl.BlockSpec(memory_space=pl.ANY)] * len(anywhere)
    args = (*args, *(pltpu.with_memory_space_constraint(a, pltpu.HBM) for a in there), *anywhere)
    if flags is not None:
        args, specs = (flags, *args), [pl.BlockSpec(memory_space=pltpu.SMEM), *specs]
    return pl.pallas_call(
        kernel,
        out_shape=[(pltpu.HBM if len(out) == 3 else pltpu.VMEM)(*out[:2]) for out in outs],
        in_specs=specs,
        out_specs=[pl.BlockSpec(memory_space=pltpu.HBM) if len(out) == 3 else vmem for out in outs],
        scratch_shapes=[pltpu.VMEM(shape, dtype) for shape, dtype in scratch]
        + [pltpu.SemaphoreType.DMA((k,)) for k in sems],
        compiler_params=pltpu.CompilerParams(vmem_limit_bytes=vmem_mib * 1024 * 1024),
        cost_estimate=pl.CostEstimate(flops=flops, bytes_accessed=8_000_000, transcendentals=0),
    )(*args)


def per_device(fake_tokens, real_tokens, proj_weight, score_vector):
    ylo, x, z, yhi, c = (lax.axis_index(a) for a in AXES)
    y = yhi * 2 + ylo
    gray_x = (x == 1) | (x == 2)
    core0 = c == 0
    tok = fake_tokens.shape[1]
    rows, hid = proj_weight.shape
    half = hid // 2
    d_in = rows * NZ * 4
    n = 2 * tok
    scale = math.sqrt(hid / (8 * 32 * tok))

    def slice_of(side):
        start = jnp.where(side == 0, x * 256, half + ylo * 512 + gray_x * 256)
        return lax.dynamic_slice_in_dim(proj_weight, start, 256, 1)

    block = ordered(core0, slice_of(c), to_core(slice_of(1 - c)), 0)
    over_z = lax.all_to_all(jnp.broadcast_to(block[None], (NZ, *block.shape)), "z", 0, 0)
    sub = over_z.reshape(d_in // 2, 256)
    own = ordered(jnp.where(core0, yhi == 0, ~gray_x), sub, send(sub, pair), 0)

    own_tokens = jnp.concatenate([fake_tokens[0], real_tokens[0]], 0)
    def join_tokens(other_tokens):
        return call(
            tokens_kernel, 2 * n * d_in * 128,
            [((2 * n, d_in), BF16), ((d_in, 2 * n), BF16, True), ((16, 128), F32)],
            [((n, d_in), BF16), ((n, d_in), BF16), ((d_in, 2 * n), BF16)],
            flags=c[None].astype(jnp.int32), there=(fake_tokens[0], real_tokens[0], other_tokens), sems=[3],
        )

    left, right, tokens, tokens_t, peak = together((own, own), (ring(1), ring(-1)), join_tokens, (to_core(own_tokens),))
    across = together((left[: d_in // 2], right[d_in // 2 :]), (ring(1), ring(-1)))

    def score_at(start):
        return lax.dynamic_slice_in_dim(score_vector, c * half + start, 256, 0)

    def scores(one, two, group):
        blocks = (jnp.where(core0, one % 4 * 256, group * 512), jnp.where(core0, two % 4 * 256, group * 512 + 256))
        return jnp.concatenate([score_at(b) for b in blocks])[None]

    flags_1, flags_2 = (jnp.stack([c, at]).astype(jnp.int32) for at in ((y + 3) % 4 // 2, yhi))
    turn, wide = d_in // NZ, half // 2
    states = [((NZ, turn, wide), BF16), ((2 * n, wide), F32), ((n, wide), F32), ((n, wide), BF16)]
    sums = [((2 * n, 128), F32), ((d_in, n), F32)]
    marked = lambda shapes: [(*shape, True) for shape in shapes]

    def forward(flags, score, pieces, earlier):
        return call(
            functools.partial(forward_kernel, so_far=bool(earlier)), 6 * n * d_in * wide, [*marked(states), *sums],
            [((2 * n, d_in), BF16), *states], score, *earlier,
            flags=flags, there=(tokens,), anywhere=pieces, sems=[6, 4], vmem_mib=24,
        )

    left, right, own = (p.reshape(2, NZ, 2 * rows, 256) for p in (left, right, own))
    w_1, slope_1, curve_1, lifted_1, *earlier = forward(flags_1, scores(x + 3, x + 1, 1 - ylo), (left, right), ())
    across = [p.reshape(NZ, 2 * rows, 256) for p in across]
    w_2, slope_2, curve_2, lifted_2, logit, part = forward(flags_2, scores(x, x + 2, ylo), (own, *across), earlier)
    part_in, logit_in = to_core(part), to_core(logit)

    works = [((n, wide), BF16)] * 2
    terms, tall, r1_shape = ((2, 2, d_in // 2, 256), F32), ((d_in, 2 * n), BF16), ((d_in, n), BF16)
    term_2, r1_t, fake_1, real_1, exponent = call(
        functools.partial(third_kernel, scale), 6 * n * d_in * half,
        [*marked([terms, r1_shape, *works]), ((16, 128), F32)],
        [terms, r1_shape, *works, ((n, d_in), BF16), *works, *states[:3], *states, states[3], tall],
        part, part_in, logit, logit_in, peak, flags=flags_2,
        there=(w_2, slope_2, curve_2, w_1, slope_1, curve_1, lifted_1, lifted_2, tokens_t),
        sems=[9, 3, 16], vmem_mib=36,
    )
    exponent = jnp.concatenate([exponent[:1]] * 2, 1)

    def rest_of_term(r1_t):
        (term_1,) = call(
            fourth_kernel, 6 * n * d_in * wide, marked([terms]), [terms, r1_shape, *works, states[3], tall],
            flags=flags_1, there=(r1_t, fake_1, real_1, lifted_1, tokens_t), sems=[5, 16], vmem_mib=28,
        )
        return (term_1,)

    across, term_1 = together(
        (packed(lax.optimization_barrier(scaled_down(term_2, exponent))[1].reshape(d_in, 256), exponent),),
        (ring(2),), rest_of_term, (r1_t,),
    )
    halves = lax.optimization_barrier(scaled_down(term_1, exponent))
    beside = [packed(halves[k].reshape(d_in, 256), exponent) for k in (1, 0)]
    from_left, from_right = together(beside, (ring(1), ring(-1)))

    def summed(own, exponent, *messages):
        for values, theirs in map(unpacked, messages):
            own, exponent = own + values, jnp.maximum(exponent, theirs)
        return own, exponent + 2.0

    total, exponent = summed(term_2[0].reshape(d_in, 256), exponent, from_left, from_right, across)

    place = jnp.where(core0, y, x)
    total = total.reshape(2, NZ, 2, rows, 256)

    def quarter(k):
        at = (place + k) % 4
        zero = jnp.zeros_like(at)
        return lax.dynamic_slice(total, (at // 2, zero, at % 2, zero, zero), (1, NZ, 1, rows, 256)).reshape(NZ * rows, 256)

    away = (1, 3, 2)
    got = together([packed(quarter(k), exponent) for k in away], [other_ring(k) for k in away])
    both = summed(quarter(0), exponent, *got)[0].reshape(NZ, rows, 256)
    both = jnp.sum(lax.all_to_all(both, "z", 0, 0), 0)

    spread = lax.all_to_all(jnp.broadcast_to(both[None], (8, *both.shape)), ("ylo", "x"), 0, 0)
    spread = spread.reshape(2, 4, rows, 256)

    def row_group(r):
        first = [spread[r, k] for k in range(4)]
        second = [spread[v, 2 * j + r] for v in (0, 1) for j in (0, 1)]
        return jnp.concatenate([jnp.where(core0, f, g) for f, g in zip(first, second)], 1)

    zero, one = row_group(0), row_group(1)
    theirs = to_core(jnp.where(core0, one, zero))
    return ordered(core0, jnp.where(core0, zero, one), theirs, 1)


def solution(mesh):
    split = Mesh(mesh.devices.reshape(2, NX, NZ, 2, 2), AXES)
    tokens = P(("ylo", "x"), ("z", "yhi", "c"), None)
    shard = P(("z", "yhi", "c"), None)
    return jax.shard_map(
        per_device, mesh=split, in_specs=(tokens, tokens, shard, P()), out_specs=shard, check_vma=False
    )
```

```python
import functools
import math

import jax
import jax.numpy as jnp
from jax import lax
from jax.experimental import pallas as pl
from jax.experimental.pallas import tpu as pltpu
from jax.sharding import Mesh
from jax.sharding import PartitionSpec as P

R1_WEIGHT = 40.0
NX, NY, NZ = 4, 4, 8
AXES = ("ylo", "x", "z", "yhi", "c")
BF16, F16, F32 = jnp.bfloat16, jnp.float16, jnp.float32


def flat_index(x, y, z, c):
    return ((y % 2) * NX + x) * (NZ * 4) + z * 4 + (y // 2) * 2 + c


def send(array, to):
    pairs = []
    for x in range(NX):
        for y in range(NY):
            for z in range(NZ):
                for c in range(2):
                    tx, ty, tc = to(x, y, c)
                    pairs.append((flat_index(x, y, z, c), flat_index(tx % NX, ty % NY, z, tc)))
    return lax.ppermute(array, AXES, pairs)


def to_core(array):
    return send(array, lambda x, y, c: (x, y, 1 - c))


def together(arrays, routes, beside=None, extra=()):
    arrays = lax.optimization_barrier((*arrays, *extra))
    sent = tuple(send(a, to) for a, to in zip(arrays, routes))
    return lax.optimization_barrier((*sent, *(beside(*arrays[len(sent) :]) if beside else ())))


def ring(step):
    return lambda x, y, c: (x + step, y, c) if c == 0 else (x, y + step, c)


def other_ring(step):
    return lambda x, y, c: (x, y + step, c) if c == 0 else (x + step, y, c)


def pair(x, y, c):
    return (x, 3 - y, c) if c == 0 else (x ^ 1, y, c)


def ordered(first_is_mine, mine, theirs, axis):
    return jnp.concatenate(
        [jnp.where(first_is_mine, mine, theirs), jnp.where(first_is_mine, theirs, mine)], axis
    )


def packed(piece, exponent):
    scaled = (piece * jnp.exp2(-exponent)).astype(F16)
    return jnp.concatenate([scaled, jnp.broadcast_to(exponent.astype(F16), (16, piece.shape[1]))], 0)


def unpacked(message):
    exponent = message[-16:-15].astype(F32)
    return message[:-16].astype(F32) * jnp.exp2(exponent), exponent


def column_tiles(width):
    return [(start, min(256, width - start)) for start in range(0, width, 256)]


def nt(a, b):
    return lax.dot_general(a, b, (((1,), (1,)), ((), ())), preferred_element_type=F32)


def flat(block):
    return block.reshape(block.shape[0] * block.shape[1], block.shape[2])


def forward_tiles(tokens_ref, w_ref, score_ref, slope_ref, curve_ref, lifted_ref, logit_ref, first, arriving):
    n = tokens_ref.shape[0] // 2
    for kind in (0, 1):
        arriving[kind].wait()
        rows = slice(kind * n, kind * n + n)
        total = jnp.zeros((n, 128), F32) if first is None else first[rows, :]
        for start, width in column_tiles(w_ref.shape[2]):
            cols = slice(start, start + width)
            preact = jnp.dot(tokens_ref[rows, :], flat(w_ref[:, :, cols]), preferred_element_type=F32)
            score = score_ref[:, cols]
            squash = jax.nn.sigmoid(preact)
            rest = 1.0 - squash
            act = preact * squash * score
            for lane in range(0, width, 128):
                total = total + act[:, lane : lane + 128]
            slope = squash * (1.0 + preact * rest) * score
            slope_ref[rows, cols] = slope
            if kind == 1:
                lifted_ref[:, cols] = slope.astype(BF16)
                curve_ref[:, cols] = squash * rest * (2.0 + preact * (1.0 - 2.0 * squash)) * score
        logit_ref[rows, :] = total


def pull_back(w_ref, lifted_ref, part_ref, so_far):
    height = 2 * w_ref.shape[1]
    for k in range(w_ref.shape[0] // 2):
        rows = slice(k * height, k * height + height)
        value = nt(flat(w_ref[2 * k : 2 * k + 2]), lifted_ref[...])
        part_ref[rows, :] = value if so_far is None else so_far[rows, :] + value


def place_of(flag_ref, piece, sub):
    return jnp.where(flag_ref[0] == 0, sub, flag_ref[1] ^ piece), jnp.where(flag_ref[0] == 0, piece, sub)


def laid(flag_ref, subs, w_ref):
    pairs = []
    for piece in (0, 1):
        for sub in (0, 1):
            half, block = place_of(flag_ref, piece, sub)
            ref = subs[2 * piece + sub]
            height = ref.shape[1]
            rows = pl.ds(pl.multiple_of(half * height, 16), height)
            pairs.append((ref, w_ref.at[:, rows, pl.ds(pl.multiple_of(block * 256, 128), 256)]))
    return pairs


def fetched(sems, *pairs):
    copies = [pltpu.make_async_copy(source, target, sems.at[k]) for k, (source, target) in enumerate(pairs)]
    for copy in copies:
        copy.start()
    return copies


def done(copies):
    for copy in copies:
        copy.wait()


def forward_kernel(flag_ref, score_ref, *refs, so_far):
    earlier, refs = (refs[:2], refs[2:]) if so_far else ((None, None), refs)
    tokens_hbm, one_hbm, refs = refs[0], refs[1], refs[2:]
    two, refs = ((refs[0], refs[1]), refs[2:]) if so_far else ((refs[0].at[0], refs[0].at[1]), refs[1:])
    (w_hbm, slope_hbm, curve_hbm, lifted_hbm, logit_ref, part_ref,
     tokens_ref, w_ref, slope_ref, curve_ref, lifted_ref, sems, out_sems) = refs
    n = lifted_ref.shape[0]
    copies = fetched(
        sems,
        *laid(flag_ref, (one_hbm.at[0], one_hbm.at[1], *two), w_ref),
        *((tokens_hbm.at[k * n : k * n + n, :], tokens_ref.at[k * n : k * n + n, :]) for k in (0, 1)),
    )
    done(copies[:4])
    forward_tiles(tokens_ref, w_ref, score_ref, slope_ref, curve_ref, lifted_ref, logit_ref, earlier[0], copies[4:])
    copies = fetched(
        out_sems, (w_ref, w_hbm), (slope_ref, slope_hbm), (curve_ref, curve_hbm), (lifted_ref, lifted_hbm)
    )
    pull_back(w_ref, lifted_ref, part_ref, earlier[1])
    done(copies)


def tokens_kernel(flag_ref, fake_hbm, real_hbm, other_hbm, tokens_ref, tokens_t_hbm, peak_ref,
                  own_ref, other_ref, tokens_t_ref, sems):
    tok = fake_hbm.shape[0]
    done(
        fetched(
            sems, (fake_hbm, own_ref.at[0:tok, :]), (real_hbm, own_ref.at[tok : 2 * tok, :]), (other_hbm, other_ref)
        )
    )
    first = flag_ref[0] == 0
    for kind in (0, 1):
        mine, theirs = (ref[kind * tok : kind * tok + tok, :] for ref in (own_ref, other_ref))
        start = 2 * kind * tok
        tokens_ref[start : start + tok, :] = jnp.where(first, mine, theirs)
        tokens_ref[start + tok : start + 2 * tok, :] = jnp.where(first, theirs, mine)
        peak = peak_of(tokens_ref[start : start + 2 * tok, :])
        peak_ref[8 * kind : 8 * kind + 8, :] = jnp.broadcast_to(peak, (8, 128))
    tokens_t_ref[...] = tokens_ref[...].T
    done(fetched(sems, (tokens_t_ref, tokens_t_hbm)))


def peak_of(array):
    flat = jnp.max(jnp.abs(array).astype(F32), axis=0, keepdims=True)
    return jnp.max(flat, axis=1, keepdims=True)


def cotangents(scale, logits, r1_ref, w_ref, slope_ref, curve_ref, fake_ref, real_ref):
    n = r1_ref.shape[0]
    fake_ref[...] = (scale * jax.nn.sigmoid(logits[:n]) * slope_ref[0:n, :]).astype(BF16)
    real_gain = -scale * jax.nn.sigmoid(-logits[n:])
    for start, width in column_tiles(w_ref.shape[2]):
        cols = slice(start, start + width)
        back = jnp.dot(r1_ref[...], flat(w_ref[:, :, cols]), preferred_element_type=F32)
        real_ref[:, cols] = (real_gain * slope_ref[n : 2 * n, cols] + back * curve_ref[:, cols]).astype(BF16)


def term_tiles(flag_ref, cotangent_refs, tokens_t_ref, r1_t_ref, term_ref, term_hbm, sems):
    fake_ref, real_ref, lifted_ref = cotangent_refs
    d_in, n = r1_t_ref.shape
    turn = d_in // (2 * NZ)
    leaving = []
    for block in (0, 1):
        cols = slice(256 * block, 256 * block + 256)
        for row in range(0, d_in, 4 * turn):
            rows = slice(row, row + 4 * turn)
            value = (
                jnp.dot(tokens_t_ref[rows, 0:n], fake_ref[:, cols], preferred_element_type=F32)
                + jnp.dot(tokens_t_ref[rows, n : 2 * n], real_ref[:, cols], preferred_element_type=F32)
                + jnp.dot(r1_t_ref[rows, :], lifted_ref[:, cols], preferred_element_type=F32)
            )
            there = slice(row // 2, row // 2 + 2 * turn)
            for half in (0, 1):
                for k in range(2):
                    at = row // 2 + k * turn
                    term_ref[half, block, at : at + turn, :] = value[(2 * k + half) * turn : (2 * k + half + 1) * turn, :]
                piece = jnp.where(flag_ref[0] == 0, block, flag_ref[1] ^ half)
                sub = jnp.where(flag_ref[0] == 0, half, block)
                leaving.append(
                    pltpu.make_async_copy(
                        term_ref.at[half, block, there, :], term_hbm.at[piece, sub, there, :], sems.at[len(leaving)]
                    )
                )
                leaving[-1].start()
    done(leaving)


def third_kernel(scale, flag_ref, part_ref, part_in_ref, logit_ref, logit_in_ref, peak_ref,
                 w_2_hbm, slope_2_hbm, curve_2_hbm, w_1_hbm, slope_1_hbm, curve_1_hbm, lifted_1_hbm, lifted_2_hbm,
                 tokens_t_hbm,
                 term_hbm, r1_t_hbm, fake_1_hbm, real_1_hbm, exp_ref,
                 term_ref, r1_t_ref, fake_1_ref, real_1_ref, r1_ref, fake_2_ref, real_2_ref,
                 w_2_ref, slope_2_ref, curve_2_ref, w_1_ref, slope_1_ref, curve_1_ref, lifted_1_ref, lifted_2_ref,
                 tokens_t_ref, sems, r1_sems, out_sems):
    copies = fetched(
        sems,
        (w_2_hbm, w_2_ref), (slope_2_hbm, slope_2_ref), (curve_2_hbm, curve_2_ref),
        (w_1_hbm, w_1_ref), (slope_1_hbm, slope_1_ref), (curve_1_hbm, curve_1_ref),
        (lifted_1_hbm, lifted_1_ref), (lifted_2_hbm, lifted_2_ref), (tokens_t_hbm, tokens_t_ref),
    )
    r1_t_ref[...] = (scale * R1_WEIGHT * (part_ref[...] + part_in_ref[...])).astype(BF16)
    r1_ref[...] = r1_t_ref[...].T
    logits = jnp.sum(logit_ref[...] + logit_in_ref[...], axis=1, keepdims=True)
    done(copies[:3])
    cotangents(scale, logits, r1_ref, w_2_ref, slope_2_ref, curve_2_ref, fake_2_ref, real_2_ref)
    done(copies[3:6])
    cotangents(scale, logits, r1_ref, w_1_ref, slope_1_ref, curve_1_ref, fake_1_ref, real_1_ref)
    passed = fetched(r1_sems, (r1_t_ref, r1_t_hbm), (fake_1_ref, fake_1_hbm), (real_1_ref, real_1_hbm))
    done(copies[6:])
    first, second = (fake_1_ref, real_1_ref, lifted_1_ref), (fake_2_ref, real_2_ref, lifted_2_ref)
    peaks = [jnp.maximum(peak_of(one[...]), peak_of(two[...])) for one, two in zip(first, second)]
    n = r1_ref.shape[0]
    bound = n * (
        peak_ref[0:1, 0:1] * peaks[0] + peak_ref[8:9, 0:1] * peaks[1] + peak_of(r1_t_ref[...]) * peaks[2]
    )
    bound = jnp.broadcast_to(bound, (16, 128))
    exp_ref[...] = jnp.ceil(jnp.log(jnp.maximum(bound, 1e-30)) * (1.0 / math.log(2.0)) + 0.01) - 15.0
    term_tiles(flag_ref, second, tokens_t_ref, r1_t_ref, term_ref, term_hbm, out_sems)
    done(passed)


def fourth_kernel(flag_ref, r1_t_hbm, fake_hbm, real_hbm, lifted_hbm, tokens_t_hbm, term_hbm,
                  term_ref, r1_t_ref, fake_ref, real_ref, lifted_ref, tokens_t_ref, sems, out_sems):
    done(
        fetched(
            sems,
            (r1_t_hbm, r1_t_ref), (fake_hbm, fake_ref), (real_hbm, real_ref), (lifted_hbm, lifted_ref),
            (tokens_t_hbm, tokens_t_ref),
        )
    )
    term_tiles(flag_ref, (fake_ref, real_ref, lifted_ref), tokens_t_ref, r1_t_ref, term_ref, term_hbm, out_sems)


def call(kernel, flops, outs, scratch, *args, flags=None, there=(), anywhere=(), sems=(), vmem_mib=20):
    vmem = pl.BlockSpec(memory_space=pltpu.VMEM)
    specs = [vmem] * len(args) + [pl.BlockSpec(memory_space=pltpu.HBM)] * len(there)
    specs += [pl.BlockSpec(memory_space=pl.ANY)] * len(anywhere)
    args = (*args, *(pltpu.with_memory_space_constraint(a, pltpu.HBM) for a in there), *anywhere)
    if flags is not None:
        args, specs = (flags, *args), [pl.BlockSpec(memory_space=pltpu.SMEM), *specs]
    return pl.pallas_call(
        kernel,
        out_shape=[(pltpu.HBM if len(out) == 3 else pltpu.VMEM)(*out[:2]) for out in outs],
        in_specs=specs,
        out_specs=[pl.BlockSpec(memory_space=pltpu.HBM) if len(out) == 3 else vmem for out in outs],
        scratch_shapes=[pltpu.VMEM(shape, dtype) for shape, dtype in scratch]
        + [pltpu.SemaphoreType.DMA((k,)) for k in sems],
        compiler_params=pltpu.CompilerParams(vmem_limit_bytes=vmem_mib * 1024 * 1024),
        cost_estimate=pl.CostEstimate(flops=flops, bytes_accessed=8_000_000, transcendentals=0),
    )(*args)


def per_device(fake_tokens, real_tokens, proj_weight, score_vector):
    ylo, x, z, yhi, c = (lax.axis_index(a) for a in AXES)
    y = yhi * 2 + ylo
    gray_x = (x == 1) | (x == 2)
    core0 = c == 0
    tok = fake_tokens.shape[1]
    rows, hid = proj_weight.shape
    half = hid // 2
    d_in = rows * NZ * 4
    n = 2 * tok
    scale = math.sqrt(hid / (8 * 32 * tok))

    def slice_of(side):
        start = jnp.where(side == 0, x * 256, half + ylo * 512 + gray_x * 256)
        return lax.dynamic_slice_in_dim(proj_weight, start, 256, 1)

    block = ordered(core0, slice_of(c), to_core(slice_of(1 - c)), 0)
    over_z = lax.all_to_all(jnp.broadcast_to(block[None], (NZ, *block.shape)), "z", 0, 0)
    sub = over_z.reshape(d_in // 2, 256)
    own = ordered(jnp.where(core0, yhi == 0, ~gray_x), sub, send(sub, pair), 0)

    own_tokens = jnp.concatenate([fake_tokens[0], real_tokens[0]], 0)
    def join_tokens(other_tokens):
        return call(
            tokens_kernel, 2 * n * d_in * 128,
            [((2 * n, d_in), BF16), ((d_in, 2 * n), BF16, True), ((16, 128), F32)],
            [((n, d_in), BF16), ((n, d_in), BF16), ((d_in, 2 * n), BF16)],
            flags=c[None].astype(jnp.int32), there=(fake_tokens[0], real_tokens[0], other_tokens), sems=[3],
        )

    left, right, tokens, tokens_t, peak = together((own, own), (ring(1), ring(-1)), join_tokens, (to_core(own_tokens),))
    across = together((left[: d_in // 2], right[d_in // 2 :]), (ring(1), ring(-1)))

    def score_at(start):
        return lax.dynamic_slice_in_dim(score_vector, c * half + start, 256, 0)

    def scores(one, two, group):
        blocks = (jnp.where(core0, one % 4 * 256, group * 512), jnp.where(core0, two % 4 * 256, group * 512 + 256))
        return jnp.concatenate([score_at(b) for b in blocks])[None]

    flags_1, flags_2 = (jnp.stack([c, at]).astype(jnp.int32) for at in ((y + 3) % 4 // 2, yhi))
    turn, wide = d_in // NZ, half // 2
    states = [((NZ, turn, wide), BF16), ((2 * n, wide), F32), ((n, wide), F32), ((n, wide), BF16)]
    sums = [((2 * n, 128), F32), ((d_in, n), F32)]
    marked = lambda shapes: [(*shape, True) for shape in shapes]

    def forward(flags, score, pieces, earlier):
        return call(
            functools.partial(forward_kernel, so_far=bool(earlier)), 6 * n * d_in * wide, [*marked(states), *sums],
            [((2 * n, d_in), BF16), *states], score, *earlier,
            flags=flags, there=(tokens,), anywhere=pieces, sems=[6, 4], vmem_mib=24,
        )

    left, right, own = (p.reshape(2, NZ, 2 * rows, 256) for p in (left, right, own))
    w_1, slope_1, curve_1, lifted_1, *earlier = forward(flags_1, scores(x + 3, x + 1, 1 - ylo), (left, right), ())
    across = [p.reshape(NZ, 2 * rows, 256) for p in across]
    w_2, slope_2, curve_2, lifted_2, logit, part = forward(flags_2, scores(x, x + 2, ylo), (own, *across), earlier)
    part_in, logit_in = to_core(part), to_core(logit)

    works = [((n, wide), BF16)] * 2
    terms, tall, r1_shape = ((2, 2, d_in // 2, 256), F32), ((d_in, 2 * n), BF16), ((d_in, n), BF16)
    term_2, r1_t, fake_1, real_1, exponent = call(
        functools.partial(third_kernel, scale), 6 * n * d_in * half,
        [*marked([terms, r1_shape, *works]), ((16, 128), F32)],
        [terms, r1_shape, *works, ((n, d_in), BF16), *works, *states[:3], *states, states[3], tall],
        part, part_in, logit, logit_in, peak, flags=flags_2,
        there=(w_2, slope_2, curve_2, w_1, slope_1, curve_1, lifted_1, lifted_2, tokens_t),
        sems=[9, 3, 16], vmem_mib=36,
    )
    exponent = jnp.concatenate([exponent[:1]] * 2, 1)

    def rest_of_term(r1_t):
        (term_1,) = call(
            fourth_kernel, 6 * n * d_in * wide, marked([terms]), [terms, r1_shape, *works, states[3], tall],
            flags=flags_1, there=(r1_t, fake_1, real_1, lifted_1, tokens_t), sems=[5, 16], vmem_mib=28,
        )
        raw.append(term_1)
        return (term_1,)

    raw = []
    across, _ = together(
        (packed(term_2[1].reshape(d_in, 256), exponent),), (ring(2),), rest_of_term, (r1_t,)
    )
    beside = [packed(raw[0][k].reshape(d_in, 256), exponent) for k in (1, 0)]
    from_left, from_right, across = together(beside, (ring(1), ring(-1)), lambda a: (a,), (across,))

    def summed(own, exponent, *messages):
        for values, theirs in map(unpacked, messages):
            own, exponent = own + values, jnp.maximum(exponent, theirs)
        return own, exponent + 2.0

    total, exponent = summed(term_2[0].reshape(d_in, 256), exponent, from_left, from_right, across)

    place = jnp.where(core0, y, x)
    total = total.reshape(2, NZ, 2, rows, 256)

    def quarter(k):
        at = (place + k) % 4
        zero = jnp.zeros_like(at)
        return lax.dynamic_slice(total, (at // 2, zero, at % 2, zero, zero), (1, NZ, 1, rows, 256)).reshape(NZ * rows, 256)

    away = (1, 3, 2)
    got = together([packed(quarter(k), exponent) for k in away], [other_ring(k) for k in away])
    both = summed(quarter(0), exponent, *got)[0].reshape(NZ, rows, 256)
    both = jnp.sum(lax.all_to_all(both, "z", 0, 0), 0)

    spread = lax.all_to_all(jnp.broadcast_to(both[None], (8, *both.shape)), ("ylo", "x"), 0, 0)
    spread = spread.reshape(2, 4, rows, 256)

    def row_group(r):
        first = [spread[r, k] for k in range(4)]
        second = [spread[v, 2 * j + r] for v in (0, 1) for j in (0, 1)]
        return jnp.concatenate([jnp.where(core0, f, g) for f, g in zip(first, second)], 1)

    zero, one = row_group(0), row_group(1)
    theirs = to_core(jnp.where(core0, one, zero))
    return ordered(core0, jnp.where(core0, zero, one), theirs, 1)


def solution(mesh):
    split = Mesh(mesh.devices.reshape(2, NX, NZ, 2, 2), AXES)
    tokens = P(("ylo", "x"), ("z", "yhi", "c"), None)
    shard = P(("z", "yhi", "c"), None)
    return jax.shard_map(
        per_device, mesh=split, in_specs=(tokens, tokens, shard, P()), out_specs=shard, check_vma=False
    )
```
